32 devices in a mesh: dp: 8 (over z, core), tensor: 4 (over y, x).
Axes of the slice: x: 2, y: 2, z: 4, core: 2. Of those that a mesh axis runs over, the one named last changes fastest.
Arguments:
- layer_input: bfloat16 [16384, 2048], P(('dp', 'tensor')), may hold values from -6 to 6
- cotangent: bfloat16 [16384, 2048], P(('dp', 'tensor')), may hold values from -6 to 6
- firstgain: bfloat16 [2048], P('dp'), may hold values from 0.5 to 1.5
- firstbias: bfloat16 [2048], P('dp'), may hold values from -1 to 1
- secondgain: bfloat16 [2048], P('dp'), may hold values from 0.5 to 1.5
- secondbias: bfloat16 [2048], P('dp'), may hold values from -1 to 1
- project: bfloat16 [2048, 8, 768], P('dp', 'tensor'), may hold values from -0.125 to 0.125
- projbias: bfloat16 [8, 768], P('tensor', 'dp'), may hold values from -3 to 3
- merging: bfloat16 [2048, 2048], P('tensor', 'dp'), may hold values from -1.5 to 1.5
- mergebias: bfloat16 [2048], P('dp'), may hold values from -2 to 2
- expand: bfloat16 [2048, 8192], P('dp', 'tensor'), may hold values from -0.125 to 0.125
- expandbias: bfloat16 [8192], P(('tensor', 'dp')), may hold values from -3 to 3
- shrink: bfloat16 [8192, 2048], P('tensor', 'dp'), may hold values from -0.0625 to 0.0625
- shrinkbias: bfloat16 [2048], P('dp'), may hold values from -2 to 2
Outputs:
- layer_output: bfloat16 [16384, 2048], P(('dp', 'tensor'))
- input_grad: float32 [16384, 2048], P(('dp', 'tensor'))
- firstgain_grad: float32 [2048], P('dp')
- firstbias_grad: float32 [2048], P('dp')
- secondgain_grad: float32 [2048], P('dp')
- secondbias_grad: float32 [2048], P('dp')
- project_grad: float32 [2048, 8, 768], P('dp', 'tensor')
- projbias_grad: float32 [8, 768], P('tensor', 'dp')
- merging_grad: float32 [2048, 2048], P('tensor', 'dp')
- mergebias_grad: float32 [2048], P('dp')
- expand_grad: float32 [2048, 8192], P('dp', 'tensor')
- expandbias_grad: float32 [8192], P(('tensor', 'dp'))
- shrink_grad: float32 [8192, 2048], P('tensor', 'dp')
- shrinkbias_grad: float32 [2048], P('dp')
The draws below stay inside these ranges and needn't reach their ends.
All inputs are finite; a program needn't handle non-finite values.
Results may differ from the reference program's by a relative error of at most 0.015.
Values may be sent and summed in bfloat16 or wider, within the bound.
No kernel may reach another device: no remote copies, remote signals or barrier semaphores. Data moves between devices by JAX's collectives and lax.ppermute only.
A program may use at most 256 MiB of HBM per device.

```python
import jax
import jax.numpy as jnp
from jax import lax

D = 2048
HEADS = 8
HEAD_DIM = 256
ROTARY = 64
FF = 8192
LENGTH = 2048
TOKENS = 16384


def shard_levels(key, dims, split, low, largest):
    def one(dim, parts):
        steps = jax.random.uniform(jax.random.fold_in(jax.random.fold_in(key, 6), dim), (parts,), jnp.float32, low / len(split), largest / len(split))
        return jnp.repeat(jnp.exp(steps), dims[dim] // parts).reshape((-1,) + (1,) * (len(dims) - dim - 1))

    level = one(*split[0])
    for cut in split[1:]:
        level = level * one(*cut)
    return level


def scatter_about(stream_key, dims, deviation, limit, split=(), held_as=jnp.bfloat16):
    array = deviation * jax.random.normal(stream_key, dims, jnp.float32)
    if split:
        array = array * shard_levels(stream_key, dims, split, -0.22, 0.18)
    return jnp.clip(array, -limit, limit).astype(held_as)


def setup_inputs(seed: int = 0) -> dict:
    splits = jax.random.split(jax.random.key(seed), 15)
    return {
        "layer_input": scatter_about(splits[0], (TOKENS, D), 1.0, 6.0, ((0, 32),)),
        "cotangent": scatter_about(splits[1], (TOKENS, D), 1.0, 6.0, ((0, 32),)),
        "firstgain": jnp.clip(1.0 + 0.1 * jax.random.normal(splits[2], (D,), jnp.float32), 0.5, 1.5).astype(jnp.bfloat16),
        "firstbias": scatter_about(splits[3], (D,), 0.2, 1.0, ((0, 8),)),
        "secondgain": jnp.clip(1.0 + 0.1 * jax.random.normal(splits[4], (D,), jnp.float32), 0.5, 1.5).astype(jnp.bfloat16),
        "secondbias": scatter_about(splits[5], (D,), 0.2, 1.0, ((0, 8),)),
        "project": scatter_about(splits[6], (D, HEADS, 3 * HEAD_DIM), D ** -0.5, 0.125, ((0, 8), (1, 4))),
        "projbias": scatter_about(splits[7], (HEADS, 3 * HEAD_DIM), 0.5, 3.0, ((0, 4), (1, 8))),
        "merging": scatter_about(splits[8], (D, D), (D * 16 // LENGTH) ** -0.5, 1.5, ((0, 4), (1, 8))),
        "mergebias": scatter_about(splits[9], (D,), 0.3, 2.0, ((0, 8),)),
        "expand": scatter_about(splits[10], (D, FF), D ** -0.5, 0.125, ((0, 8), (1, 4))),
        "expandbias": scatter_about(splits[11], (FF,), 0.5, 3.0, ((0, 32),)),
        "shrink": scatter_about(splits[12], (FF, D), FF ** -0.5, 0.0625, ((0, 4), (1, 8))),
        "shrinkbias": scatter_about(splits[13], (D,), 0.3, 2.0, ((0, 8),)),
    }


epsilon = 1e-05
highest = lax.Precision.HIGHEST

@jax.custom_vjp
def low(v):
    return lax.optimization_barrier(v.astype(jnp.bfloat16)).astype(jnp.float32)

@jax.custom_vjp
def low_back(v):
    return v

def low_keep(v):
    return (low(v), None)

def low_pass(kept, grad):
    return (grad,)

def back_keep(v):
    return (v, None)

def back_low(kept, grad):
    return (low(grad),)
low.defvjp(low_keep, low_pass)
low_back.defvjp(back_keep, back_low)

def normalize(row_data, gain_vec, shift_vec):
    centre = row_data - lax.optimization_barrier(jnp.mean(row_data, axis=-1, keepdims=True))
    spread = lax.optimization_barrier(jnp.mean(centre * centre, axis=-1, keepdims=True))
    return centre * lax.rsqrt(spread + epsilon) * gain_vec + shift_vec

def rotary_tables(length, rotary):
    position = jnp.arange(length, dtype=jnp.float32)
    frequency = 10000.0 ** (-jnp.arange(0, rotary, 2, dtype=jnp.float32) / rotary)
    angles = position[:, None] * frequency[None, :]
    return (jnp.cos(angles), jnp.sin(angles))

def rotate_heads(values, cosine_table, sine_table):
    halfway = cosine_table.shape[-1]
    leading = values[..., :halfway]
    trailing = values[..., halfway:2 * halfway]
    return jnp.concatenate([leading * cosine_table - trailing * sine_table, trailing * cosine_table + leading * sine_table, values[..., 2 * halfway:]], axis=-1)

def layer_forward(row_data, params, cosine_table, sine_table):
    firstgain, firstbias, secondgain, secondbias, project, projbias, merging, mergebias, expand, expandbias, shrink, shrinkbias = params
    first = low(normalize(row_data, firstgain, firstbias))
    second = low(normalize(row_data, secondgain, secondbias))
    mixed_rows = low_back(jnp.einsum('sd,dhe->hse', first, project, precision=highest) + projbias[:, None, :])
    queries = low(rotate_heads(mixed_rows[..., :HEAD_DIM], cosine_table, sine_table))
    keyset = low(rotate_heads(mixed_rows[..., HEAD_DIM:2 * HEAD_DIM], cosine_table, sine_table))
    valueset = low(mixed_rows[..., 2 * HEAD_DIM:])
    scores = low_back(jnp.einsum('hqe,hke->hqk', queries, keyset, precision=highest) * HEAD_DIM ** (-0.5))
    row_at = jnp.arange(LENGTH)[:, None]
    col_at = jnp.arange(LENGTH)[None, :]
    scores = jnp.where(col_at <= row_at, scores, -1000000000.0)
    probability = low(jax.nn.softmax(scores, axis=-1))
    context = jnp.einsum('hqk,hke->qhe', probability, valueset, precision=highest).reshape(row_data.shape[0], -1)
    context = low_back(low(context))
    attended = jnp.dot(context, merging, precision=highest) + mergebias
    preact = low_back(jnp.dot(second, expand, precision=highest) + expandbias)
    hidden = low(jax.nn.gelu(preact, approximate=False))
    fed = jnp.dot(hidden, shrink, precision=highest) + shrinkbias
    return row_data + attended + fed

def reference(layer_input, cotangent, firstgain, firstbias, secondgain, secondbias, project, projbias, merging, mergebias, expand, expandbias, shrink, shrinkbias):
    params = tuple((entry.astype(jnp.float32) for entry in (firstgain, firstbias, secondgain, secondbias, project, projbias, merging, mergebias, expand, expandbias, shrink, shrinkbias)))
    seq_count = layer_input.shape[0] // LENGTH
    inputs = layer_input.astype(jnp.float32).reshape(seq_count, LENGTH, -1)
    seed_rows = cotangent.astype(jnp.float32).reshape(seq_count, LENGTH, -1)
    cosine_table, sine_table = rotary_tables(LENGTH, ROTARY)

    def one_sequence(totals, paired):
        rows_in, rows_seed = paired

        def forward_only(row_data, weights):
            return layer_forward(row_data, weights, cosine_table, sine_table)
        result, pullback = jax.vjp(forward_only, rows_in, params)
        row_grad, weight_grads = pullback(rows_seed)
        totals = tuple((left + right for left, right in zip(totals, weight_grads)))
        return (totals, (result.astype(jnp.bfloat16), row_grad))
    zero_grads = tuple((jnp.zeros_like(entry) for entry in params))
    totals, (outputs, row_grads) = lax.scan(one_sequence, zero_grads, (inputs, seed_rows))
    return (outputs.reshape(layer_input.shape), row_grads.reshape(layer_input.shape), totals[0], totals[1], totals[2], totals[3], totals[4], totals[5], totals[6], totals[7], totals[8], totals[9], totals[10], totals[11])
```

```python
import jax
import jax.numpy as jnp
from jax import lax
from jax.experimental import pallas as pl
from jax.experimental.pallas import tpu as pltpu
from jax.sharding import PartitionSpec as P

HEAD_DIM = 256
ROTARY = 64
LENGTH = 2048
EPSILON = 1e-05
BIG = -1e30
F32 = jnp.float32
BF16 = jnp.bfloat16
DIMS = {
    "NN": (((1,), (0,)), ((), ())),
    "NT": (((1,), (1,)), ((), ())),
    "TN": (((0,), (0,)), ((), ())),
}


def product(left, right, mode):
    return lax.dot_general(left, right, DIMS[mode], preferred_element_type=F32)


def params():
    return pltpu.CompilerParams(vmem_limit_bytes=56 << 20)


def cost(flops, nbytes, transcendentals=0):
    return pl.CostEstimate(
        flops=int(flops), bytes_accessed=int(nbytes), transcendentals=int(transcendentals)
    )


def tile_of(width, most):
    best = 128
    for size in range(128, most + 1, 128):
        if width % size == 0:
            best = size
    return best


def call(kernel, ids, grid, in_specs, out_specs, out_shape, args, cost_of, scratch=()):
    return pl.pallas_call(
        kernel,
        grid_spec=pltpu.PrefetchScalarGridSpec(
            num_scalar_prefetch=1,
            grid=grid,
            in_specs=in_specs,
            out_specs=out_specs,
            scratch_shapes=list(scratch),
        ),
        out_shape=out_shape,
        compiler_params=params(),
        cost_estimate=cost_of,
    )(ids, *args)


def norm_kernel(ids, pieces, vectors, unit):
    rows = sum(piece.shape[0] for piece in pieces)
    width = pieces[0].shape[1]
    starts = []
    for piece in pieces:
        starts.append((starts[-1][1] if starts else 0,) * 2)
        starts[-1] = (starts[-1][0], starts[-1][0] + piece.shape[0] // unit)

    def kernel(ids_ref, *refs):
        step = pl.program_id(0)
        vec = refs[len(pieces)]
        first_ref, second_ref = refs[len(pieces) + 1 :]
        for (low, high), piece_ref in zip(starts, refs):

            @pl.when((step >= low) & (step < high))
            def _(piece_ref=piece_ref):
                data = piece_ref[...].astype(F32)
                centre = data - jnp.mean(data, axis=-1, keepdims=True)
                spread = jnp.mean(centre * centre, axis=-1, keepdims=True)
                scaled = centre * lax.rsqrt(spread + EPSILON)
                first_ref[...] = (scaled * vec[0:1, :] + vec[1:2, :]).astype(BF16)
                second_ref[...] = (scaled * vec[2:3, :] + vec[3:4, :]).astype(BF16)

    def spec(low, high):
        return pl.BlockSpec((unit, width), lambda i, ids: (jnp.clip(i - low, 0, high - low - 1), 0))

    out = pl.BlockSpec((unit, width), lambda i, ids: (i, 0))
    shape = jax.ShapeDtypeStruct((rows, width), BF16)
    return call(
        kernel,
        ids,
        (rows // unit,),
        [spec(low, high) for low, high in starts] + [pl.BlockSpec(vectors.shape, lambda i, ids: (0, 0))],
        [out, out],
        [shape, shape],
        (*pieces, vectors),
        cost(12 * rows * width, 6 * rows * width),
    )


def rotate(block, cos, sin_low, sin_high, sign):
    lead = block[:, :128]
    turned = (
        lead * cos
        + sign * (pltpu.roll(lead, 96, 1) * sin_low + pltpu.roll(lead, 32, 1) * sin_high)
    )
    return jnp.concatenate([turned, block[:, 128:]], axis=1)


def mixed_kernel(ids, first, weight, bias, tables, blocks):
    rows, depth = first.shape
    heads = weight.shape[1] // (3 * HEAD_DIM)
    unit = rows // blocks
    wide = 3 * HEAD_DIM

    def kernel(ids_ref, a_ref, w_ref, b_ref, cos, low, high, out_ref):
        for part in range(3):
            here = slice(part * HEAD_DIM, (part + 1) * HEAD_DIM)
            value = product(a_ref[...], w_ref[:, here], "NN") + b_ref[:, here]
            if part < 2:
                value = rotate(value, cos[...], low[...], high[...], 1.0)
            out_ref[:, here] = value.astype(BF16)

    table = pl.BlockSpec((unit, 128), lambda j, i, ids: (ids[0] ^ i, 0))
    return call(
        kernel,
        ids,
        (heads, blocks),
        [
            pl.BlockSpec((unit, depth), lambda j, i, ids: (i, 0)),
            pl.BlockSpec((depth, wide), lambda j, i, ids: (0, j)),
            pl.BlockSpec((1, wide), lambda j, i, ids: (0, j)),
            table,
            table,
            table,
        ],
        pl.BlockSpec((unit, wide), lambda j, i, ids: (i, j)),
        jax.ShapeDtypeStruct((rows, heads * wide), BF16),
        (first, weight, bias, *tables),
        cost(2 * rows * depth * heads * wide, 2 * (heads * rows * depth + depth * heads * wide + rows * heads * wide)),
    )


def attend_kernel(ids, mixed, blocks):
    rows, width = mixed.shape
    heads = width // (3 * HEAD_DIM)
    unit = rows // blocks
    scale = HEAD_DIM ** (-0.5)

    def kernel(ids_ref, x_ref, ctx_ref, lse_ref, top_s, total_s, acc_s):
        block = pl.program_id(0)
        me = ids_ref[0]
        here = pl.ds(pl.multiple_of((me ^ block) * unit, unit), unit)

        def step(other, diagonal):
            there = pl.ds(pl.multiple_of((me ^ other) * unit, unit), unit)
            for head in range(heads):
                at = 3 * HEAD_DIM * head
                scores = (
                    product(
                        x_ref[here, at : at + HEAD_DIM],
                        x_ref[there, at + HEAD_DIM : at + 2 * HEAD_DIM],
                        "NT",
                    )
                    * scale
                )
                value = x_ref[there, at + 2 * HEAD_DIM : at + 3 * HEAD_DIM]
                if diagonal:
                    row_at = lax.broadcasted_iota(jnp.int32, scores.shape, 0)
                    col_at = lax.broadcasted_iota(jnp.int32, scores.shape, 1)
                    scores = jnp.where(col_at <= row_at, scores, BIG)
                    top = jnp.max(scores, axis=1, keepdims=True)
                    weight = jnp.exp(scores - top)
                    top_s[head] = top
                    total_s[head] = jnp.sum(weight, axis=1, keepdims=True)
                    acc_s[head] = product(weight.astype(BF16), value, "NN")
                else:
                    before = top_s[head]
                    top = jnp.maximum(before, jnp.max(scores, axis=1, keepdims=True))
                    weight = jnp.exp(scores - top)
                    shrunk = jnp.exp(before - top)
                    top_s[head] = top
                    total_s[head] = total_s[head] * shrunk + jnp.sum(weight, axis=1, keepdims=True)
                    acc_s[head] = acc_s[head] * shrunk + product(weight.astype(BF16), value, "NN")

        step(block, True)

        @pl.loop(0, block)
        def _(other):
            step(other, False)

        for head in range(heads):
            at = HEAD_DIM * head
            ctx_ref[:, at : at + HEAD_DIM] = (acc_s[head] / total_s[head]).astype(BF16)
            log_total = top_s[head] + jnp.log(total_s[head])
            lse_ref[head, 0] = jnp.transpose(jnp.broadcast_to(log_total, (unit, 128)))[:8]

    return call(
        kernel,
        ids,
        (blocks,),
        [pl.BlockSpec((rows, width), lambda b, ids: (0, 0))],
        [
            pl.BlockSpec((unit, heads * HEAD_DIM), lambda b, ids: (ids[0] ^ b, 0)),
            pl.BlockSpec((heads, 1, 8, unit), lambda b, ids: (0, b, 0, 0)),
        ],
        [
            jax.ShapeDtypeStruct((rows, heads * HEAD_DIM), BF16),
            jax.ShapeDtypeStruct((heads, blocks, 8, unit), F32),
        ],
        (mixed,),
        cost(2 * heads * rows * rows * HEAD_DIM, 3 * rows * width, heads * rows * rows // 2),
        [
            pltpu.VMEM((heads, unit, 1), F32),
            pltpu.VMEM((heads, unit, 1), F32),
            pltpu.VMEM((heads, unit, HEAD_DIM), F32),
        ],
    )


def attend_back_kernel(ids, mixed, grad, context, lse, tables, blocks):
    rows, width = mixed.shape
    heads = width // (3 * HEAD_DIM)
    unit = rows // blocks
    scale = HEAD_DIM ** (-0.5)

    def kernel(ids_ref, x_ref, g_ref, c_ref, lse_ref, cos, low, high, out_ref, sum_ref, dk_s, dv_s, dq_s, inner_s):
        turn = pl.program_id(0)
        block = blocks - 1 - turn
        me = ids_ref[0]

        @pl.when(turn == 0)
        def _():
            dk_s[...] = jnp.zeros_like(dk_s)
            dv_s[...] = jnp.zeros_like(dv_s)
            sum_ref[...] = jnp.zeros_like(sum_ref)

        here = pl.ds(pl.multiple_of((me ^ block) * unit, unit), unit)
        for head in range(heads):
            cols = slice(HEAD_DIM * head, HEAD_DIM * (head + 1))
            inner = jnp.sum(g_ref[here, cols].astype(F32) * c_ref[here, cols].astype(F32), axis=1, keepdims=True)
            inner_s[head] = jnp.transpose(jnp.broadcast_to(inner, (unit, 128)))[:8]

        def step(other, diagonal):
            there = pl.ds(pl.multiple_of((me ^ other) * unit, unit), unit)
            for head in range(heads):
                at = 3 * HEAD_DIM * head
                query = x_ref[here, at : at + HEAD_DIM]
                seed = g_ref[here, HEAD_DIM * head : HEAD_DIM * (head + 1)]
                key = x_ref[there, at + HEAD_DIM : at + 2 * HEAD_DIM]
                value = x_ref[there, at + 2 * HEAD_DIM : at + 3 * HEAD_DIM]
                scores = product(key, query, "NT") * scale
                prob = jnp.exp(scores - lse_ref[head, 0][:1])
                if diagonal:
                    key_at = lax.broadcasted_iota(jnp.int32, scores.shape, 0)
                    row_at = lax.broadcasted_iota(jnp.int32, scores.shape, 1)
                    prob = jnp.where(key_at <= row_at, prob, 0.0)
                dprob = product(value, seed, "NT")
                dscore = (prob * (dprob - inner_s[head][:1])).astype(BF16)
                dv_s[head, other] += product(prob.astype(BF16), seed, "NN")
                dk_s[head, other] += product(dscore, query, "NN")
                dquery = product(dscore, key, "TN")
                if diagonal:
                    dq_s[head] = dquery
                else:
                    dq_s[head] += dquery

        step(block, True)

        @pl.loop(0, block)
        def _(other):
            step(other, False)

        for head in range(heads):
            at = 3 * HEAD_DIM * head
            dquery = rotate(dq_s[head] * scale, cos[...], low[...], high[...], -1.0)
            dkey = rotate(dk_s[head, block] * scale, cos[...], low[...], high[...], -1.0)
            for part, value in enumerate((dquery, dkey, dv_s[head, block])):
                cols = slice(at + part * HEAD_DIM, at + (part + 1) * HEAD_DIM)
                rounded = value.astype(BF16)
                out_ref[:, cols] = rounded
                sum_ref[:, cols] += jnp.sum(rounded.astype(F32), axis=0, keepdims=True)

    def whole(cols):
        return pl.BlockSpec((rows, cols), lambda b, ids: (0, 0))

    table = pl.BlockSpec((unit, 128), lambda b, ids: (blocks - 1 - b, 0))
    return call(
        kernel,
        ids,
        (blocks,),
        [
            whole(width),
            whole(heads * HEAD_DIM),
            whole(heads * HEAD_DIM),
            pl.BlockSpec((heads, 1, 8, unit), lambda b, ids: (0, blocks - 1 - b, 0, 0)),
            table,
            table,
            table,
        ],
        [
            pl.BlockSpec((unit, width), lambda b, ids: (ids[0] ^ (blocks - 1 - b), 0)),
            pl.BlockSpec((1, width), lambda b, ids: (0, 0)),
        ],
        [jax.ShapeDtypeStruct((rows, width), BF16), jax.ShapeDtypeStruct((1, width), F32)],
        (mixed, grad, context, lse, *tables),
        cost(5 * heads * rows * rows * HEAD_DIM, 6 * rows * width, heads * rows * rows // 2),
        [
            pltpu.VMEM((heads, blocks, unit, HEAD_DIM), F32),
            pltpu.VMEM((heads, blocks, unit, HEAD_DIM), F32),
            pltpu.VMEM((heads, unit, HEAD_DIM), F32),
            pltpu.VMEM((heads, 8, unit), F32),
        ],
    )


def expand_kernel(ids, second, weight, bias):
    rows, depth = second.shape
    width = weight.shape[1]
    tall, wide = tile_of(rows, 1024), tile_of(width, 1024)
    unit = tile_of(wide, 512)

    def kernel(ids_ref, a_ref, w_ref, b_ref, hidden_ref, slope_ref):
        for part in range(wide // unit):
            here = slice(part * unit, (part + 1) * unit)
            pre = product(a_ref[...], w_ref[:, here], "NN") + b_ref[:, here]
            phi = 0.5 + 0.5 * lax.erf(pre * 0.7071067811865476)
            hidden_ref[:, here] = (pre * phi).astype(BF16)
            slope = phi + pre * (jnp.exp(-0.5 * pre * pre) * 0.3989422804014327)
            slope_ref[:, here] = slope.astype(BF16)

    out = pl.BlockSpec((tall, wide), lambda i, j, ids: (i, j))
    shape = jax.ShapeDtypeStruct((rows, width), BF16)
    return call(
        kernel,
        ids,
        (rows // tall, width // wide),
        [
            pl.BlockSpec((tall, depth), lambda i, j, ids: (i, 0)),
            pl.BlockSpec((depth, wide), lambda i, j, ids: (0, j)),
            pl.BlockSpec((1, wide), lambda i, j, ids: (0, j)),
        ],
        [out, out],
        [shape, shape],
        (second, weight, bias),
        cost(2 * rows * depth * width, 2 * (rows * depth + 2 * depth * width + 2 * rows * width), 2 * rows * width),
    )


def shrink_back_kernel(ids, seed, weight, slope):
    rows, depth = seed.shape
    width = weight.shape[0]
    tall, wide = tile_of(rows, 1024), tile_of(width, 1024)
    unit = tile_of(wide, 512)

    def kernel(ids_ref, a_ref, w_ref, s_ref, out_ref, sum_ref):
        @pl.when(pl.program_id(1) == 0)
        def _():
            sum_ref[...] = jnp.zeros_like(sum_ref)

        for part in range(wide // unit):
            here = slice(part * unit, (part + 1) * unit)
            grad = product(a_ref[...], w_ref[here, :], "NT") * s_ref[:, here].astype(F32)
            rounded = grad.astype(BF16)
            out_ref[:, here] = rounded
            sum_ref[:, here] += jnp.sum(rounded.astype(F32), axis=0, keepdims=True)

    tile = pl.BlockSpec((tall, wide), lambda j, i, ids: (i, j))
    return call(
        kernel,
        ids,
        (width // wide, rows // tall),
        [
            pl.BlockSpec((tall, depth), lambda j, i, ids: (i, 0)),
            pl.BlockSpec((wide, depth), lambda j, i, ids: (j, 0)),
            tile,
        ],
        [tile, pl.BlockSpec((1, wide), lambda j, i, ids: (0, j))],
        [jax.ShapeDtypeStruct((rows, width), BF16), jax.ShapeDtypeStruct((1, width), F32)],
        (seed, weight, slope),
        cost(2 * rows * depth * width, 2 * (2 * rows * depth + depth * width + 2 * rows * width)),
    )


def plain_kernel(ids, left, right, mode):
    rows, depth = left.shape
    width = right.shape[1] if mode == "NN" else right.shape[0]
    tall = tile_of(rows, 512)

    def kernel(ids_ref, a_ref, b_ref, out_ref):
        out_ref[...] = product(a_ref[...], b_ref[...], mode).astype(BF16)

    return call(
        kernel,
        ids,
        (rows // tall,),
        [
            pl.BlockSpec((tall, depth), lambda i, ids: (i, 0)),
            pl.BlockSpec(right.shape, lambda i, ids: (0, 0)),
        ],
        pl.BlockSpec((tall, width), lambda i, ids: (i, 0)),
        jax.ShapeDtypeStruct((rows, width), BF16),
        (left, right),
        cost(2 * rows * depth * width, 2 * (rows * depth + depth * width + rows * width)),
    )


def pair_kernel(ids, left_a, right_a, left_b, right_b, mode, scales, blocks):
    rows = left_a.shape[0]
    width = right_a.shape[1] if mode == "NN" else right_a.shape[0]
    deep_a, deep_b = left_a.shape[1], left_b.shape[1]
    tall, wide = rows // blocks, tile_of(width, 1024)
    unit = tile_of(wide, 512)

    def kernel(ids_ref, a_ref, b_ref, c_ref, d_ref, s_ref, out_ref):
        for part in range(wide // unit):
            here = slice(part * unit, (part + 1) * unit)
            if mode == "NN":
                one = product(a_ref[...], b_ref[:, here], mode)
                two = product(c_ref[...], d_ref[:, here], mode)
            else:
                one = product(a_ref[...], b_ref[here, :], mode) * s_ref[0:1, here]
                two = product(c_ref[...], d_ref[here, :], mode) * s_ref[1:2, here]
            out_ref[:, here] = (one + two).astype(BF16)

    def weight(deep):
        if mode == "NN":
            return pl.BlockSpec((deep, wide), lambda j, i, ids: (0, j))
        return pl.BlockSpec((wide, deep), lambda j, i, ids: (j, 0))

    return call(
        kernel,
        ids,
        (width // wide, blocks),
        [
            pl.BlockSpec((tall, deep_a), lambda j, i, ids: (i, 0)),
            weight(deep_a),
            pl.BlockSpec((tall, deep_b), lambda j, i, ids: (i, 0)),
            weight(deep_b),
            pl.BlockSpec((2, wide), lambda j, i, ids: (0, j)),
        ],
        pl.BlockSpec((tall, wide), lambda j, i, ids: (ids[0] ^ i, j)),
        jax.ShapeDtypeStruct((rows, width), BF16),
        (left_a, right_a, left_b, right_b, scales),
        cost(2 * rows * (deep_a + deep_b) * width, 2 * (2 * rows + width) * (deep_a + deep_b) + 2 * rows * width),
    )


def half_grad_kernel(ids, left, right, mine, added=None):
    rows, depth = left.shape
    width = right.shape[1] // 2
    tall = tile_of(depth, 1024)
    unit = tile_of(width, 512)

    def kernel(ids_ref, a_ref, b_ref, *refs):
        out_ref = refs[-1]
        for part in range(width // unit):
            here = slice(part * unit, (part + 1) * unit)
            value = product(a_ref[...], b_ref[:, here], "TN")
            if added is not None:
                value = value + refs[0][:, here].astype(F32)
            out_ref[:, here] = value.astype(BF16)

    if mine:
        pick = pl.BlockSpec((rows, width), lambda i, ids: (0, ids[1]))
    else:
        pick = pl.BlockSpec((rows, width), lambda i, ids: (0, 1 - ids[1]))
    tile = pl.BlockSpec((tall, width), lambda i, ids: (i, 0))
    extra = [] if added is None else [added]
    return call(
        kernel,
        ids,
        (depth // tall,),
        [pl.BlockSpec((rows, tall), lambda i, ids: (0, i)), pick] + [tile] * len(extra),
        tile,
        jax.ShapeDtypeStruct((depth, width), BF16),
        (left, right, *extra),
        cost(2 * rows * depth * width, 2 * (rows * depth + rows * width + (1 + len(extra)) * depth * width)),
    )


def rotary_tables(length):
    position = jnp.arange(length, dtype=F32)[:, None]
    lane = jnp.arange(128)
    half = ROTARY // 2
    frequency = 10000.0 ** (-2.0 * (lane % half).astype(F32) / ROTARY)
    angles = position * frequency[None, :]
    sine = jnp.sin(angles)
    return (
        jnp.where(lane < ROTARY, jnp.cos(angles), 1.0),
        jnp.where(lane < half, -sine, 0.0),
        jnp.where((lane >= half) & (lane < ROTARY), sine, 0.0),
    )


def flip(value, axis, bit, size):
    return lax.ppermute(value, axis, [(i, i ^ bit) for i in range(size)])


def sum_over(value, axis, size):
    bit = 1
    while bit < size:
        value = value + flip(value, axis, bit, size)
        bit *= 2
    return value


def gather_rows(rows, size):
    if size != 4:
        return [rows] + [flip(rows, "tensor", k, size) for k in range(1, size)]
    half = rows.shape[0] // 2
    one = flip(rows, "tensor", 1, size)
    two = flip(rows, "tensor", 2, size)
    upper = flip(two[:half], "tensor", 1, size)
    lower = flip(one[half:], "tensor", 2, size)
    return [rows, one, two, upper, lower]


def swap_core(value, size):
    return flip(value, "dp", 1, size)


def line_sum(value, chip, core, size):
    chips = size // 2
    depth, width = value.shape
    chunks = value.reshape(chips, depth // chips, width)

    def chunk(index):
        return lax.dynamic_index_in_dim(chunks, jnp.clip(index, 0, chips - 1), 0, keepdims=False)

    up = down = None
    for step in range(1, chips):
        send_up, send_down = chunk(chips - step + chip), chunk(chip + step - chips)
        if step > 1:
            send_up = (send_up.astype(F32) + up.astype(F32)).astype(BF16)
            send_down = (send_down.astype(F32) + down.astype(F32)).astype(BF16)
        pairs = [(i, i + 1) for i in range(step)]
        up = lax.ppermute(send_up, "dp", [(2 * a + k, 2 * b + k) for a, b in pairs for k in (0, 1)])
        pairs = [(chips - 1 - i, chips - 2 - i) for i in range(step)]
        down = lax.ppermute(send_down, "dp", [(2 * a + k, 2 * b + k) for a, b in pairs for k in (0, 1)])
    total = chunk(chip).astype(F32)
    if chips > 1:
        total = total + up.astype(F32) + down.astype(F32)
    total = total.astype(BF16).reshape(2, depth // size, width)
    mine = lax.dynamic_index_in_dim(total, core, 0, keepdims=False)
    other = swap_core(lax.dynamic_index_in_dim(total, 1 - core, 0, keepdims=False), size)
    low = jnp.where(core == 0, mine, other)
    high = jnp.where(core == 0, other, mine)
    return jnp.concatenate([low, high], axis=1).astype(F32)


def body(
    layer_input,
    cotangent,
    firstgain,
    firstbias,
    secondgain,
    secondbias,
    project,
    projbias,
    merging,
    mergebias,
    expand,
    expandbias,
    shrink,
    shrinkbias,
):
    n_dp, n_tensor = lax.axis_size("dp"), lax.axis_size("tensor")
    dp_at, tensor_at = lax.axis_index("dp"), lax.axis_index("tensor")
    chip, core = dp_at // 2, dp_at % 2
    ids = jnp.stack([tensor_at, core]).astype(jnp.int32)
    own_count, width = layer_input.shape
    group_count = own_count * n_tensor
    assert group_count == LENGTH
    depth = width // n_dp
    heads = project.shape[1]
    mixed_width = heads * 3 * HEAD_DIM
    hidden_width = expand.shape[1]

    rows_pieces = gather_rows(layer_input, n_tensor)
    own_project = project.reshape(depth, mixed_width)
    w_project = lax.all_gather(own_project, "dp", axis=0, tiled=True)
    w_merge = lax.all_gather(merging, "dp", axis=1, tiled=True)
    w_expand = lax.all_gather(expand, "dp", axis=0, tiled=True)
    w_shrink = lax.all_gather(shrink, "dp", axis=1, tiled=True)
    seed_pieces = gather_rows(cotangent, n_tensor)

    packed = jnp.concatenate(
        [firstgain, firstbias, secondgain, secondbias, mergebias, shrinkbias, expandbias, projbias.reshape(-1)]
    )
    slots = jnp.where(jnp.arange(n_dp)[:, None] == dp_at, packed[None, :], jnp.zeros((), BF16))
    slots = sum_over(slots, "dp", n_dp).astype(F32)
    vectors = jnp.transpose(slots[:, : 6 * depth].reshape(n_dp, 6, depth), (1, 0, 2)).reshape(6, width)
    at = 6 * depth
    part = hidden_width // n_dp
    b_expand = slots[:, at : at + part].reshape(1, hidden_width)
    at += part
    b_project = jnp.transpose(slots[:, at:].reshape(n_dp, heads, -1), (1, 0, 2)).reshape(1, mixed_width)

    tables = rotary_tables(LENGTH)
    unit = own_count // 2
    first, second = norm_kernel(ids, rows_pieces, vectors, unit)
    seed = jnp.concatenate(seed_pieces, axis=0)

    mixed = mixed_kernel(ids, first, w_project, b_project, tables, n_tensor)
    context, lse = attend_kernel(ids, mixed, n_tensor)
    cgrad = plain_kernel(ids, seed, w_merge, "NT")
    mgrad, mixed_sum = attend_back_kernel(ids, mixed, cgrad, context, lse, tables, n_tensor)
    hidden, slope = expand_kernel(ids, second, w_expand, b_expand)
    pgrad, expand_sum = shrink_back_kernel(ids, seed, w_shrink, slope)

    def grad_of(left, right):
        other = half_grad_kernel(ids, left, right, False)
        came = swap_core(other, n_dp)
        return line_sum(half_grad_kernel(ids, left, right, True, came), chip, core, n_dp)

    merging_grad = jnp.transpose(grad_of(seed, context))
    project_grad = grad_of(first, mgrad)
    shrink_grad = jnp.transpose(grad_of(seed, hidden))
    expand_grad = grad_of(second, pgrad)

    ones = jnp.ones((2, width), F32)
    branches = pair_kernel(ids, context, w_merge, hidden, w_shrink, "NN", ones, n_tensor)
    summed = lax.psum_scatter(branches, "tensor", scatter_dimension=0, tiled=True).astype(F32)
    layer_output = (layer_input.astype(F32) + summed + (vectors[4] + vectors[5])).astype(BF16)

    gains = jnp.stack([vectors[0], vectors[2]])
    back = pair_kernel(ids, mgrad, w_project, pgrad, w_expand, "NT", gains, n_tensor)
    back = lax.psum_scatter(back, "tensor", scatter_dimension=0, tiled=True).astype(F32)
    data = layer_input.astype(F32)
    centre = data - jnp.mean(data, axis=-1, keepdims=True)
    rstd = lax.rsqrt(jnp.mean(centre * centre, axis=-1, keepdims=True) + EPSILON)
    scaled = centre * rstd
    inner = jnp.mean(back * scaled, axis=-1, keepdims=True)
    seed_own = cotangent.astype(F32)
    input_grad = seed_own + rstd * (back - jnp.mean(back, axis=-1, keepdims=True) - scaled * inner)

    seed_sum = sum_over(jnp.sum(seed_own, axis=0, keepdims=True), "tensor", n_tensor)
    sums = sum_over(jnp.concatenate([seed_sum, expand_sum, mixed_sum], axis=1), "dp", n_dp)
    seed_sum = lax.dynamic_slice_in_dim(sums[0, :width], dp_at * depth, depth)
    expand_sum = sums[0, width : width + hidden_width]
    mixed_sum = sums[0, width + hidden_width :]
    expandbias_grad = lax.dynamic_slice_in_dim(expand_sum, dp_at * part, part)
    piece = projbias.shape[1]
    projbias_grad = lax.dynamic_slice_in_dim(mixed_sum.reshape(heads, -1), dp_at * piece, piece, axis=1)

    def norm_grads(weight, weight_grad, total, gain, bias):
        weight = weight.astype(F32)
        gain, bias = gain.astype(F32), bias.astype(F32)
        scaled_sum = jnp.sum(weight * (weight_grad - bias[:, None] * total[None, :]), axis=1) / gain
        return scaled_sum, jnp.sum(weight * total[None, :], axis=1)

    norms = jnp.stack(
        norm_grads(own_project, project_grad, mixed_sum, firstgain, firstbias)
        + norm_grads(expand, expand_grad, expand_sum, secondgain, secondbias)
    )
    norms = sum_over(norms, "tensor", n_tensor)
    return (
        layer_output,
        input_grad,
        norms[0],
        norms[1],
        norms[2],
        norms[3],
        project_grad.reshape(project.shape),
        projbias_grad,
        merging_grad,
        seed_sum,
        expand_grad,
        expandbias_grad,
        shrink_grad,
        seed_sum,
    )


def solution(mesh):
    specs = (
        P(("dp", "tensor"), None),
        P(("dp", "tensor"), None),
        P("dp"),
        P("dp"),
        P("dp"),
        P("dp"),
        P("dp", "tensor", None),
        P("tensor", "dp"),
        P("tensor", "dp"),
        P("dp"),
        P("dp", "tensor"),
        P(("tensor", "dp")),
        P("tensor", "dp"),
        P("dp"),
    )
    return jax.shard_map(body, mesh=mesh, in_specs=specs, out_specs=specs, check_vma=False)
```

```python
import jax
import jax.numpy as jnp
from jax import lax
from jax.experimental import pallas as pl
from jax.experimental.pallas import tpu as pltpu
from jax.sharding import PartitionSpec as P

HEAD_DIM = 256
ROTARY = 64
LENGTH = 2048
EPSILON = 1e-05
BIG = -1e30
F32 = jnp.float32
BF16 = jnp.bfloat16
DIMS = {
    "NN": (((1,), (0,)), ((), ())),
    "NT": (((1,), (1,)), ((), ())),
    "TN": (((0,), (0,)), ((), ())),
}


def product(left, right, mode):
    return lax.dot_general(left, right, DIMS[mode], preferred_element_type=F32)


def params():
    return pltpu.CompilerParams(vmem_limit_bytes=56 << 20)


def cost(flops, nbytes, transcendentals=0):
    return pl.CostEstimate(
        flops=int(flops), bytes_accessed=int(nbytes), transcendentals=int(transcendentals)
    )


def tile_of(width, most):
    best = 128
    for size in range(128, most + 1, 128):
        if width % size == 0:
            best = size
    return best


def call(kernel, ids, grid, in_specs, out_specs, out_shape, args, cost_of, scratch=(), after=()):
    count = len(args)

    def run(ids_ref, *refs):
        kernel(ids_ref, *refs[:count], *refs[count + len(after) :])

    return pl.pallas_call(
        run,
        grid_spec=pltpu.PrefetchScalarGridSpec(
            num_scalar_prefetch=1,
            grid=grid,
            in_specs=list(in_specs) + [pl.BlockSpec(memory_space=pl.ANY)] * len(after),
            out_specs=out_specs,
            scratch_shapes=list(scratch),
        ),
        out_shape=out_shape,
        compiler_params=params(),
        cost_estimate=cost_of,
    )(ids, *args, *after)


def norm_kernel(ids, pieces, vectors, unit, after=()):
    rows = sum(piece.shape[0] for piece in pieces)
    width = pieces[0].shape[1]
    starts = []
    for piece in pieces:
        starts.append((starts[-1][1] if starts else 0,) * 2)
        starts[-1] = (starts[-1][0], starts[-1][0] + piece.shape[0] // unit)

    def kernel(ids_ref, *refs):
        step = pl.program_id(0)
        vec = refs[len(pieces)]
        first_ref, second_ref = refs[len(pieces) + 1 :]
        for (low, high), piece_ref in zip(starts, refs):

            @pl.when((step >= low) & (step < high))
            def _(piece_ref=piece_ref):
                data = piece_ref[...].astype(F32)
                centre = data - jnp.mean(data, axis=-1, keepdims=True)
                spread = jnp.mean(centre * centre, axis=-1, keepdims=True)
                scaled = centre * lax.rsqrt(spread + EPSILON)
                first_ref[...] = (scaled * vec[0:1, :] + vec[1:2, :]).astype(BF16)
                second_ref[...] = (scaled * vec[2:3, :] + vec[3:4, :]).astype(BF16)

    def spec(low, high):
        return pl.BlockSpec((unit, width), lambda i, ids: (jnp.clip(i - low, 0, high - low - 1), 0))

    out = pl.BlockSpec((unit, width), lambda i, ids: (i, 0))
    shape = jax.ShapeDtypeStruct((rows, width), BF16)
    return call(
        kernel,
        ids,
        (rows // unit,),
        [spec(low, high) for low, high in starts] + [pl.BlockSpec(vectors.shape, lambda i, ids: (0, 0))],
        [out, out],
        [shape, shape],
        (*pieces, vectors),
        cost(12 * rows * width, 6 * rows * width),
        after=after,
    )


def rotate(block, cos, sin_low, sin_high, sign):
    lead = block[:, :128]
    turned = (
        lead * cos
        + sign * (pltpu.roll(lead, 96, 1) * sin_low + pltpu.roll(lead, 32, 1) * sin_high)
    )
    return jnp.concatenate([turned, block[:, 128:]], axis=1)


def mixed_kernel(ids, first, weight, bias, tables, blocks, after=()):
    rows, depth = first.shape
    heads = weight.shape[1] // (3 * HEAD_DIM)
    unit = rows // blocks
    wide = 3 * HEAD_DIM

    def kernel(ids_ref, a_ref, w_ref, b_ref, cos, low, high, out_ref):
        for part in range(3):
            here = slice(part * HEAD_DIM, (part + 1) * HEAD_DIM)
            value = product(a_ref[...], w_ref[:, here], "NN") + b_ref[:, here]
            if part < 2:
                value = rotate(value, cos[...], low[...], high[...], 1.0)
            out_ref[:, here] = value.astype(BF16)

    table = pl.BlockSpec((unit, 128), lambda j, i, ids: (ids[0] ^ i, 0))
    return call(
        kernel,
        ids,
        (heads, blocks),
        [
            pl.BlockSpec((unit, depth), lambda j, i, ids: (i, 0)),
            pl.BlockSpec((depth, wide), lambda j, i, ids: (0, j)),
            pl.BlockSpec((1, wide), lambda j, i, ids: (0, j)),
            table,
            table,
            table,
        ],
        pl.BlockSpec((unit, wide), lambda j, i, ids: (i, j)),
        jax.ShapeDtypeStruct((rows, heads * wide), BF16),
        (first, weight, bias, *tables),
        cost(2 * rows * depth * heads * wide, 2 * (heads * rows * depth + depth * heads * wide + rows * heads * wide)),
        after=after,
    )


def attend_kernel(ids, mixed, blocks, after=()):
    rows, width = mixed.shape
    heads = width // (3 * HEAD_DIM)
    unit = rows // blocks
    scale = HEAD_DIM ** (-0.5)

    def kernel(ids_ref, x_ref, ctx_ref, lse_ref, top_s, total_s, acc_s):
        block = pl.program_id(0)
        me = ids_ref[0]
        here = pl.ds(pl.multiple_of((me ^ block) * unit, unit), unit)

        def step(other, diagonal):
            there = pl.ds(pl.multiple_of((me ^ other) * unit, unit), unit)
            for head in range(heads):
                at = 3 * HEAD_DIM * head
                scores = (
                    product(
                        x_ref[here, at : at + HEAD_DIM],
                        x_ref[there, at + HEAD_DIM : at + 2 * HEAD_DIM],
                        "NT",
                    )
                    * scale
                )
                value = x_ref[there, at + 2 * HEAD_DIM : at + 3 * HEAD_DIM]
                if diagonal:
                    row_at = lax.broadcasted_iota(jnp.int32, scores.shape, 0)
                    col_at = lax.broadcasted_iota(jnp.int32, scores.shape, 1)
                    scores = jnp.where(col_at <= row_at, scores, BIG)
                    top = jnp.max(scores, axis=1, keepdims=True)
                    weight = jnp.exp(scores - top)
                    top_s[head] = top
                    total_s[head] = jnp.sum(weight, axis=1, keepdims=True)
                    acc_s[head] = product(weight.astype(BF16), value, "NN")
                else:
                    before = top_s[head]
                    top = jnp.maximum(before, jnp.max(scores, axis=1, keepdims=True))
                    weight = jnp.exp(scores - top)
                    shrunk = jnp.exp(before - top)
                    top_s[head] = top
                    total_s[head] = total_s[head] * shrunk + jnp.sum(weight, axis=1, keepdims=True)
                    acc_s[head] = acc_s[head] * shrunk + product(weight.astype(BF16), value, "NN")

        step(block, True)

        @pl.loop(0, block)
        def _(other):
            step(other, False)

        for head in range(heads):
            at = HEAD_DIM * head
            ctx_ref[:, at : at + HEAD_DIM] = (acc_s[head] / total_s[head]).astype(BF16)
            log_total = top_s[head] + jnp.log(total_s[head])
            lse_ref[head, 0] = jnp.transpose(jnp.broadcast_to(log_total, (unit, 128)))[:8]

    return call(
        kernel,
        ids,
        (blocks,),
        [pl.BlockSpec((rows, width), lambda b, ids: (0, 0))],
        [
            pl.BlockSpec((unit, heads * HEAD_DIM), lambda b, ids: (ids[0] ^ b, 0)),
            pl.BlockSpec((heads, 1, 8, unit), lambda b, ids: (0, b, 0, 0)),
        ],
        [
            jax.ShapeDtypeStruct((rows, heads * HEAD_DIM), BF16),
            jax.ShapeDtypeStruct((heads, blocks, 8, unit), F32),
        ],
        (mixed,),
        cost(2 * heads * rows * rows * HEAD_DIM, 3 * rows * width, heads * rows * rows // 2),
        [
            pltpu.VMEM((heads, unit, 1), F32),
            pltpu.VMEM((heads, unit, 1), F32),
            pltpu.VMEM((heads, unit, HEAD_DIM), F32),
        ],
        after=after,
    )


def attend_back_kernel(ids, mixed, grad, context, lse, tables, blocks, after=()):
    rows, width = mixed.shape
    heads = width // (3 * HEAD_DIM)
    unit = rows // blocks
    scale = HEAD_DIM ** (-0.5)

    def kernel(ids_ref, x_ref, g_ref, c_ref, lse_ref, cos, low, high, out_ref, sum_ref, dk_s, dv_s, dq_s, inner_s):
        turn = pl.program_id(0)
        block = blocks - 1 - turn
        me = ids_ref[0]

        @pl.when(turn == 0)
        def _():
            dk_s[...] = jnp.zeros_like(dk_s)
            dv_s[...] = jnp.zeros_like(dv_s)
            sum_ref[...] = jnp.zeros_like(sum_ref)

        here = pl.ds(pl.multiple_of((me ^ block) * unit, unit), unit)
        for head in range(heads):
            cols = slice(HEAD_DIM * head, HEAD_DIM * (head + 1))
            inner = jnp.sum(g_ref[here, cols].astype(F32) * c_ref[here, cols].astype(F32), axis=1, keepdims=True)
            inner_s[head] = jnp.transpose(jnp.broadcast_to(inner, (unit, 128)))[:8]

        def step(other, diagonal):
            there = pl.ds(pl.multiple_of((me ^ other) * unit, unit), unit)
            for head in range(heads):
                at = 3 * HEAD_DIM * head
                query = x_ref[here, at : at + HEAD_DIM]
                seed = g_ref[here, HEAD_DIM * head : HEAD_DIM * (head + 1)]
                key = x_ref[there, at + HEAD_DIM : at + 2 * HEAD_DIM]
                value = x_ref[there, at + 2 * HEAD_DIM : at + 3 * HEAD_DIM]
                scores = product(key, query, "NT") * scale
                prob = jnp.exp(scores - lse_ref[head, 0][:1])
                if diagonal:
                    key_at = lax.broadcasted_iota(jnp.int32, scores.shape, 0)
                    row_at = lax.broadcasted_iota(jnp.int32, scores.shape, 1)
                    prob = jnp.where(key_at <= row_at, prob, 0.0)
                dprob = product(value, seed, "NT")
                dscore = (prob * (dprob - inner_s[head][:1])).astype(BF16)
                dv_s[head, other] += product(prob.astype(BF16), seed, "NN")
                dk_s[head, other] += product(dscore, query, "NN")
                dquery = product(dscore, key, "TN")
                if diagonal:
                    dq_s[head] = dquery
                else:
                    dq_s[head] += dquery

        step(block, True)

        @pl.loop(0, block)
        def _(other):
            step(other, False)

        for head in range(heads):
            at = 3 * HEAD_DIM * head
            dquery = rotate(dq_s[head] * scale, cos[...], low[...], high[...], -1.0)
            dkey = rotate(dk_s[head, block] * scale, cos[...], low[...], high[...], -1.0)
            for part, value in enumerate((dquery, dkey, dv_s[head, block])):
                cols = slice(at + part * HEAD_DIM, at + (part + 1) * HEAD_DIM)
                rounded = value.astype(BF16)
                out_ref[:, cols] = rounded
                sum_ref[:, cols] += jnp.sum(rounded.astype(F32), axis=0, keepdims=True)

    def whole(cols):
        return pl.BlockSpec((rows, cols), lambda b, ids: (0, 0))

    table = pl.BlockSpec((unit, 128), lambda b, ids: (blocks - 1 - b, 0))
    return call(
        kernel,
        ids,
        (blocks,),
        [
            whole(width),
            whole(heads * HEAD_DIM),
            whole(heads * HEAD_DIM),
            pl.BlockSpec((heads, 1, 8, unit), lambda b, ids: (0, blocks - 1 - b, 0, 0)),
            table,
            table,
            table,
        ],
        [
            pl.BlockSpec((unit, width), lambda b, ids: (ids[0] ^ (blocks - 1 - b), 0)),
            pl.BlockSpec((1, width), lambda b, ids: (0, 0)),
        ],
        [jax.ShapeDtypeStruct((rows, width), BF16), jax.ShapeDtypeStruct((1, width), F32)],
        (mixed, grad, context, lse, *tables),
        cost(5 * heads * rows * rows * HEAD_DIM, 6 * rows * width, heads * rows * rows // 2),
        [
            pltpu.VMEM((heads, blocks, unit, HEAD_DIM), F32),
            pltpu.VMEM((heads, blocks, unit, HEAD_DIM), F32),
            pltpu.VMEM((heads, unit, HEAD_DIM), F32),
            pltpu.VMEM((heads, 8, unit), F32),
        ],
        after=after,
    )


def expand_kernel(ids, second, weight, bias, after=()):
    rows, depth = second.shape
    width = weight.shape[1]
    tall, wide = tile_of(rows, 1024), tile_of(width, 1024)
    unit = tile_of(wide, 512)

    def kernel(ids_ref, a_ref, w_ref, b_ref, hidden_ref, slope_ref):
        for part in range(wide // unit):
            here = slice(part * unit, (part + 1) * unit)
            pre = product(a_ref[...], w_ref[:, here], "NN") + b_ref[:, here]
            phi = 0.5 + 0.5 * lax.erf(pre * 0.7071067811865476)
            hidden_ref[:, here] = (pre * phi).astype(BF16)
            slope = phi + pre * (jnp.exp(-0.5 * pre * pre) * 0.3989422804014327)
            slope_ref[:, here] = slope.astype(BF16)

    out = pl.BlockSpec((tall, wide), lambda i, j, ids: (i, j))
    shape = jax.ShapeDtypeStruct((rows, width), BF16)
    return call(
        kernel,
        ids,
        (rows // tall, width // wide),
        [
            pl.BlockSpec((tall, depth), lambda i, j, ids: (i, 0)),
            pl.BlockSpec((depth, wide), lambda i, j, ids: (0, j)),
            pl.BlockSpec((1, wide), lambda i, j, ids: (0, j)),
        ],
        [out, out],
        [shape, shape],
        (second, weight, bias),
        cost(2 * rows * depth * width, 2 * (rows * depth + 2 * depth * width + 2 * rows * width), 2 * rows * width),
        after=after,
    )


def stack_kernel(ids, pieces, unit, after=()):
    rows = sum(piece.shape[0] for piece in pieces)
    width = pieces[0].shape[1]
    ends = [0]
    for piece in pieces:
        ends.append(ends[-1] + piece.shape[0] // unit)

    def kernel(ids_ref, *refs):
        step = pl.program_id(0)
        for low, high, piece_ref in zip(ends, ends[1:], refs):

            @pl.when((step >= low) & (step < high))
            def _(piece_ref=piece_ref):
                refs[-1][...] = piece_ref[...]

    def spec(low, high):
        return pl.BlockSpec((unit, width), lambda i, ids: (jnp.clip(i - low, 0, high - low - 1), 0))

    return call(
        kernel,
        ids,
        (rows // unit,),
        [spec(low, high) for low, high in zip(ends, ends[1:])],
        pl.BlockSpec((unit, width), lambda i, ids: (i, 0)),
        jax.ShapeDtypeStruct((rows, width), BF16),
        tuple(pieces),
        cost(0, 4 * rows * width),
        after=after,
    )


def shrink_back_kernel(ids, seed, weight, slope, after=()):
    rows, depth = seed.shape
    width = weight.shape[0]
    tall, wide = tile_of(rows, 1024), tile_of(width, 1024)
    unit = tile_of(wide, 512)

    def kernel(ids_ref, a_ref, w_ref, s_ref, out_ref, sum_ref):
        @pl.when(pl.program_id(1) == 0)
        def _():
            sum_ref[...] = jnp.zeros_like(sum_ref)

        for part in range(wide // unit):
            here = slice(part * unit, (part + 1) * unit)
            grad = product(a_ref[...], w_ref[here, :], "NT") * s_ref[:, here].astype(F32)
            rounded = grad.astype(BF16)
            out_ref[:, here] = rounded
            sum_ref[:, here] += jnp.sum(rounded.astype(F32), axis=0, keepdims=True)

    tile = pl.BlockSpec((tall, wide), lambda j, i, ids: (i, j))
    return call(
        kernel,
        ids,
        (width // wide, rows // tall),
        [
            pl.BlockSpec((tall, depth), lambda j, i, ids: (i, 0)),
            pl.BlockSpec((wide, depth), lambda j, i, ids: (j, 0)),
            tile,
        ],
        [tile, pl.BlockSpec((1, wide), lambda j, i, ids: (0, j))],
        [jax.ShapeDtypeStruct((rows, width), BF16), jax.ShapeDtypeStruct((1, width), F32)],
        (seed, weight, slope),
        cost(2 * rows * depth * width, 2 * (2 * rows * depth + depth * width + 2 * rows * width)),
        after=after,
    )


def halves_kernel(ids, left, mine, other, after=()):
    rows, depth = left.shape
    width = mine.shape[1]
    tall = tile_of(rows, 512)

    def kernel(ids_ref, a_ref, m_ref, o_ref, out_ref):
        @pl.when(ids_ref[1] == 0)
        def _():
            out_ref[:, :width] = product(a_ref[...], m_ref[...], "NN").astype(BF16)
            out_ref[:, width:] = product(a_ref[...], o_ref[...], "NN").astype(BF16)

        @pl.when(ids_ref[1] != 0)
        def _():
            out_ref[:, :width] = product(a_ref[...], o_ref[...], "NN").astype(BF16)
            out_ref[:, width:] = product(a_ref[...], m_ref[...], "NN").astype(BF16)

    whole = pl.BlockSpec((depth, width), lambda i, ids: (0, 0))
    return call(
        kernel,
        ids,
        (rows // tall,),
        [pl.BlockSpec((tall, depth), lambda i, ids: (i, 0)), whole, whole],
        pl.BlockSpec((tall, 2 * width), lambda i, ids: (i, 0)),
        jax.ShapeDtypeStruct((rows, 2 * width), BF16),
        (left, mine, other),
        cost(4 * rows * depth * width, 2 * (rows * depth + 2 * depth * width + 2 * rows * width)),
        after=after,
    )


def branches_kernel(ids, context, mine, other, hidden, shrink, blocks, after=()):
    rows, deep_b = hidden.shape
    depth, half = mine.shape
    tall, wide = rows // blocks, tile_of(depth, 1024)
    unit = tile_of(wide, 512)

    def kernel(ids_ref, a_ref, b_ref, m_ref, o_ref, h_ref, s_ref, out_ref):
        for part in range(wide // unit):
            here = slice(part * unit, (part + 1) * unit)
            value = product(h_ref[...], s_ref[:, here], "NN")
            value = value + product(a_ref[...], m_ref[here, :], "NT")
            value = value + product(b_ref[...], o_ref[here, :], "NT")
            out_ref[:, here] = value.astype(BF16)

    return call(
        kernel,
        ids,
        (depth // wide, blocks),
        [
            pl.BlockSpec((tall, half), lambda j, i, ids: (i, ids[1])),
            pl.BlockSpec((tall, half), lambda j, i, ids: (i, 1 - ids[1])),
            pl.BlockSpec((wide, half), lambda j, i, ids: (j, 0)),
            pl.BlockSpec((wide, half), lambda j, i, ids: (j, 0)),
            pl.BlockSpec((tall, deep_b), lambda j, i, ids: (i, 0)),
            pl.BlockSpec((deep_b, wide), lambda j, i, ids: (0, j)),
        ],
        pl.BlockSpec((tall, wide), lambda j, i, ids: (ids[0] ^ i, j)),
        jax.ShapeDtypeStruct((rows, depth), BF16),
        (context, context, mine, other, hidden, shrink),
        cost(2 * rows * (2 * half + deep_b) * depth, 2 * (2 * rows + depth) * (2 * half + deep_b) + 2 * rows * depth),
        after=after,
    )


def back_kernel(ids, left_a, right_a, left_b, right_b, scales, block, blocks, after=()):
    rows = left_a.shape[0] // blocks
    width = right_a.shape[0]
    deep_a, deep_b = left_a.shape[1], left_b.shape[1]
    wide = tile_of(width, 512)

    def kernel(ids_ref, a_ref, b_ref, c_ref, d_ref, s_ref, out_ref):
        one = product(a_ref[...], b_ref[...], "NT") * s_ref[0:1, :]
        two = product(c_ref[...], d_ref[...], "NT") * s_ref[1:2, :]
        out_ref[...] = (one + two).astype(BF16)

    return call(
        kernel,
        ids,
        (width // wide,),
        [
            pl.BlockSpec((rows, deep_a), lambda j, ids: (block, 0)),
            pl.BlockSpec((wide, deep_a), lambda j, ids: (j, 0)),
            pl.BlockSpec((rows, deep_b), lambda j, ids: (block, 0)),
            pl.BlockSpec((wide, deep_b), lambda j, ids: (j, 0)),
            pl.BlockSpec((2, wide), lambda j, ids: (0, j)),
        ],
        pl.BlockSpec((rows, wide), lambda j, ids: (0, j)),
        jax.ShapeDtypeStruct((rows, width), BF16),
        (left_a, right_a, left_b, right_b, scales),
        cost(2 * rows * (deep_a + deep_b) * width, 2 * (rows + width) * (deep_a + deep_b) + 2 * rows * width),
        after=after,
    )


def grad_kernel(ids, left, right, weight=None, total=None, after=()):
    rows, depth = left.shape
    width = right.shape[1] // 2
    tall = tile_of(depth, 512)
    steps = depth // tall
    unit = tile_of(width, 512)
    summed = weight is not None

    def kernel(ids_ref, a_ref, b_ref, *refs):
        half = pl.program_id(0)
        other_ref, mine_ref = refs[2:4] if summed else refs
        at = pl.ds(pl.multiple_of(pl.program_id(1) * tall, tall), tall)
        for turn, out_ref in ((0, other_ref), (1, mine_ref)):

            @pl.when(half == turn)
            def _(turn=turn, out_ref=out_ref):
                gain = jnp.zeros((tall, 128), F32)
                shift = jnp.zeros((tall, 128), F32)
                for part in range(width // unit):
                    here = slice(part * unit, (part + 1) * unit)
                    value = product(a_ref[...], b_ref[:, here], "TN")
                    out_ref[:, here] = value.astype(BF16)
                    if summed:
                        held = refs[0][:, here].astype(F32)
                        one, two = held * value, held * refs[1][:, here]
                        for lane in range(0, unit, 128):
                            gain = gain + one[:, lane : lane + 128]
                            shift = shift + two[:, lane : lane + 128]
                if summed:
                    if turn == 0:
                        refs[4][at, :] = gain
                        refs[5][at, :] = shift
                    else:
                        refs[4][at, :] += gain
                        refs[5][at, :] += shift

    def column(half, ids):
        return ids[1] ^ 1 ^ half

    in_specs = [
        pl.BlockSpec((rows, tall), lambda half, i, ids: (0, i)),
        pl.BlockSpec((rows, width), lambda half, i, ids: (0, column(half, ids))),
    ]
    out_specs = [
        pl.BlockSpec((tall, width), lambda half, i, ids: (jnp.where(half == 0, i, steps - 1), 0)),
        pl.BlockSpec((tall, width), lambda half, i, ids: (jnp.where(half == 0, 0, i), 0)),
    ]
    out_shape = [jax.ShapeDtypeStruct((depth, width), BF16)] * 2
    args = (left, right)
    if summed:
        args += (weight, total)
        in_specs += [
            pl.BlockSpec((tall, width), lambda half, i, ids: (i, column(half, ids))),
            pl.BlockSpec((1, width), lambda half, i, ids: (0, column(half, ids))),
        ]
        out_specs += [pl.BlockSpec((depth, 128), lambda half, i, ids: (0, 0))] * 2
        out_shape += [jax.ShapeDtypeStruct((depth, 128), F32)] * 2
    return call(
        kernel,
        ids,
        (2, steps),
        in_specs,
        out_specs,
        out_shape,
        args,
        cost(4 * rows * depth * width, 2 * (2 * rows * depth + 2 * rows * width + 4 * depth * width)),
        after=after,
    )


def add_kernel(ids, arrays, places, count, rows, after=()):
    width = arrays[0].shape[1]

    def kernel(ids_ref, *refs):
        total = refs[0][...].astype(F32)
        for ref in refs[1:-1]:
            total = total + ref[...].astype(F32)
        refs[-1][...] = total.astype(BF16)

    cut = max(1, rows // 256)
    unit = rows // cut

    def spec(place):
        return pl.BlockSpec((unit, width), lambda i, j, ids: (place(i, ids) * cut + j, 0))

    return call(
        kernel,
        ids,
        (count, cut),
        [spec(place) for place in places],
        spec(lambda i, ids: i),
        jax.ShapeDtypeStruct((count * rows, width), BF16),
        tuple(arrays),
        cost(len(arrays) * count * rows * width, 2 * (len(arrays) + 1) * count * rows * width),
        after=after,
    )


def rotary_tables(length):
    position = jnp.arange(length, dtype=F32)[:, None]
    lane = jnp.arange(128)
    half = ROTARY // 2
    frequency = 10000.0 ** (-2.0 * (lane % half).astype(F32) / ROTARY)
    angles = position * frequency[None, :]
    sine = jnp.sin(angles)
    return (
        jnp.where(lane < ROTARY, jnp.cos(angles), 1.0),
        jnp.where(lane < half, -sine, 0.0),
        jnp.where((lane >= half) & (lane < ROTARY), sine, 0.0),
    )


def flip(value, axis, bit, size):
    return lax.ppermute(value, axis, [(i, i ^ bit) for i in range(size)])


def sum_over(value, axis, size):
    bit = 1
    while bit < size:
        value = value + flip(value, axis, bit, size)
        bit *= 2
    return value


def gather_rows(rows, size):
    if size != 4:
        return [rows] + [flip(rows, "tensor", k, size) for k in range(1, size)]
    half = rows.shape[0] // 2
    one = flip(rows, "tensor", 1, size)
    two = flip(rows, "tensor", 2, size)
    upper = flip(two[:half], "tensor", 1, size)
    lower = flip(one[half:], "tensor", 2, size)
    return [rows, one, two, upper, lower]


def swap_core(value, size):
    return flip(value, "dp", 1, size)


class LineSum:
    def __init__(self, ids, first, mine, size):
        self.ids, self.size = ids, size
        self.chips = size // 2
        self.rows = mine.shape[0] // self.chips
        self.bit = 1
        self.parts = [(mine, lambda i, ids: i), (swap_core(first, size), lambda i, ids: i)]

    def add(self, count, place, after):
        places = [lambda i, ids, held=held: held(place(i, ids), ids) for _, held in self.parts]
        return add_kernel(self.ids, [array for array, _ in self.parts], places, count, self.rows, after)

    def step(self, after=()):
        count = self.chips // (2 * self.bit)
        at = 1 + self.bit.bit_length()
        sent = self.add(count, lambda i, ids: 2 * i + 1 - ids[at], after)
        came = flip(sent, "dp", 2 * self.bit, self.size)
        self.parts = [
            (array, lambda i, ids, held=held, at=at: held(2 * i + ids[at], ids)) for array, held in self.parts
        ]
        self.parts.append((came, lambda i, ids: i))
        self.bit *= 2
        return sent

    def finish(self, core, after=()):
        total = self.add(1, lambda i, ids: i, after)
        halves = total.reshape(2, self.rows // 2, total.shape[1])
        mine = lax.dynamic_index_in_dim(halves, core, 0, keepdims=False)
        other = swap_core(lax.dynamic_index_in_dim(halves, 1 - core, 0, keepdims=False), self.size)
        low = jnp.where(core == 0, mine, other)
        high = jnp.where(core == 0, other, mine)
        return total, jnp.concatenate([low, high], axis=1).astype(F32)


def line_gather(shard, chip, core, size):
    depth, width = shard.shape
    halves = shard.reshape(depth, 2, width // 2)
    mine = lax.dynamic_index_in_dim(halves, core, 1, keepdims=False)
    came = swap_core(lax.dynamic_index_in_dim(halves, 1 - core, 1, keepdims=False), size)
    value = jnp.where(core == 0, jnp.stack([mine, came]), jnp.stack([came, mine]))
    value = value.reshape(1, 2 * depth, width // 2)
    bit, done = size // 4, 1
    while bit >= 1:
        other = flip(value, "dp", 2 * bit, size)
        here = (chip // bit) % 2
        value = jnp.where(here == 0, jnp.stack([value, other], axis=1), jnp.stack([other, value], axis=1))
        done *= 2
        value = value.reshape(done, 2 * depth, width // 2)
        bit //= 2
    value = value.reshape(size * depth, width // 2)
    return value, swap_core(value, size)


def body(
    layer_input,
    cotangent,
    firstgain,
    firstbias,
    secondgain,
    secondbias,
    project,
    projbias,
    merging,
    mergebias,
    expand,
    expandbias,
    shrink,
    shrinkbias,
):
    n_dp, n_tensor = lax.axis_size("dp"), lax.axis_size("tensor")
    dp_at, tensor_at = lax.axis_index("dp"), lax.axis_index("tensor")
    chip, core = dp_at // 2, dp_at % 2
    bits = [(chip >> bit) & 1 for bit in range((n_dp // 2).bit_length() - 1)]
    ids = jnp.stack([tensor_at, core, *bits]).astype(jnp.int32)
    own_count, width = layer_input.shape
    group_count = own_count * n_tensor
    assert group_count == LENGTH
    depth = width // n_dp
    heads = project.shape[1]
    mixed_width = heads * 3 * HEAD_DIM
    hidden_width = expand.shape[1]

    unit = own_count // 2
    rows_pieces = gather_rows(layer_input, n_tensor)
    own_project = project.reshape(depth, mixed_width)
    w_project = lax.all_gather(own_project, "dp", axis=0, tiled=True)
    w_expand = lax.all_gather(expand, "dp", axis=0, tiled=True)
    w_shrink = lax.all_gather(shrink, "dp", axis=1, tiled=True)
    merge_mine, merge_other = line_gather(jnp.transpose(merging), chip, core, n_dp)
    later = stack_kernel(ids, [cotangent], unit, after=tuple(rows_pieces[1:]))
    seed_pieces = gather_rows(later, n_tensor)

    packed = jnp.concatenate(
        [firstgain, firstbias, secondgain, secondbias, mergebias, shrinkbias, expandbias, projbias.reshape(-1)]
    )
    slots = jnp.where(jnp.arange(n_dp)[:, None] == dp_at, packed[None, :], jnp.zeros((), BF16))
    slots = sum_over(slots, "dp", n_dp).astype(F32)
    vectors = jnp.transpose(slots[:, : 6 * depth].reshape(n_dp, 6, depth), (1, 0, 2)).reshape(6, width)
    at = 6 * depth
    part = hidden_width // n_dp
    b_expand = slots[:, at : at + part].reshape(1, hidden_width)
    at += part
    b_project = jnp.transpose(slots[:, at:].reshape(n_dp, heads, -1), (1, 0, 2)).reshape(1, mixed_width)

    tables = rotary_tables(LENGTH)
    first, second = norm_kernel(ids, rows_pieces, vectors, unit)
    mixed = mixed_kernel(ids, first, w_project, b_project, tables, n_tensor)
    context, lse = attend_kernel(ids, mixed, n_tensor)
    seed = stack_kernel(ids, seed_pieces, unit, after=(context,))
    merge_a, merge_b = grad_kernel(ids, seed, context)
    merge_sum = LineSum(ids, merge_a, merge_b, n_dp)
    hidden, slope = expand_kernel(ids, second, w_expand, b_expand, after=(merge_b,))
    last = merge_sum.step((hidden,))
    shrink_a, shrink_b = grad_kernel(ids, seed, hidden, after=(last,))
    shrink_sum = LineSum(ids, shrink_a, shrink_b, n_dp)
    cgrad = halves_kernel(ids, seed, merge_mine, merge_other, after=(shrink_b,))
    mgrad, mixed_sum = attend_back_kernel(ids, mixed, cgrad, context, lse, tables, n_tensor)
    last = shrink_sum.step((mgrad,))
    last = merge_sum.step((last,))
    pgrad, expand_sum = shrink_back_kernel(ids, seed, w_shrink, slope, after=(last,))
    expand_a, expand_b, gain_two, bias_two = grad_kernel(ids, second, pgrad, w_expand, expand_sum)
    expand_line = LineSum(ids, expand_a, expand_b, n_dp)
    last = shrink_sum.step((expand_b,))
    last, merging_grad = merge_sum.finish(core, (last,))
    branches = branches_kernel(ids, context, merge_mine, merge_other, hidden, w_shrink, n_tensor, after=(last,))
    last = expand_line.step((branches,))
    project_a, project_b, gain_one, bias_one = grad_kernel(ids, first, mgrad, w_project, mixed_sum, after=(last,))
    project_line = LineSum(ids, project_a, project_b, n_dp)
    gains = jnp.stack([vectors[0], vectors[2]])
    last, shrink_grad = shrink_sum.finish(core, (project_b,))
    back = []
    for block in reversed(range(n_tensor)):
        last = back_kernel(ids, mgrad, w_project, pgrad, w_expand, gains, block, n_tensor, after=(last,))
        back.append(last if block == 0 else flip(last, "tensor", block, n_tensor))
        if block == n_tensor - 1:
            last = project_line.step((last,))
        if block == n_tensor - 2:
            last = expand_line.step((last,))
    last = project_line.step((last,))
    last, expand_grad = expand_line.finish(core, (last,))
    last, project_grad = project_line.finish(core, (last,))
    merging_grad = jnp.transpose(merging_grad)
    shrink_grad = jnp.transpose(shrink_grad)
    back = sum(value.astype(F32) for value in back)

    summed = lax.psum_scatter(branches, "tensor", scatter_dimension=0, tiled=True).astype(F32)
    layer_output = (layer_input.astype(F32) + summed + (vectors[4] + vectors[5])).astype(BF16)

    data = layer_input.astype(F32)
    centre = data - jnp.mean(data, axis=-1, keepdims=True)
    rstd = lax.rsqrt(jnp.mean(centre * centre, axis=-1, keepdims=True) + EPSILON)
    scaled = centre * rstd
    inner = jnp.mean(back * scaled, axis=-1, keepdims=True)
    seed_own = cotangent.astype(F32)
    input_grad = seed_own + rstd * (back - jnp.mean(back, axis=-1, keepdims=True) - scaled * inner)

    sums = jnp.stack(
        [jnp.sum(seed_own, axis=0)] + [jnp.sum(value, axis=1) for value in (gain_one, bias_one, gain_two, bias_two)]
    )
    sums = sum_over(sums, "tensor", n_tensor).reshape(1, -1)
    sums = sum_over(jnp.concatenate([sums, expand_sum, mixed_sum], axis=1), "dp", n_dp)[0]
    norms = lax.dynamic_slice_in_dim(sums[: 5 * width].reshape(5, width), dp_at * depth, depth, axis=1)
    seed_sum, gain_one, bias_one, gain_two, bias_two = norms
    gain_one = (gain_one - firstbias.astype(F32) * bias_one) / firstgain.astype(F32)
    gain_two = (gain_two - secondbias.astype(F32) * bias_two) / secondgain.astype(F32)
    expand_sum = sums[5 * width : 5 * width + hidden_width]
    mixed_sum = sums[5 * width + hidden_width :]
    expandbias_grad = lax.dynamic_slice_in_dim(expand_sum, dp_at * part, part)
    piece = projbias.shape[1]
    projbias_grad = lax.dynamic_slice_in_dim(mixed_sum.reshape(heads, -1), dp_at * piece, piece, axis=1)
    return (
        layer_output,
        input_grad,
        gain_one,
        bias_one,
        gain_two,
        bias_two,
        project_grad.reshape(project.shape),
        projbias_grad,
        merging_grad,
        seed_sum,
        expand_grad,
        expandbias_grad,
        shrink_grad,
        seed_sum,
    )


def solution(mesh):
    specs = (
        P(("dp", "tensor"), None),
        P(("dp", "tensor"), None),
        P("dp"),
        P("dp"),
        P("dp"),
        P("dp"),
        P("dp", "tensor", None),
        P("tensor", "dp"),
        P("tensor", "dp"),
        P("dp"),
        P("dp", "tensor"),
        P(("tensor", "dp")),
        P("tensor", "dp"),
        P("dp"),
    )
    return jax.shard_map(body, mesh=mesh, in_specs=specs, out_specs=specs, check_vma=False)
```

```python
import jax
import jax.numpy as jnp
from jax import lax
from jax.experimental import pallas as pl
from jax.experimental.pallas import tpu as pltpu
from jax.sharding import PartitionSpec as P

HEAD_DIM = 256
ROTARY = 64
LENGTH = 2048
EPSILON = 1e-05
BIG = -1e30
F32 = jnp.float32
BF16 = jnp.bfloat16
DIMS = {
    "NN": (((1,), (0,)), ((), ())),
    "NT": (((1,), (1,)), ((), ())),
    "TN": (((0,), (0,)), ((), ())),
}


def product(left, right, mode):
    return lax.dot_general(left, right, DIMS[mode], preferred_element_type=F32)


def params():
    return pltpu.CompilerParams(vmem_limit_bytes=56 << 20)


def cost(lag):
    return pl.CostEstimate(flops=int(lag * 1e9), bytes_accessed=0, transcendentals=0)


def tile_of(width, most):
    best = 128
    for size in range(128, most + 1, 128):
        if width % size == 0:
            best = size
    return best


def call(kernel, ids, grid, in_specs, out_specs, out_shape, args, name, scratch=(), after=(), kept=(), lag=0.05):
    count = len(args)
    unread = tuple(kept) + tuple(after)

    def run(ids_ref, *refs):
        kernel(ids_ref, *refs[:count], *refs[count + len(unread) :])

    return pl.pallas_call(
        run,
        grid_spec=pltpu.PrefetchScalarGridSpec(
            num_scalar_prefetch=1,
            grid=grid,
            in_specs=list(in_specs) + [pl.BlockSpec(memory_space=pl.ANY)] * len(unread),
            out_specs=out_specs,
            scratch_shapes=list(scratch),
        ),
        out_shape=out_shape,
        input_output_aliases={1 + count + k: k for k in range(len(kept))},
        compiler_params=params(),
        cost_estimate=cost(lag),
        name=name,
    )(ids, *args, *unread)


def group(pieces, unit):
    blocks, filled = [], unit
    for number, piece in enumerate(pieces):
        if filled == unit:
            blocks.append([])
            filled = 0
        blocks[-1].append((number, filled))
        filled += piece.shape[0]
    return blocks


def norm_kernel(ids, pieces, vectors, unit, start, total, kept=(), after=(), lag=0.05):
    width = pieces[0].shape[1]
    blocks = group(pieces, unit)

    def kernel(ids_ref, *refs):
        vec = refs[len(pieces)]
        first_ref, second_ref = refs[len(pieces) + 1 :]
        for step, block in enumerate(blocks):

            @pl.when(pl.program_id(0) == step)
            def _(block=block):
                for number, row in block:
                    rows = slice(row, row + pieces[number].shape[0])
                    data = refs[number][...].astype(F32)
                    centre = data - jnp.mean(data, axis=-1, keepdims=True)
                    spread = jnp.mean(centre * centre, axis=-1, keepdims=True)
                    scaled = centre * lax.rsqrt(spread + EPSILON)
                    first_ref[rows, :] = (scaled * vec[0:1, :] + vec[1:2, :]).astype(BF16)
                    second_ref[rows, :] = (scaled * vec[2:3, :] + vec[3:4, :]).astype(BF16)

    out = pl.BlockSpec((unit, width), lambda i, ids: (start + i, 0))
    shape = jax.ShapeDtypeStruct((total * unit, width), BF16)
    return call(
        kernel,
        ids,
        (len(blocks),),
        [pl.BlockSpec(array.shape, lambda i, ids: (0, 0)) for array in (*pieces, vectors)],
        [out, out],
        [shape, shape],
        (*pieces, vectors),
        kept=kept,
        after=after,
        lag=lag,
        name="norm",
    )


def rotate(block, cos, sin_low, sin_high, sign):
    lead = block[:, :128]
    turned = (
        lead * cos
        + sign * (pltpu.roll(lead, 96, 1) * sin_low + pltpu.roll(lead, 32, 1) * sin_high)
    )
    return jnp.concatenate([turned, block[:, 128:]], axis=1)


def mixed_kernel(ids, first, weight, bias, tables, start, count, blocks, kept=(), after=(), lag=0.05):
    rows, depth = first.shape
    heads = weight.shape[1] // (3 * HEAD_DIM)
    unit = rows // blocks
    wide = 3 * HEAD_DIM

    def kernel(ids_ref, a_ref, w_ref, b_ref, cos, low, high, out_ref):
        for part in range(3):
            here = slice(part * HEAD_DIM, (part + 1) * HEAD_DIM)
            value = product(a_ref[...], w_ref[:, here], "NN") + b_ref[:, here]
            if part < 2:
                value = rotate(value, cos[...], low[...], high[...], 1.0)
            out_ref[:, here] = value.astype(BF16)

    table = pl.BlockSpec((unit, 128), lambda j, i, ids: (ids[0] ^ (start + i), 0))
    return call(
        kernel,
        ids,
        (heads, count),
        [
            pl.BlockSpec((unit, depth), lambda j, i, ids: (start + i, 0)),
            pl.BlockSpec((depth, wide), lambda j, i, ids: (0, j)),
            pl.BlockSpec((1, wide), lambda j, i, ids: (0, j)),
            table,
            table,
            table,
        ],
        [pl.BlockSpec((unit, wide), lambda j, i, ids: (start + i, j))],
        [jax.ShapeDtypeStruct((rows, heads * wide), BF16)],
        (first, weight, bias, *tables),
        kept=kept,
        after=after,
        lag=lag,
        name="mixed",
    )


def attend_kernel(ids, mixed, blocks, after=(), lag=0.05):
    rows, width = mixed.shape
    heads = width // (3 * HEAD_DIM)
    unit = rows // blocks
    scale = HEAD_DIM ** (-0.5)

    def kernel(ids_ref, x_ref, ctx_ref, lse_ref, top_s, total_s, acc_s):
        block = pl.program_id(0)
        me = ids_ref[0]
        here = pl.ds(pl.multiple_of((me ^ block) * unit, unit), unit)

        def step(other, diagonal):
            there = pl.ds(pl.multiple_of((me ^ other) * unit, unit), unit)
            for head in range(heads):
                at = 3 * HEAD_DIM * head
                scores = (
                    product(
                        x_ref[here, at : at + HEAD_DIM],
                        x_ref[there, at + HEAD_DIM : at + 2 * HEAD_DIM],
                        "NT",
                    )
                    * scale
                )
                value = x_ref[there, at + 2 * HEAD_DIM : at + 3 * HEAD_DIM]
                if diagonal:
                    row_at = lax.broadcasted_iota(jnp.int32, scores.shape, 0)
                    col_at = lax.broadcasted_iota(jnp.int32, scores.shape, 1)
                    scores = jnp.where(col_at <= row_at, scores, BIG)
                    top = jnp.max(scores, axis=1, keepdims=True)
                    weight = jnp.exp(scores - top)
                    top_s[head] = top
                    total_s[head] = jnp.sum(weight, axis=1, keepdims=True)
                    acc_s[head] = product(weight.astype(BF16), value, "NN")
                else:
                    before = top_s[head]
                    top = jnp.maximum(before, jnp.max(scores, axis=1, keepdims=True))
                    weight = jnp.exp(scores - top)
                    shrunk = jnp.exp(before - top)
                    top_s[head] = top
                    total_s[head] = total_s[head] * shrunk + jnp.sum(weight, axis=1, keepdims=True)
                    acc_s[head] = acc_s[head] * shrunk + product(weight.astype(BF16), value, "NN")

        step(block, True)

        @pl.loop(0, block)
        def _(other):
            step(other, False)

        for head in range(heads):
            at = HEAD_DIM * head
            ctx_ref[:, at : at + HEAD_DIM] = (acc_s[head] / total_s[head]).astype(BF16)
            log_total = top_s[head] + jnp.log(total_s[head])
            lse_ref[head, 0] = jnp.transpose(jnp.broadcast_to(log_total, (unit, 128)))[:8]

    return call(
        kernel,
        ids,
        (blocks,),
        [pl.BlockSpec((rows, width), lambda b, ids: (0, 0))],
        [
            pl.BlockSpec((unit, heads * HEAD_DIM), lambda b, ids: (ids[0] ^ b, 0)),
            pl.BlockSpec((heads, 1, 8, unit), lambda b, ids: (0, b, 0, 0)),
        ],
        [
            jax.ShapeDtypeStruct((rows, heads * HEAD_DIM), BF16),
            jax.ShapeDtypeStruct((heads, blocks, 8, unit), F32),
        ],
        (mixed,),
        scratch=[
            pltpu.VMEM((heads, unit, 1), F32),
            pltpu.VMEM((heads, unit, 1), F32),
            pltpu.VMEM((heads, unit, HEAD_DIM), F32),
        ],
        after=after,
        lag=lag,
        name="attend",
    )


def attend_back_kernel(ids, mixed, grad, context, lse, tables, blocks, after=(), lag=0.05):
    rows, width = mixed.shape
    heads = width // (3 * HEAD_DIM)
    unit = rows // blocks
    scale = HEAD_DIM ** (-0.5)

    def kernel(ids_ref, x_ref, g_ref, c_ref, lse_ref, cos, low, high, out_ref, sum_ref, dk_s, dv_s, dq_s, inner_s):
        turn = pl.program_id(0)
        block = blocks - 1 - turn
        me = ids_ref[0]

        @pl.when(turn == 0)
        def _():
            dk_s[...] = jnp.zeros_like(dk_s)
            dv_s[...] = jnp.zeros_like(dv_s)
            sum_ref[...] = jnp.zeros_like(sum_ref)

        here = pl.ds(pl.multiple_of((me ^ block) * unit, unit), unit)
        for head in range(heads):
            cols = slice(HEAD_DIM * head, HEAD_DIM * (head + 1))
            inner = jnp.sum(g_ref[here, cols].astype(F32) * c_ref[here, cols].astype(F32), axis=1, keepdims=True)
            inner_s[head] = jnp.transpose(jnp.broadcast_to(inner, (unit, 128)))[:8]

        def step(other, diagonal):
            there = pl.ds(pl.multiple_of((me ^ other) * unit, unit), unit)
            for head in range(heads):
                at = 3 * HEAD_DIM * head
                query = x_ref[here, at : at + HEAD_DIM]
                seed = g_ref[here, HEAD_DIM * head : HEAD_DIM * (head + 1)]
                key = x_ref[there, at + HEAD_DIM : at + 2 * HEAD_DIM]
                value = x_ref[there, at + 2 * HEAD_DIM : at + 3 * HEAD_DIM]
                scores = product(key, query, "NT") * scale
                prob = jnp.exp(scores - lse_ref[head, 0][:1])
                if diagonal:
                    key_at = lax.broadcasted_iota(jnp.int32, scores.shape, 0)
                    row_at = lax.broadcasted_iota(jnp.int32, scores.shape, 1)
                    prob = jnp.where(key_at <= row_at, prob, 0.0)
                dprob = product(value, seed, "NT")
                dscore = (prob * (dprob - inner_s[head][:1])).astype(BF16)
                dv_s[head, other] += product(prob.astype(BF16), seed, "NN")
                dk_s[head, other] += product(dscore, query, "NN")
                dquery = product(dscore, key, "TN")
                if diagonal:
                    dq_s[head] = dquery
                else:
                    dq_s[head] += dquery

        step(block, True)

        @pl.loop(0, block)
        def _(other):
            step(other, False)

        for head in range(heads):
            at = 3 * HEAD_DIM * head
            dquery = rotate(dq_s[head] * scale, cos[...], low[...], high[...], -1.0)
            dkey = rotate(dk_s[head, block] * scale, cos[...], low[...], high[...], -1.0)
            for part, value in enumerate((dquery, dkey, dv_s[head, block])):
                cols = slice(at + part * HEAD_DIM, at + (part + 1) * HEAD_DIM)
                rounded = value.astype(BF16)
                out_ref[:, cols] = rounded
                sum_ref[:, cols] += jnp.sum(rounded.astype(F32), axis=0, keepdims=True)

    def whole(cols):
        return pl.BlockSpec((rows, cols), lambda b, ids: (0, 0))

    table = pl.BlockSpec((unit, 128), lambda b, ids: (blocks - 1 - b, 0))
    return call(
        kernel,
        ids,
        (blocks,),
        [
            whole(width),
            whole(heads * HEAD_DIM),
            whole(heads * HEAD_DIM),
            pl.BlockSpec((heads, 1, 8, unit), lambda b, ids: (0, blocks - 1 - b, 0, 0)),
            table,
            table,
            table,
        ],
        [
            pl.BlockSpec((unit, width), lambda b, ids: (ids[0] ^ (blocks - 1 - b), 0)),
            pl.BlockSpec((1, width), lambda b, ids: (0, 0)),
        ],
        [jax.ShapeDtypeStruct((rows, width), BF16), jax.ShapeDtypeStruct((1, width), F32)],
        (mixed, grad, context, lse, *tables),
        scratch=[
            pltpu.VMEM((heads, blocks, unit, HEAD_DIM), F32),
            pltpu.VMEM((heads, blocks, unit, HEAD_DIM), F32),
            pltpu.VMEM((heads, unit, HEAD_DIM), F32),
            pltpu.VMEM((heads, 8, unit), F32),
        ],
        after=after,
        lag=lag,
        name="attend_back",
    )


def expand_kernel(ids, second, weight, bias, after=(), lag=0.05):
    rows, depth = second.shape
    width = weight.shape[1]
    tall, wide = tile_of(rows, 1024), tile_of(width, 1024)
    unit = tile_of(wide, 512)

    def kernel(ids_ref, a_ref, w_ref, b_ref, hidden_ref, slope_ref):
        for part in range(wide // unit):
            here = slice(part * unit, (part + 1) * unit)
            pre = product(a_ref[...], w_ref[:, here], "NN") + b_ref[:, here]
            phi = 0.5 + 0.5 * lax.erf(pre * 0.7071067811865476)
            hidden_ref[:, here] = (pre * phi).astype(BF16)
            slope = phi + pre * (jnp.exp(-0.5 * pre * pre) * 0.3989422804014327)
            slope_ref[:, here] = slope.astype(BF16)

    out = pl.BlockSpec((tall, wide), lambda i, j, ids: (i, j))
    shape = jax.ShapeDtypeStruct((rows, width), BF16)
    return call(
        kernel,
        ids,
        (rows // tall, width // wide),
        [
            pl.BlockSpec((tall, depth), lambda i, j, ids: (i, 0)),
            pl.BlockSpec((depth, wide), lambda i, j, ids: (0, j)),
            pl.BlockSpec((1, wide), lambda i, j, ids: (0, j)),
        ],
        [out, out],
        [shape, shape],
        (second, weight, bias),
        after=after,
        lag=lag,
        name="expand",
    )


def stack_kernel(ids, pieces, unit, after=(), lag=0.05):
    width = pieces[0].shape[1]
    blocks = group(pieces, unit)

    def kernel(ids_ref, *refs):
        for step, block in enumerate(blocks):

            @pl.when(pl.program_id(0) == step)
            def _(block=block):
                for number, row in block:
                    refs[-1][row : row + pieces[number].shape[0], :] = refs[number][...]

    return call(
        kernel,
        ids,
        (len(blocks),),
        [pl.BlockSpec(piece.shape, lambda i, ids: (0, 0)) for piece in pieces],
        pl.BlockSpec((unit, width), lambda i, ids: (i, 0)),
        jax.ShapeDtypeStruct((len(blocks) * unit, width), BF16),
        tuple(pieces),
        after=after,
        lag=lag,
        name="stack",
    )


def join_kernel(ids, mine, other, bit, chunks, after=(), lag=0.05):
    rows, width = mine.shape[0] // chunks, mine.shape[1]

    def kernel(ids_ref, a_ref, b_ref, out_ref):
        for side, ref in ((0, a_ref), (1, b_ref)):

            @pl.when(pl.program_id(0) == side)
            def _(ref=ref):
                out_ref[...] = ref[...]

    return call(
        kernel,
        ids,
        (2, chunks),
        [
            pl.BlockSpec((rows, width), lambda s, i, ids: (jnp.where(s == 0, i, chunks - 1), 0)),
            pl.BlockSpec((rows, width), lambda s, i, ids: (jnp.where(s == 0, 0, i), 0)),
        ],
        pl.BlockSpec((rows, width), lambda s, i, ids: (2 * i + (s ^ ids[bit]), 0)),
        jax.ShapeDtypeStruct((2 * chunks * rows, width), BF16),
        (mine, other),
        after=after,
        lag=lag,
        name="join",
    )


def assemble_kernel(ids, parts, bit, chunks, after=(), lag=0.05):
    rows, width = parts[0].shape[0] // chunks, parts[0].shape[1]

    def kernel(ids_ref, *refs):
        for step, ref in enumerate(refs[:4]):

            @pl.when(pl.program_id(0) == step)
            def _(ref=ref):
                refs[4][...] = ref[...]

    def spec(step):
        def place(s, i, ids):
            return jnp.where(s == step, i, jnp.where(s < step, 0, chunks - 1)), 0

        return pl.BlockSpec((rows, width), place)

    return call(
        kernel,
        ids,
        (4, chunks),
        [spec(step) for step in range(4)],
        pl.BlockSpec((rows, width), lambda s, i, ids: (2 * i + ((s & 1) ^ ids[bit]), (s >> 1) ^ ids[1])),
        jax.ShapeDtypeStruct((2 * chunks * rows, 2 * width), BF16),
        tuple(parts),
        after=after,
        lag=lag,
        name="assemble",
    )


def shrink_back_kernel(ids, seed, weight, slope, after=(), lag=0.05):
    rows, depth = seed.shape
    width = weight.shape[1]
    tall, wide = tile_of(rows, 1024), tile_of(width, 1024)
    unit = tile_of(wide, 512)

    def kernel(ids_ref, a_ref, w_ref, s_ref, out_ref, sum_ref):
        @pl.when(pl.program_id(1) == 0)
        def _():
            sum_ref[...] = jnp.zeros_like(sum_ref)

        for part in range(wide // unit):
            here = slice(part * unit, (part + 1) * unit)
            grad = product(a_ref[...], w_ref[:, here], "NN") * s_ref[:, here].astype(F32)
            rounded = grad.astype(BF16)
            out_ref[:, here] = rounded
            sum_ref[:, here] += jnp.sum(rounded.astype(F32), axis=0, keepdims=True)

    tile = pl.BlockSpec((tall, wide), lambda j, i, ids: (i, j))
    return call(
        kernel,
        ids,
        (width // wide, rows // tall),
        [
            pl.BlockSpec((tall, depth), lambda j, i, ids: (i, 0)),
            pl.BlockSpec((depth, wide), lambda j, i, ids: (0, j)),
            tile,
        ],
        [tile, pl.BlockSpec((1, wide), lambda j, i, ids: (0, j))],
        [jax.ShapeDtypeStruct((rows, width), BF16), jax.ShapeDtypeStruct((1, width), F32)],
        (seed, weight, slope),
        after=after,
        lag=lag,
        name="shrink_back",
    )


def plain_kernel(ids, left, right, after=(), lag=0.05):
    rows, depth = left.shape
    width = right.shape[1]
    tall = tile_of(rows, 1024)

    def kernel(ids_ref, a_ref, b_ref, out_ref):
        out_ref[...] = product(a_ref[...], b_ref[...], "NN").astype(BF16)

    return call(
        kernel,
        ids,
        (rows // tall,),
        [
            pl.BlockSpec((tall, depth), lambda i, ids: (i, 0)),
            pl.BlockSpec(right.shape, lambda i, ids: (0, 0)),
        ],
        pl.BlockSpec((tall, width), lambda i, ids: (i, 0)),
        jax.ShapeDtypeStruct((rows, width), BF16),
        (left, right),
        after=after,
        lag=lag,
        name="plain",
    )


def branches_kernel(ids, context, merge, hidden, shrink, blocks, after=(), lag=0.05):
    rows, deep_b = hidden.shape
    depth, deep_a = merge.shape
    tall, wide = rows // blocks, tile_of(depth, 1024)
    unit = tile_of(wide, 512)

    def kernel(ids_ref, a_ref, m_ref, h_ref, s_ref, *out_refs):
        for block, out_ref in enumerate(out_refs):

            @pl.when(pl.program_id(1) == block)
            def _(out_ref=out_ref):
                for part in range(wide // unit):
                    here = slice(part * unit, (part + 1) * unit)
                    value = product(h_ref[...], s_ref[here, :], "NT")
                    value = value + product(a_ref[...], m_ref[here, :], "NT")
                    out_ref[:, here] = value.astype(BF16)

    return call(
        kernel,
        ids,
        (depth // wide, blocks),
        [
            pl.BlockSpec((tall, deep_a), lambda j, i, ids: (i, 0)),
            pl.BlockSpec((wide, deep_a), lambda j, i, ids: (j, 0)),
            pl.BlockSpec((tall, deep_b), lambda j, i, ids: (i, 0)),
            pl.BlockSpec((wide, deep_b), lambda j, i, ids: (j, 0)),
        ],
        [pl.BlockSpec((tall, wide), lambda j, i, ids: (0, j))] * blocks,
        [jax.ShapeDtypeStruct((tall, depth), BF16)] * blocks,
        (context, merge, hidden, shrink),
        after=after,
        lag=lag,
        name="branches",
    )


def back_kernel(ids, left_a, right_a, left_b, right_b, scales, start, count, blocks, after=(), lag=0.05):
    rows = left_a.shape[0] // blocks
    width = right_a.shape[0]
    deep_a, deep_b = left_a.shape[1], left_b.shape[1]
    wide = tile_of(width, 1024)
    unit = tile_of(wide, 512)

    def kernel(ids_ref, a_ref, b_ref, c_ref, d_ref, s_ref, *out_refs):
        for block, out_ref in enumerate(out_refs):

            @pl.when(pl.program_id(1) == block)
            def _(out_ref=out_ref):
                for part in range(wide // unit):
                    here = slice(part * unit, (part + 1) * unit)
                    one = product(a_ref[...], b_ref[here, :], "NT") * s_ref[0:1, here]
                    two = product(c_ref[...], d_ref[here, :], "NT") * s_ref[1:2, here]
                    out_ref[:, here] = (one + two).astype(BF16)

    return call(
        kernel,
        ids,
        (width // wide, count),
        [
            pl.BlockSpec((rows, deep_a), lambda j, i, ids: (start + i, 0)),
            pl.BlockSpec((wide, deep_a), lambda j, i, ids: (j, 0)),
            pl.BlockSpec((rows, deep_b), lambda j, i, ids: (start + i, 0)),
            pl.BlockSpec((wide, deep_b), lambda j, i, ids: (j, 0)),
            pl.BlockSpec((2, wide), lambda j, i, ids: (0, j)),
        ],
        [pl.BlockSpec((rows, wide), lambda j, i, ids: (0, j))] * count,
        [jax.ShapeDtypeStruct((rows, width), BF16)] * count,
        (left_a, right_a, left_b, right_b, scales),
        after=after,
        lag=lag,
        name="back",
    )


def full_grad_kernel(ids, left, right, weight=None, total=None, spare=0, after=(), lag=0.05):
    rows, depth = left.shape
    width = right.shape[1]
    tall, wide = tile_of(depth, 1024), tile_of(width, 1024)
    unit = tile_of(wide, 512)
    summed = weight is not None

    def kernel(ids_ref, a_ref, b_ref, *refs):
        out_ref = refs[2 if summed else 0]
        if summed:

            @pl.when(pl.program_id(1) == 0)
            def _():
                refs[3][...] = jnp.zeros_like(refs[3])
                refs[4][...] = jnp.zeros_like(refs[4])

        for part in range(wide // unit):
            here = slice(part * unit, (part + 1) * unit)
            value = product(a_ref[...], b_ref[:, here], "TN")
            out_ref[:, here] = value.astype(BF16)
            if summed:
                held = refs[0][:, here].astype(F32)
                one, two = held * value, held * refs[1][:, here]
                refs[3][...] += sum(one[:, lane : lane + 128] for lane in range(0, unit, 128))
                refs[4][...] += sum(two[:, lane : lane + 128] for lane in range(0, unit, 128))

    tile = pl.BlockSpec((tall, wide), lambda i, j, ids: (i, j))
    in_specs = [
        pl.BlockSpec((rows, tall), lambda i, j, ids: (0, i)),
        pl.BlockSpec((rows, wide), lambda i, j, ids: (0, j)),
    ]
    out_specs = [tile]
    out_shape = [jax.ShapeDtypeStruct((depth, width + spare), BF16)]
    args = (left, right)
    if summed:
        args += (weight, total)
        in_specs += [tile, pl.BlockSpec((1, wide), lambda i, j, ids: (0, j))]
        out_specs += [pl.BlockSpec((tall, 128), lambda i, j, ids: (i, 0))] * 2
        out_shape += [jax.ShapeDtypeStruct((depth, 128), F32)] * 2
    return call(
        kernel,
        ids,
        (depth // tall, width // wide),
        in_specs,
        out_specs,
        out_shape,
        args,
        after=after,
        lag=lag,
        name="full_grad",
    )


def spare_kernel(ids, kept, wide, narrow, after=(), lag=0.05):
    depth = kept.shape[0]

    def kernel(ids_ref, *refs):
        lane = lax.broadcasted_iota(jnp.int32, (depth, 128), 1)
        value = refs[len(wide)][...]
        for number, ref in enumerate(refs[: len(wide)]):
            value = jnp.where(lane == number, jnp.sum(ref[...], axis=1, keepdims=True), value)
        rounded = value.astype(BF16).astype(F32)
        rest = pltpu.roll(value - rounded, 64, 1)
        refs[-1][...] = jnp.where(lane < 64, rounded, rest).astype(BF16)

    block = pl.BlockSpec((depth, 128), lambda i, ids: (0, 0))
    return call(
        kernel,
        ids,
        (1,),
        [block] * (len(wide) + 1),
        [pl.BlockSpec((depth, 128), lambda i, ids: (0, kept.shape[1] // 128 - 1))],
        [jax.ShapeDtypeStruct(kept.shape, BF16)],
        (*wide, narrow),
        kept=(kept,),
        after=after,
        lag=lag,
        name="spare",
    )[0]


def output_kernel(ids, rows, parts, vectors, after=(), lag=0.05):
    count, width = rows.shape

    def kernel(ids_ref, x_ref, vec, *refs):
        total = refs[0][...].astype(F32)
        for ref in refs[1:-1]:
            total = total + ref[...].astype(F32)
        refs[-1][...] = (x_ref[...].astype(F32) + total + (vec[4:5, :] + vec[5:6, :])).astype(BF16)

    unit = tile_of(count, 256)
    tile = pl.BlockSpec((unit, width), lambda i, ids: (i, 0))
    return call(
        kernel,
        ids,
        (count // unit,),
        [tile, pl.BlockSpec(vectors.shape, lambda i, ids: (0, 0))] + [tile] * len(parts),
        tile,
        jax.ShapeDtypeStruct((count, width), BF16),
        (rows, vectors, *parts),
        after=after,
        lag=lag,
        name="output",
    )


def widen_kernel(ids, rows, spare=0, after=(), lag=0.05):
    count, width = rows.shape[0], rows.shape[1] - spare

    def kernel(ids_ref, *refs):
        half = len(refs) // 2
        for in_ref, out_ref in zip(refs[:half], refs[half:]):
            out_ref[...] = in_ref[...].astype(F32)

    specs = [pl.BlockSpec((count, width), lambda i, ids: (0, 0))]
    shapes = [jax.ShapeDtypeStruct((count, width), F32)]
    if spare:
        specs.append(pl.BlockSpec((count, spare), lambda i, ids: (0, width // spare)))
        shapes.append(jax.ShapeDtypeStruct((count, spare), F32))
    out_specs = [pl.BlockSpec(shape.shape, lambda i, ids: (0, 0)) for shape in shapes]
    return call(
        kernel,
        ids,
        (1,),
        specs,
        out_specs,
        shapes,
        (rows,) * len(specs),
        after=after,
        lag=lag,
        name="widen",
    )


def total_kernel(ids, parts, after=(), lag=0.05):
    rows, width = parts[0].shape

    def kernel(ids_ref, *refs):
        total = refs[0][...].astype(F32)
        for ref in refs[1:-1]:
            total = total + ref[...].astype(F32)
        refs[-1][...] = total

    unit = min(rows, 256)
    tile = pl.BlockSpec((unit, width), lambda i, ids: (i, 0))
    return call(
        kernel,
        ids,
        (rows // unit,),
        [tile] * len(parts),
        tile,
        jax.ShapeDtypeStruct((rows, width), F32),
        tuple(parts),
        after=after,
        lag=lag,
        name="total",
    )


def input_kernel(ids, rows, seed, parts, after=(), lag=0.05):
    count, width = rows.shape

    def kernel(ids_ref, x_ref, g_ref, *refs):
        back = refs[0][...].astype(F32)
        for ref in refs[1:-1]:
            back = back + ref[...].astype(F32)
        data = x_ref[...].astype(F32)
        centre = data - jnp.mean(data, axis=-1, keepdims=True)
        rstd = lax.rsqrt(jnp.mean(centre * centre, axis=-1, keepdims=True) + EPSILON)
        scaled = centre * rstd
        inner = jnp.mean(back * scaled, axis=-1, keepdims=True)
        back = back - jnp.mean(back, axis=-1, keepdims=True) - scaled * inner
        refs[-1][...] = g_ref[...].astype(F32) + rstd * back

    unit = tile_of(count, 256)
    tile = pl.BlockSpec((unit, width), lambda i, ids: (i, 0))
    return call(
        kernel,
        ids,
        (count // unit,),
        [tile] * (2 + len(parts)),
        tile,
        jax.ShapeDtypeStruct((count, width), F32),
        (rows, seed, *parts),
        after=after,
        lag=lag,
        name="input",
    )


def rotary_tables(length):
    position = jnp.arange(length, dtype=F32)[:, None]
    lane = jnp.arange(128)
    half = ROTARY // 2
    frequency = 10000.0 ** (-2.0 * (lane % half).astype(F32) / ROTARY)
    angles = position * frequency[None, :]
    sine = jnp.sin(angles)
    return (
        jnp.where(lane < ROTARY, jnp.cos(angles), 1.0),
        jnp.where(lane < half, -sine, 0.0),
        jnp.where((lane >= half) & (lane < ROTARY), sine, 0.0),
    )


def flip(value, axis, bit, size):
    return lax.ppermute(value, axis, [(i, i ^ bit) for i in range(size)])


def sum_over(value, axis, size):
    bit = 1
    while bit < size:
        value = value + flip(value, axis, bit, size)
        bit *= 2
    return value


def half_kernel(ids, rows, number, after=(), lag=0.05):
    count, width = rows.shape[0] // 2, rows.shape[1]

    def kernel(ids_ref, in_ref, out_ref):
        out_ref[...] = in_ref[...]

    return call(
        kernel,
        ids,
        (1,),
        [pl.BlockSpec((count, width), lambda i, ids: (number, 0))],
        pl.BlockSpec((count, width), lambda i, ids: (0, 0)),
        jax.ShapeDtypeStruct((count, width), BF16),
        (rows,),
        after=after,
        lag=lag,
        name="half",
    )


def gather_rows(ids, rows, size, after=()):
    if size != 4:
        return [rows] + [flip(rows, "tensor", k, size) for k in range(1, size)]
    one = flip(rows, "tensor", 1, size)
    two = flip(rows, "tensor", 2, size)
    upper = flip(half_kernel(ids, two, 0, after), "tensor", 1, size)
    lower = flip(half_kernel(ids, one, 1, after), "tensor", 2, size)
    return [rows, one, two, upper, lower]


def swap_core(value, size):
    return flip(value, "dp", 1, size)


class LineGather:
    def __init__(self, ids, shard, core, size):
        self.ids, self.size = ids, size
        depth, width = shard.shape
        halves = jnp.transpose(shard.reshape(depth, 2, width // 2), (1, 0, 2))
        self.mine = lax.dynamic_index_in_dim(halves, core, 0, keepdims=False)
        self.other = swap_core(lax.dynamic_index_in_dim(halves, 1 - core, 0, keepdims=False), size)
        self.bit, self.place, self.chunks = size // 4, 1, 1
        self.first = True

    def step(self, after=()):
        self.mine = join_kernel(self.ids, self.mine, self.other, self.place, self.chunks, after)
        self.chunks = 1 if self.first else 2 * self.chunks
        self.first = False
        self.place = 1 + self.bit.bit_length()
        self.other = flip(self.mine, "dp", 2 * self.bit, self.size)
        self.bit //= 2
        return self.mine

    def open(self):
        return self.bit >= 1

    def cross(self, after=()):
        self.other = stack_kernel(self.ids, [self.other], self.other.shape[0], after=after)
        self.across = [swap_core(value, self.size) for value in (self.mine, self.other)]
        return self.other

    def finish(self, after=()):
        return assemble_kernel(self.ids, (self.mine, self.other, *self.across), self.place, self.chunks, after)


def body(
    layer_input,
    cotangent,
    firstgain,
    firstbias,
    secondgain,
    secondbias,
    project,
    projbias,
    merging,
    mergebias,
    expand,
    expandbias,
    shrink,
    shrinkbias,
):
    n_dp, n_tensor = lax.axis_size("dp"), lax.axis_size("tensor")
    dp_at, tensor_at = lax.axis_index("dp"), lax.axis_index("tensor")
    chip, core = dp_at // 2, dp_at % 2
    bits = [(chip >> bit) & 1 for bit in range((n_dp // 2).bit_length() - 1)]
    ids = jnp.stack([tensor_at, core, *bits]).astype(jnp.int32)
    own_count, width = layer_input.shape
    group_count = own_count * n_tensor
    assert group_count == LENGTH
    depth = width // n_dp
    heads = project.shape[1]
    mixed_width = heads * 3 * HEAD_DIM
    hidden_width = expand.shape[1]

    packed = jnp.concatenate(
        [firstgain, firstbias, secondgain, secondbias, mergebias, shrinkbias, expandbias, projbias.reshape(-1)]
    )
    slots = jnp.where(jnp.arange(n_dp)[:, None] == dp_at, packed[None, :], jnp.zeros((), BF16))
    slots = sum_over(slots, "dp", n_dp).astype(F32)
    vectors = jnp.transpose(slots[:, : 6 * depth].reshape(n_dp, 6, depth), (1, 0, 2)).reshape(6, width)
    at = 6 * depth
    part = hidden_width // n_dp
    b_expand = slots[:, at : at + part].reshape(1, hidden_width)
    at += part
    b_project = jnp.transpose(slots[:, at:].reshape(n_dp, heads, -1), (1, 0, 2)).reshape(1, mixed_width)

    tables = rotary_tables(LENGTH)
    own_project = project.reshape(depth, mixed_width)
    w_project = lax.all_gather(own_project, "dp", axis=0, tiled=True)
    w_expand = lax.all_gather(expand, "dp", axis=0, tiled=True)
    shrink_line = LineGather(ids, jnp.transpose(shrink), core, n_dp)
    merge_line = LineGather(ids, jnp.transpose(merging), core, n_dp)
    last = shrink_line.step()
    last = merge_line.step((last,))

    unit = own_count
    rows_pieces = gather_rows(ids, layer_input, n_tensor, (vectors, last))
    near, far = (rows_pieces[:-1], rows_pieces[-1:]) if n_tensor != 4 else (rows_pieces[:3], rows_pieces[3:])
    pair = norm_kernel(ids, near, vectors, unit, 0, n_tensor)
    mixed = mixed_kernel(ids, pair[0], w_project, b_project, tables, 0, n_tensor - 1, n_tensor)
    later = stack_kernel(ids, [cotangent], unit, after=(mixed[0], *far))
    seed_pieces = [later] + [flip(later, "tensor", k, n_tensor) for k in range(n_tensor - 1, 0, -1)]
    last = later
    while shrink_line.open():
        last = shrink_line.step((last,))
    first, second = norm_kernel(ids, far, vectors, unit, n_tensor - 1, n_tensor, kept=pair, after=(last,))
    (mixed,) = mixed_kernel(ids, first, w_project, b_project, tables, n_tensor - 1, 1, n_tensor, kept=mixed)
    last = mixed
    while merge_line.open():
        last = merge_line.step((last,))
    context, lse = attend_kernel(ids, mixed, n_tensor, after=(last,), lag=12)
    last = merge_line.cross((context,))
    hidden, slope = expand_kernel(ids, second, w_expand, b_expand, after=(last,))
    last = shrink_line.cross((hidden,))
    seed = stack_kernel(ids, seed_pieces[:1] + seed_pieces[:0:-1], unit, after=(last,))
    w_merge = merge_line.finish((seed,))
    w_shrink = shrink_line.finish((w_merge,))
    (merge_part,) = full_grad_kernel(ids, context, seed, after=(w_shrink,))
    merging_grad = lax.psum_scatter(merge_part, "dp", scatter_dimension=1, tiled=True)
    (shrink_part,) = full_grad_kernel(ids, hidden, seed, after=(merge_part,))
    shrink_grad = lax.psum_scatter(shrink_part, "dp", scatter_dimension=1, tiled=True)
    cgrad = plain_kernel(ids, seed, w_merge, after=(shrink_part,))
    (merging_grad,) = widen_kernel(ids, merging_grad, after=(cgrad,))
    mgrad, mixed_sum = attend_back_kernel(
        ids, mixed, cgrad, context, lse, tables, n_tensor, after=(merging_grad,), lag=30
    )
    project_part, gain_one, bias_one = full_grad_kernel(ids, first, mgrad, w_project, mixed_sum)
    project_grad = lax.psum_scatter(project_part, "dp", scatter_dimension=0, tiled=True)
    branches = branches_kernel(ids, context, w_merge, hidden, w_shrink, n_tensor, after=(project_part,))
    summed = [branches[0]] + [flip(branches[k], "tensor", k, n_tensor) for k in range(n_tensor - 1, 0, -1)]
    pgrad, expand_sum = shrink_back_kernel(ids, seed, w_shrink, slope, after=(branches[0],))
    expand_part, gain_two, bias_two = full_grad_kernel(ids, second, pgrad, w_expand, expand_sum, spare=128)

    def slots(values):
        return jnp.pad(values, ((0, 0), (0, depth - values.shape[1]))).reshape(width)

    narrow = [
        jnp.sum(cotangent.astype(F32), axis=0),
        slots(expand_sum.reshape(n_dp, -1)),
        slots(jnp.transpose(mixed_sum.reshape(heads, n_dp, -1), (1, 0, 2)).reshape(n_dp, -1)),
    ]
    narrow = jnp.pad(jnp.stack(narrow, axis=1), ((0, 0), (4, 128 - 4 - len(narrow))))
    expand_part = spare_kernel(ids, expand_part, [gain_one, bias_one, gain_two, bias_two], narrow)
    expand_grad = lax.psum_scatter(expand_part, "dp", scatter_dimension=0, tiled=True)
    (shrink_grad,) = widen_kernel(ids, shrink_grad, after=(expand_part,))
    gains = jnp.stack([vectors[0], vectors[2]])
    step = n_tensor // 2
    made = back_kernel(ids, mgrad, w_project, pgrad, w_expand, gains, step, step, n_tensor, after=(shrink_grad,))
    back_far = [flip(made[k], "tensor", step + k, n_tensor) for k in range(step - 1, -1, -1)]
    made = back_kernel(ids, mgrad, w_project, pgrad, w_expand, gains, 0, step, n_tensor, after=(made[0],))
    back = [made[0]] + [flip(made[k], "tensor", k, n_tensor) for k in range(step - 1, 0, -1)]
    layer_output = output_kernel(ids, layer_input, summed, vectors, after=(made[0],), lag=10)
    (project_grad,) = widen_kernel(ids, project_grad, after=(layer_output,))
    back_far = total_kernel(ids, back_far, after=(project_grad,), lag=4)
    input_grad = input_kernel(ids, layer_input, cotangent, back + [back_far], lag=160)

    expand_grad, sums = widen_kernel(ids, expand_grad, spare=128)
    sums = jnp.transpose(sums[:, :7] + sums[:, 64:71])
    norms = sums[:5]
    norms = norms + sum(flip(norms, "tensor", k, n_tensor) for k in range(1, n_tensor))
    gain_one, bias_one, gain_two, bias_two, seed_sum = norms
    gain_one = (gain_one - firstbias.astype(F32) * bias_one) / firstgain.astype(F32)
    gain_two = (gain_two - secondbias.astype(F32) * bias_two) / secondgain.astype(F32)
    expandbias_grad = sums[5, : expandbias.shape[0]]
    projbias_grad = sums[6, : projbias.size].reshape(projbias.shape)
    return (
        layer_output,
        input_grad,
        gain_one,
        bias_one,
        gain_two,
        bias_two,
        project_grad.reshape(project.shape),
        projbias_grad,
        merging_grad,
        seed_sum,
        expand_grad,
        expandbias_grad,
        shrink_grad,
        seed_sum,
    )


def solution(mesh):
    specs = (
        P(("dp", "tensor"), None),
        P(("dp", "tensor"), None),
        P("dp"),
        P("dp"),
        P("dp"),
        P("dp"),
        P("dp", "tensor", None),
        P("tensor", "dp"),
        P("tensor", "dp"),
        P("dp"),
        P("dp", "tensor"),
        P(("tensor", "dp")),
        P("tensor", "dp"),
        P("dp"),
    )
    return jax.shard_map(body, mesh=mesh, in_specs=specs, out_specs=specs, check_vma=False)
```

```python
import jax
import jax.numpy as jnp
from jax import lax
from jax.experimental import pallas as pl
from jax.experimental.pallas import tpu as pltpu
from jax.sharding import PartitionSpec as P

HEAD_DIM = 256
ROTARY = 64
LENGTH = 2048
EPSILON = 1e-05
BIG = -1e30
F32 = jnp.float32
BF16 = jnp.bfloat16
DIMS = {
    "NN": (((1,), (0,)), ((), ())),
    "NT": (((1,), (1,)), ((), ())),
    "TN": (((0,), (0,)), ((), ())),
}


def product(left, right, mode):
    return lax.dot_general(left, right, DIMS[mode], preferred_element_type=F32)


def params():
    return pltpu.CompilerParams(vmem_limit_bytes=56 << 20)


def cost(lag):
    return pl.CostEstimate(flops=int(lag * 1e9), bytes_accessed=0, transcendentals=0)


def tile_of(width, most):
    best = 128
    for size in range(128, most + 1, 128):
        if width % size == 0:
            best = size
    return best


def call(kernel, ids, grid, in_specs, out_specs, out_shape, args, name, scratch=(), after=(), kept=(), lag=0.05):
    count = len(args)
    unread = tuple(kept) + tuple(after)

    def run(ids_ref, *refs):
        kernel(ids_ref, *refs[:count], *refs[count + len(unread) :])

    return pl.pallas_call(
        run,
        grid_spec=pltpu.PrefetchScalarGridSpec(
            num_scalar_prefetch=1,
            grid=grid,
            in_specs=list(in_specs) + [pl.BlockSpec(memory_space=pl.ANY)] * len(unread),
            out_specs=out_specs,
            scratch_shapes=list(scratch),
        ),
        out_shape=out_shape,
        input_output_aliases={1 + count + k: k for k in range(len(kept))},
        compiler_params=params(),
        cost_estimate=cost(lag),
        name=name,
    )(ids, *args, *unread)


def group(pieces, unit):
    blocks, filled = [], unit
    for number, piece in enumerate(pieces):
        if filled == unit:
            blocks.append([])
            filled = 0
        blocks[-1].append((number, filled))
        filled += piece.shape[0]
    return blocks


def norm_kernel(ids, pieces, vectors, unit, start, total, kept=(), after=(), lag=0.05):
    width = pieces[0].shape[1]
    blocks = group(pieces, unit)

    def kernel(ids_ref, *refs):
        vec = refs[len(pieces)]
        first_ref, second_ref = refs[len(pieces) + 1 :]
        for step, block in enumerate(blocks):

            @pl.when(pl.program_id(0) == step)
            def _(block=block):
                for number, row in block:
                    rows = slice(row, row + pieces[number].shape[0])
                    data = refs[number][...].astype(F32)
                    centre = data - jnp.mean(data, axis=-1, keepdims=True)
                    spread = jnp.mean(centre * centre, axis=-1, keepdims=True)
                    scaled = centre * lax.rsqrt(spread + EPSILON)
                    first_ref[rows, :] = (scaled * vec[0:1, :] + vec[1:2, :]).astype(BF16)
                    second_ref[rows, :] = (scaled * vec[2:3, :] + vec[3:4, :]).astype(BF16)

    out = pl.BlockSpec((unit, width), lambda i, ids: (start + i, 0))
    shape = jax.ShapeDtypeStruct((total * unit, width), BF16)
    return call(
        kernel,
        ids,
        (len(blocks),),
        [pl.BlockSpec(array.shape, lambda i, ids: (0, 0)) for array in (*pieces, vectors)],
        [out, out],
        [shape, shape],
        (*pieces, vectors),
        kept=kept,
        after=after,
        lag=lag,
        name="norm",
    )


def rotate(block, cos, sin_low, sin_high, sign):
    lead = block[:, :128]
    turned = (
        lead * cos
        + sign * (pltpu.roll(lead, 96, 1) * sin_low + pltpu.roll(lead, 32, 1) * sin_high)
    )
    return jnp.concatenate([turned, block[:, 128:]], axis=1)


def mixed_kernel(ids, first, weight, bias, tables, start, count, blocks, kept=(), after=(), lag=0.05):
    rows, depth = first.shape
    heads = weight.shape[1] // (3 * HEAD_DIM)
    unit = rows // blocks
    wide = 3 * HEAD_DIM

    def kernel(ids_ref, a_ref, w_ref, b_ref, cos, low, high, out_ref):
        for part in range(3):
            here = slice(part * HEAD_DIM, (part + 1) * HEAD_DIM)
            value = product(a_ref[...], w_ref[:, here], "NN") + b_ref[:, here]
            if part < 2:
                value = rotate(value, cos[...], low[...], high[...], 1.0)
            out_ref[:, here] = value.astype(BF16)

    table = pl.BlockSpec((unit, 128), lambda j, i, ids: (ids[0] ^ (start + i), 0))
    return call(
        kernel,
        ids,
        (heads, count),
        [
            pl.BlockSpec((unit, depth), lambda j, i, ids: (start + i, 0)),
            pl.BlockSpec((depth, wide), lambda j, i, ids: (0, j)),
            pl.BlockSpec((1, wide), lambda j, i, ids: (0, j)),
            table,
            table,
            table,
        ],
        [pl.BlockSpec((unit, wide), lambda j, i, ids: (start + i, j))],
        [jax.ShapeDtypeStruct((rows, heads * wide), BF16)],
        (first, weight, bias, *tables),
        kept=kept,
        after=after,
        lag=lag,
        name="mixed",
    )


def attend_kernel(ids, mixed, blocks, after=(), lag=0.05):
    rows, width = mixed.shape
    heads = width // (3 * HEAD_DIM)
    unit = rows // blocks
    scale = HEAD_DIM ** (-0.5)

    def kernel(ids_ref, x_ref, ctx_ref, lse_ref, top_s, total_s, acc_s):
        block = pl.program_id(0)
        me = ids_ref[0]
        here = pl.ds(pl.multiple_of((me ^ block) * unit, unit), unit)

        def step(other, diagonal):
            there = pl.ds(pl.multiple_of((me ^ other) * unit, unit), unit)
            for head in range(heads):
                at = 3 * HEAD_DIM * head
                scores = (
                    product(
                        x_ref[here, at : at + HEAD_DIM],
                        x_ref[there, at + HEAD_DIM : at + 2 * HEAD_DIM],
                        "NT",
                    )
                    * scale
                )
                value = x_ref[there, at + 2 * HEAD_DIM : at + 3 * HEAD_DIM]
                if diagonal:
                    row_at = lax.broadcasted_iota(jnp.int32, scores.shape, 0)
                    col_at = lax.broadcasted_iota(jnp.int32, scores.shape, 1)
                    scores = jnp.where(col_at <= row_at, scores, BIG)
                    top = jnp.max(scores, axis=1, keepdims=True)
                    weight = jnp.exp(scores - top)
                    top_s[head] = top
                    total_s[head] = jnp.sum(weight, axis=1, keepdims=True)
                    acc_s[head] = product(weight.astype(BF16), value, "NN")
                else:
                    before = top_s[head]
                    top = jnp.maximum(before, jnp.max(scores, axis=1, keepdims=True))
                    weight = jnp.exp(scores - top)
                    shrunk = jnp.exp(before - top)
                    top_s[head] = top
                    total_s[head] = total_s[head] * shrunk + jnp.sum(weight, axis=1, keepdims=True)
                    acc_s[head] = acc_s[head] * shrunk + product(weight.astype(BF16), value, "NN")

        step(block, True)

        @pl.loop(0, block)
        def _(other):
            step(other, False)

        for head in range(heads):
            at = HEAD_DIM * head
            ctx_ref[:, at : at + HEAD_DIM] = (acc_s[head] / total_s[head]).astype(BF16)
            log_total = top_s[head] + jnp.log(total_s[head])
            lse_ref[head, 0] = jnp.transpose(jnp.broadcast_to(log_total, (unit, 128)))[:8]

    return call(
        kernel,
        ids,
        (blocks,),
        [pl.BlockSpec((rows, width), lambda b, ids: (0, 0))],
        [
            pl.BlockSpec((unit, heads * HEAD_DIM), lambda b, ids: (ids[0] ^ b, 0)),
            pl.BlockSpec((heads, 1, 8, unit), lambda b, ids: (0, b, 0, 0)),
        ],
        [
            jax.ShapeDtypeStruct((rows, heads * HEAD_DIM), BF16),
            jax.ShapeDtypeStruct((heads, blocks, 8, unit), F32),
        ],
        (mixed,),
        scratch=[
            pltpu.VMEM((heads, unit, 1), F32),
            pltpu.VMEM((heads, unit, 1), F32),
            pltpu.VMEM((heads, unit, HEAD_DIM), F32),
        ],
        after=after,
        lag=lag,
        name="attend",
    )


def attend_back_kernel(ids, mixed, grad, context, lse, tables, blocks, after=(), lag=0.05):
    rows, width = mixed.shape
    heads = width // (3 * HEAD_DIM)
    unit = rows // blocks
    scale = HEAD_DIM ** (-0.5)

    def kernel(ids_ref, x_ref, g_ref, c_ref, lse_ref, cos, low, high, out_ref, sum_ref, dk_s, dv_s, dq_s, inner_s):
        turn = pl.program_id(0)
        block = blocks - 1 - turn
        me = ids_ref[0]

        @pl.when(turn == 0)
        def _():
            dk_s[...] = jnp.zeros_like(dk_s)
            dv_s[...] = jnp.zeros_like(dv_s)
            sum_ref[...] = jnp.zeros_like(sum_ref)

        here = pl.ds(pl.multiple_of((me ^ block) * unit, unit), unit)
        for head in range(heads):
            cols = slice(HEAD_DIM * head, HEAD_DIM * (head + 1))
            inner = jnp.sum(g_ref[here, cols].astype(F32) * c_ref[here, cols].astype(F32), axis=1, keepdims=True)
            inner_s[head] = jnp.transpose(jnp.broadcast_to(inner, (unit, 128)))[:8]

        def step(other, diagonal):
            there = pl.ds(pl.multiple_of((me ^ other) * unit, unit), unit)
            for head in range(heads):
                at = 3 * HEAD_DIM * head
                query = x_ref[here, at : at + HEAD_DIM]
                seed = g_ref[here, HEAD_DIM * head : HEAD_DIM * (head + 1)]
                key = x_ref[there, at + HEAD_DIM : at + 2 * HEAD_DIM]
                value = x_ref[there, at + 2 * HEAD_DIM : at + 3 * HEAD_DIM]
                scores = product(key, query, "NT") * scale
                prob = jnp.exp(scores - lse_ref[head, 0][:1])
                if diagonal:
                    key_at = lax.broadcasted_iota(jnp.int32, scores.shape, 0)
                    row_at = lax.broadcasted_iota(jnp.int32, scores.shape, 1)
                    prob = jnp.where(key_at <= row_at, prob, 0.0)
                dprob = product(value, seed, "NT")
                dscore = (prob * (dprob - inner_s[head][:1])).astype(BF16)
                dv_s[head, other] += product(prob.astype(BF16), seed, "NN")
                dk_s[head, other] += product(dscore, query, "NN")
                dquery = product(dscore, key, "TN")
                if diagonal:
                    dq_s[head] = dquery
                else:
                    dq_s[head] += dquery

        step(block, True)

        @pl.loop(0, block)
        def _(other):
            step(other, False)

        for head in range(heads):
            at = 3 * HEAD_DIM * head
            dquery = rotate(dq_s[head] * scale, cos[...], low[...], high[...], -1.0)
            dkey = rotate(dk_s[head, block] * scale, cos[...], low[...], high[...], -1.0)
            for part, value in enumerate((dquery, dkey, dv_s[head, block])):
                cols = slice(at + part * HEAD_DIM, at + (part + 1) * HEAD_DIM)
                rounded = value.astype(BF16)
                out_ref[:, cols] = rounded
                sum_ref[:, cols] += jnp.sum(rounded.astype(F32), axis=0, keepdims=True)

    def whole(cols):
        return pl.BlockSpec((rows, cols), lambda b, ids: (0, 0))

    table = pl.BlockSpec((unit, 128), lambda b, ids: (blocks - 1 - b, 0))
    return call(
        kernel,
        ids,
        (blocks,),
        [
            whole(width),
            whole(heads * HEAD_DIM),
            whole(heads * HEAD_DIM),
            pl.BlockSpec((heads, 1, 8, unit), lambda b, ids: (0, blocks - 1 - b, 0, 0)),
            table,
            table,
            table,
        ],
        [
            pl.BlockSpec((unit, width), lambda b, ids: (ids[0] ^ (blocks - 1 - b), 0)),
            pl.BlockSpec((1, width), lambda b, ids: (0, 0)),
        ],
        [jax.ShapeDtypeStruct((rows, width), BF16), jax.ShapeDtypeStruct((1, width), F32)],
        (mixed, grad, context, lse, *tables),
        scratch=[
            pltpu.VMEM((heads, blocks, unit, HEAD_DIM), F32),
            pltpu.VMEM((heads, blocks, unit, HEAD_DIM), F32),
            pltpu.VMEM((heads, unit, HEAD_DIM), F32),
            pltpu.VMEM((heads, 8, unit), F32),
        ],
        after=after,
        lag=lag,
        name="attend_back",
    )


def expand_kernel(ids, second, weight, bias, after=(), lag=0.05):
    rows, depth = second.shape
    width = weight.shape[1]
    tall, wide = tile_of(rows, 1024), tile_of(width, 1024)
    unit = tile_of(wide, 512)

    def kernel(ids_ref, a_ref, w_ref, b_ref, hidden_ref, slope_ref):
        for part in range(wide // unit):
            here = slice(part * unit, (part + 1) * unit)
            pre = product(a_ref[...], w_ref[:, here], "NN") + b_ref[:, here]
            phi = 0.5 + 0.5 * lax.erf(pre * 0.7071067811865476)
            hidden_ref[:, here] = (pre * phi).astype(BF16)
            slope = phi + pre * (jnp.exp(-0.5 * pre * pre) * 0.3989422804014327)
            slope_ref[:, here] = slope.astype(BF16)

    out = pl.BlockSpec((tall, wide), lambda i, j, ids: (i, j))
    shape = jax.ShapeDtypeStruct((rows, width), BF16)
    return call(
        kernel,
        ids,
        (rows // tall, width // wide),
        [
            pl.BlockSpec((tall, depth), lambda i, j, ids: (i, 0)),
            pl.BlockSpec((depth, wide), lambda i, j, ids: (0, j)),
            pl.BlockSpec((1, wide), lambda i, j, ids: (0, j)),
        ],
        [out, out],
        [shape, shape],
        (second, weight, bias),
        after=after,
        lag=lag,
        name="expand",
    )


def stack_kernel(ids, pieces, unit, after=(), lag=0.05):
    width = pieces[0].shape[1]
    blocks = group(pieces, unit)

    def kernel(ids_ref, *refs):
        for step, block in enumerate(blocks):

            @pl.when(pl.program_id(0) == step)
            def _(block=block):
                for number, row in block:
                    refs[-1][row : row + pieces[number].shape[0], :] = refs[number][...]

    return call(
        kernel,
        ids,
        (len(blocks),),
        [pl.BlockSpec(piece.shape, lambda i, ids: (0, 0)) for piece in pieces],
        pl.BlockSpec((unit, width), lambda i, ids: (i, 0)),
        jax.ShapeDtypeStruct((len(blocks) * unit, width), BF16),
        tuple(pieces),
        after=after,
        lag=lag,
        name="stack",
    )


def join_kernel(ids, mine, other, bit, chunks, after=(), lag=0.05):
    rows, width = mine.shape[0] // chunks, mine.shape[1]

    def kernel(ids_ref, a_ref, b_ref, out_ref):
        for side, ref in ((0, a_ref), (1, b_ref)):

            @pl.when(pl.program_id(0) == side)
            def _(ref=ref):
                out_ref[...] = ref[...]

    return call(
        kernel,
        ids,
        (2, chunks),
        [
            pl.BlockSpec((rows, width), lambda s, i, ids: (jnp.where(s == 0, i, chunks - 1), 0)),
            pl.BlockSpec((rows, width), lambda s, i, ids: (jnp.where(s == 0, 0, i), 0)),
        ],
        pl.BlockSpec((rows, width), lambda s, i, ids: (2 * i + (s ^ ids[bit]), 0)),
        jax.ShapeDtypeStruct((2 * chunks * rows, width), BF16),
        (mine, other),
        after=after,
        lag=lag,
        name="join",
    )


def assemble_kernel(ids, parts, bit, chunks, after=(), lag=0.05):
    rows, width = parts[0].shape[0] // chunks, parts[0].shape[1]

    def kernel(ids_ref, *refs):
        for step, ref in enumerate(refs[:4]):

            @pl.when(pl.program_id(0) == step)
            def _(ref=ref):
                refs[4][...] = ref[...].reshape(chunks, 1, rows, width)

    whole = pl.BlockSpec((chunks * rows, width), lambda s, ids: (0, 0))
    made = call(
        kernel,
        ids,
        (4,),
        [whole] * 4,
        pl.BlockSpec((chunks, 1, rows, width), lambda s, ids: (0, (s & 1) ^ ids[bit], 0, (s >> 1) ^ ids[1])),
        jax.ShapeDtypeStruct((chunks, 2, rows, 2 * width), BF16),
        tuple(parts),
        after=after,
        lag=lag,
        name="assemble",
    )
    return made.reshape(2 * chunks * rows, 2 * width)


def shrink_back_kernel(ids, seed, weight, slope, after=(), lag=0.05):
    rows, depth = seed.shape
    width = weight.shape[0]
    tall, wide = tile_of(rows, 1024), tile_of(width, 1024)
    unit = tile_of(wide, 512)

    def kernel(ids_ref, a_ref, w_ref, s_ref, out_ref, sum_ref):
        @pl.when(pl.program_id(1) == 0)
        def _():
            sum_ref[...] = jnp.zeros_like(sum_ref)

        for part in range(wide // unit):
            here = slice(part * unit, (part + 1) * unit)
            grad = product(a_ref[...], w_ref[here, :], "NT") * s_ref[:, here].astype(F32)
            rounded = grad.astype(BF16)
            out_ref[:, here] = rounded
            sum_ref[:, here] += jnp.sum(rounded.astype(F32), axis=0, keepdims=True)

    tile = pl.BlockSpec((tall, wide), lambda j, i, ids: (i, j))
    return call(
        kernel,
        ids,
        (width // wide, rows // tall),
        [
            pl.BlockSpec((tall, depth), lambda j, i, ids: (i, 0)),
            pl.BlockSpec((wide, depth), lambda j, i, ids: (j, 0)),
            tile,
        ],
        [tile, pl.BlockSpec((1, wide), lambda j, i, ids: (0, j))],
        [jax.ShapeDtypeStruct((rows, width), BF16), jax.ShapeDtypeStruct((1, width), F32)],
        (seed, weight, slope),
        after=after,
        lag=lag,
        name="shrink_back",
    )


def plain_kernel(ids, left, right, after=(), lag=0.05):
    rows, depth = left.shape
    width = right.shape[1]
    tall = tile_of(rows, 1024)

    def kernel(ids_ref, a_ref, b_ref, out_ref):
        out_ref[...] = product(a_ref[...], b_ref[...], "NN").astype(BF16)

    return call(
        kernel,
        ids,
        (rows // tall,),
        [
            pl.BlockSpec((tall, depth), lambda i, ids: (i, 0)),
            pl.BlockSpec(right.shape, lambda i, ids: (0, 0)),
        ],
        pl.BlockSpec((tall, width), lambda i, ids: (i, 0)),
        jax.ShapeDtypeStruct((rows, width), BF16),
        (left, right),
        after=after,
        lag=lag,
        name="plain",
    )


def branches_kernel(ids, context, merge, hidden, shrink, blocks, after=(), lag=0.05):
    rows, deep_b = hidden.shape
    depth, deep_a = merge.shape
    tall, wide = rows // blocks, tile_of(depth, 1024)
    unit = tile_of(wide, 512)

    def kernel(ids_ref, a_ref, m_ref, h_ref, s_ref, *out_refs):
        for block, out_ref in enumerate(out_refs):

            @pl.when(pl.program_id(1) == block)
            def _(out_ref=out_ref):
                for part in range(wide // unit):
                    here = slice(part * unit, (part + 1) * unit)
                    value = product(h_ref[...], s_ref[:, here], "NN")
                    value = value + product(a_ref[...], m_ref[here, :], "NT")
                    out_ref[:, here] = value.astype(BF16)

    return call(
        kernel,
        ids,
        (depth // wide, blocks),
        [
            pl.BlockSpec((tall, deep_a), lambda j, i, ids: (i, 0)),
            pl.BlockSpec((wide, deep_a), lambda j, i, ids: (j, 0)),
            pl.BlockSpec((tall, deep_b), lambda j, i, ids: (i, 0)),
            pl.BlockSpec((deep_b, wide), lambda j, i, ids: (0, j)),
        ],
        [pl.BlockSpec((tall, wide), lambda j, i, ids: (0, j))] * blocks,
        [jax.ShapeDtypeStruct((tall, depth), BF16)] * blocks,
        (context, merge, hidden, shrink),
        after=after,
        lag=lag,
        name="branches",
    )


def back_kernel(ids, left_a, right_a, left_b, right_b, scales, start, count, blocks, after=(), lag=0.05):
    rows = left_a.shape[0] // blocks
    width = right_a.shape[0]
    deep_a, deep_b = left_a.shape[1], left_b.shape[1]
    wide = tile_of(width, 1024)
    unit = tile_of(wide, 512)

    def kernel(ids_ref, a_ref, b_ref, c_ref, d_ref, s_ref, *out_refs):
        for block, out_ref in enumerate(out_refs):

            @pl.when(pl.program_id(1) == block)
            def _(out_ref=out_ref):
                for part in range(wide // unit):
                    here = slice(part * unit, (part + 1) * unit)
                    one = product(a_ref[...], b_ref[here, :], "NT") * s_ref[0:1, here]
                    two = product(c_ref[...], d_ref[here, :], "NT") * s_ref[1:2, here]
                    out_ref[:, here] = (one + two).astype(BF16)

    return call(
        kernel,
        ids,
        (width // wide, count),
        [
            pl.BlockSpec((rows, deep_a), lambda j, i, ids: (start + i, 0)),
            pl.BlockSpec((wide, deep_a), lambda j, i, ids: (j, 0)),
            pl.BlockSpec((rows, deep_b), lambda j, i, ids: (start + i, 0)),
            pl.BlockSpec((wide, deep_b), lambda j, i, ids: (j, 0)),
            pl.BlockSpec((2, wide), lambda j, i, ids: (0, j)),
        ],
        [pl.BlockSpec((rows, wide), lambda j, i, ids: (0, j))] * count,
        [jax.ShapeDtypeStruct((rows, width), BF16)] * count,
        (left_a, right_a, left_b, right_b, scales),
        after=after,
        lag=lag,
        name="back",
    )


def full_grad_kernel(ids, left, right, weight=None, total=None, spare=0, start=0, count=0, kept=(), after=(), lag=0.05):
    rows, depth = left.shape
    width = right.shape[1]
    tall, wide = tile_of(depth, 1024), tile_of(width, 1024)
    unit = tile_of(wide, 512)
    summed = weight is not None

    def kernel(ids_ref, a_ref, b_ref, *refs):
        out_ref = refs[2 if summed else 0]
        if summed:

            @pl.when(pl.program_id(1) == 0)
            def _():
                refs[3][...] = jnp.zeros_like(refs[3])
                refs[4][...] = jnp.zeros_like(refs[4])

        for part in range(wide // unit):
            here = slice(part * unit, (part + 1) * unit)
            value = product(a_ref[...], b_ref[:, here], "TN")
            out_ref[:, here] = value.astype(BF16)
            if summed:
                held = refs[0][:, here].astype(F32)
                one, two = held * value, held * refs[1][:, here]
                refs[3][...] += sum(one[:, lane : lane + 128] for lane in range(0, unit, 128))
                refs[4][...] += sum(two[:, lane : lane + 128] for lane in range(0, unit, 128))

    tile = pl.BlockSpec((tall, wide), lambda i, j, ids: (i, j))
    in_specs = [
        pl.BlockSpec((rows, tall), lambda i, j, ids: (0, i)),
        pl.BlockSpec((rows, wide), lambda i, j, ids: (0, j)),
    ]
    out_specs = [pl.BlockSpec((tall, wide), lambda i, j, ids: (start // tall + i, j))]
    out_shape = [jax.ShapeDtypeStruct((count or depth, width + spare), BF16)]
    args = (left, right)
    if summed:
        args += (weight, total)
        in_specs += [tile, pl.BlockSpec((1, wide), lambda i, j, ids: (0, j))]
        out_specs += [pl.BlockSpec((tall, 128), lambda i, j, ids: (i, 0))] * 2
        out_shape += [jax.ShapeDtypeStruct((depth, 128), F32)] * 2
    return call(
        kernel,
        ids,
        (depth // tall, width // wide),
        in_specs,
        out_specs,
        out_shape,
        args,
        kept=kept,
        after=after,
        lag=lag,
        name="full_grad",
    )


def spare_kernel(ids, kept, wide, narrow, after=(), lag=0.05):
    depth = kept.shape[0]

    def kernel(ids_ref, *refs):
        lane = lax.broadcasted_iota(jnp.int32, (depth, 128), 1)
        value = refs[len(wide)][...]
        for number, ref in enumerate(refs[: len(wide)]):
            value = jnp.where(lane == number, jnp.sum(ref[...], axis=1, keepdims=True), value)
        rounded = value.astype(BF16).astype(F32)
        rest = pltpu.roll(value - rounded, 64, 1)
        refs[-1][...] = jnp.where(lane < 64, rounded, rest).astype(BF16)

    block = pl.BlockSpec((depth, 128), lambda i, ids: (0, 0))
    return call(
        kernel,
        ids,
        (1,),
        [block] * (len(wide) + 1),
        [pl.BlockSpec((depth, 128), lambda i, ids: (0, kept.shape[1] // 128 - 1))],
        [jax.ShapeDtypeStruct(kept.shape, BF16)],
        (*wide, narrow),
        kept=(kept,),
        after=after,
        lag=lag,
        name="spare",
    )[0]


def output_kernel(ids, rows, parts, vectors, after=(), lag=0.05):
    count, width = rows.shape

    def kernel(ids_ref, x_ref, vec, *refs):
        total = refs[0][...].astype(F32)
        for ref in refs[1:-1]:
            total = total + ref[...].astype(F32)
        refs[-1][...] = (x_ref[...].astype(F32) + total + (vec[4:5, :] + vec[5:6, :])).astype(BF16)

    unit = tile_of(count, 256)
    tile = pl.BlockSpec((unit, width), lambda i, ids: (i, 0))
    return call(
        kernel,
        ids,
        (count // unit,),
        [tile, pl.BlockSpec(vectors.shape, lambda i, ids: (0, 0))] + [tile] * len(parts),
        tile,
        jax.ShapeDtypeStruct((count, width), BF16),
        (rows, vectors, *parts),
        after=after,
        lag=lag,
        name="output",
    )


def widen_kernel(ids, rows, spare=0, after=(), lag=0.05):
    count, width = rows.shape[0], rows.shape[1] - spare

    def kernel(ids_ref, *refs):
        half = len(refs) // 2
        for in_ref, out_ref in zip(refs[:half], refs[half:]):
            out_ref[...] = in_ref[...].astype(F32)

    specs = [pl.BlockSpec((count, width), lambda i, ids: (0, 0))]
    shapes = [jax.ShapeDtypeStruct((count, width), F32)]
    if spare:
        specs.append(pl.BlockSpec((count, spare), lambda i, ids: (0, width // spare)))
        shapes.append(jax.ShapeDtypeStruct((count, spare), F32))
    out_specs = [pl.BlockSpec(shape.shape, lambda i, ids: (0, 0)) for shape in shapes]
    return call(
        kernel,
        ids,
        (1,),
        specs,
        out_specs,
        shapes,
        (rows,) * len(specs),
        after=after,
        lag=lag,
        name="widen",
    )


def total_kernel(ids, parts, after=(), lag=0.05):
    rows, width = parts[0].shape

    def kernel(ids_ref, *refs):
        total = refs[0][...].astype(F32)
        for ref in refs[1:-1]:
            total = total + ref[...].astype(F32)
        refs[-1][...] = total

    unit = min(rows, 256)
    tile = pl.BlockSpec((unit, width), lambda i, ids: (i, 0))
    return call(
        kernel,
        ids,
        (rows // unit,),
        [tile] * len(parts),
        tile,
        jax.ShapeDtypeStruct((rows, width), F32),
        tuple(parts),
        after=after,
        lag=lag,
        name="total",
    )


def input_kernel(ids, rows, seed, parts, after=(), lag=0.05):
    count, width = rows.shape

    def kernel(ids_ref, x_ref, g_ref, *refs):
        back = refs[0][...].astype(F32)
        for ref in refs[1:-1]:
            back = back + ref[...].astype(F32)
        data = x_ref[...].astype(F32)
        centre = data - jnp.mean(data, axis=-1, keepdims=True)
        rstd = lax.rsqrt(jnp.mean(centre * centre, axis=-1, keepdims=True) + EPSILON)
        scaled = centre * rstd
        inner = jnp.mean(back * scaled, axis=-1, keepdims=True)
        back = back - jnp.mean(back, axis=-1, keepdims=True) - scaled * inner
        refs[-1][...] = g_ref[...].astype(F32) + rstd * back

    unit = tile_of(count, 256)
    tile = pl.BlockSpec((unit, width), lambda i, ids: (i, 0))
    return call(
        kernel,
        ids,
        (count // unit,),
        [tile] * (2 + len(parts)),
        tile,
        jax.ShapeDtypeStruct((count, width), F32),
        (rows, seed, *parts),
        after=after,
        lag=lag,
        name="input",
    )


def rotary_tables(length):
    position = jnp.arange(length, dtype=F32)[:, None]
    lane = jnp.arange(128)
    half = ROTARY // 2
    frequency = 10000.0 ** (-2.0 * (lane % half).astype(F32) / ROTARY)
    angles = position * frequency[None, :]
    sine = jnp.sin(angles)
    return (
        jnp.where(lane < ROTARY, jnp.cos(angles), 1.0),
        jnp.where(lane < half, -sine, 0.0),
        jnp.where((lane >= half) & (lane < ROTARY), sine, 0.0),
    )


def flip(value, axis, bit, size):
    return lax.ppermute(value, axis, [(i, i ^ bit) for i in range(size)])


def sum_over(value, axis, size):
    bit = 1
    while bit < size:
        value = value + flip(value, axis, bit, size)
        bit *= 2
    return value


def half_kernel(ids, rows, number, after=(), lag=0.05):
    count, width = rows.shape[0] // 2, rows.shape[1]

    def kernel(ids_ref, in_ref, out_ref):
        out_ref[...] = in_ref[...]

    return call(
        kernel,
        ids,
        (1,),
        [pl.BlockSpec((count, width), lambda i, ids: (number, 0))],
        pl.BlockSpec((count, width), lambda i, ids: (0, 0)),
        jax.ShapeDtypeStruct((count, width), BF16),
        (rows,),
        after=after,
        lag=lag,
        name="half",
    )


def gather_rows(ids, rows, size, after=()):
    if size != 4:
        return [rows] + [flip(rows, "tensor", k, size) for k in range(1, size)]
    one = flip(rows, "tensor", 1, size)
    two = flip(rows, "tensor", 2, size)
    upper = flip(half_kernel(ids, two, 0, after), "tensor", 1, size)
    lower = flip(half_kernel(ids, one, 1, after), "tensor", 2, size)
    return [rows, one, two, upper, lower]


def swap_core(value, size):
    return flip(value, "dp", 1, size)


class LineGather:
    def __init__(self, ids, shard, core, size):
        self.ids, self.size = ids, size
        depth, width = shard.shape
        halves = jnp.transpose(shard.reshape(depth, 2, width // 2), (1, 0, 2))
        self.mine = lax.dynamic_index_in_dim(halves, core, 0, keepdims=False)
        self.other = swap_core(lax.dynamic_index_in_dim(halves, 1 - core, 0, keepdims=False), size)
        self.bit, self.place, self.chunks = size // 4, 1, 1
        self.first = True

    def step(self, after=()):
        self.mine = join_kernel(self.ids, self.mine, self.other, self.place, self.chunks, after)
        self.chunks = 1 if self.first else 2 * self.chunks
        self.first = False
        self.place = 1 + self.bit.bit_length()
        self.other = flip(self.mine, "dp", 2 * self.bit, self.size)
        self.bit //= 2
        return self.mine

    def open(self):
        return self.bit >= 1

    def cross(self, after=()):
        self.other = stack_kernel(self.ids, [self.other], self.other.shape[0], after=after)
        self.across = [swap_core(value, self.size) for value in (self.mine, self.other)]
        return self.other

    def finish(self, after=()):
        return assemble_kernel(self.ids, (self.mine, self.other, *self.across), self.place, self.chunks, after)


def body(
    layer_input,
    cotangent,
    firstgain,
    firstbias,
    secondgain,
    secondbias,
    project,
    projbias,
    merging,
    mergebias,
    expand,
    expandbias,
    shrink,
    shrinkbias,
):
    n_dp, n_tensor = lax.axis_size("dp"), lax.axis_size("tensor")
    dp_at, tensor_at = lax.axis_index("dp"), lax.axis_index("tensor")
    chip, core = dp_at // 2, dp_at % 2
    bits = [(chip >> bit) & 1 for bit in range((n_dp // 2).bit_length() - 1)]
    ids = jnp.stack([tensor_at, core, *bits]).astype(jnp.int32)
    own_count, width = layer_input.shape
    group_count = own_count * n_tensor
    assert group_count == LENGTH
    depth = width // n_dp
    heads = project.shape[1]
    mixed_width = heads * 3 * HEAD_DIM
    hidden_width = expand.shape[1]

    packed = jnp.concatenate(
        [firstgain, firstbias, secondgain, secondbias, mergebias, shrinkbias, expandbias, projbias.reshape(-1)]
    )
    slots = jnp.where(jnp.arange(n_dp)[:, None] == dp_at, packed[None, :], jnp.zeros((), BF16))
    slots = sum_over(slots, "dp", n_dp).astype(F32)
    vectors = jnp.transpose(slots[:, : 6 * depth].reshape(n_dp, 6, depth), (1, 0, 2)).reshape(6, width)
    at = 6 * depth
    part = hidden_width // n_dp
    b_expand = slots[:, at : at + part].reshape(1, hidden_width)
    at += part
    b_project = jnp.transpose(slots[:, at:].reshape(n_dp, heads, -1), (1, 0, 2)).reshape(1, mixed_width)

    tables = rotary_tables(LENGTH)
    own_project = project.reshape(depth, mixed_width)
    w_project = lax.all_gather(own_project, "dp", axis=0, tiled=True)
    w_expand = lax.all_gather(expand, "dp", axis=0, tiled=True)
    w_shrink = lax.all_gather(shrink, "dp", axis=1, tiled=True)
    merge_line = LineGather(ids, jnp.transpose(merging), core, n_dp)
    unit = own_count
    rows_pieces = gather_rows(ids, layer_input, n_tensor, (vectors,))
    near, far = (rows_pieces[:-1], rows_pieces[-1:]) if n_tensor != 4 else (rows_pieces[:3], rows_pieces[3:])
    pair = norm_kernel(ids, near, vectors, unit, 0, n_tensor)
    mixed = mixed_kernel(ids, pair[0], w_project, b_project, tables, 0, n_tensor - 1, n_tensor)
    last = merge_line.step((mixed[0],))
    later = stack_kernel(ids, [cotangent], unit, after=(last, *far))
    seed_pieces = [later] + [flip(later, "tensor", k, n_tensor) for k in range(n_tensor - 1, 0, -1)]
    first, second = norm_kernel(ids, far, vectors, unit, n_tensor - 1, n_tensor, kept=pair, after=(later,))
    (mixed,) = mixed_kernel(ids, first, w_project, b_project, tables, n_tensor - 1, 1, n_tensor, kept=mixed)
    last = mixed
    while merge_line.open():
        last = merge_line.step((last,))
    context, lse = attend_kernel(ids, mixed, n_tensor, after=(last,), lag=12)
    last = merge_line.cross((context,))
    hidden, slope = expand_kernel(ids, second, w_expand, b_expand, after=(last,))
    w_merge = merge_line.finish((hidden,))
    seed = stack_kernel(ids, seed_pieces[:1] + seed_pieces[:0:-1], unit, after=(w_merge,))
    merge_width = merging.shape[0]
    joint = hidden_width + merge_width
    part = full_grad_kernel(ids, context, seed, start=hidden_width, count=joint)
    part = full_grad_kernel(ids, hidden, seed, count=joint, kept=part)
    joint_grad = lax.psum_scatter(part[0], "dp", scatter_dimension=1, tiled=True)
    cgrad = plain_kernel(ids, seed, w_merge, after=part)
    mgrad, mixed_sum = attend_back_kernel(ids, mixed, cgrad, context, lse, tables, n_tensor)
    project_part, gain_one, bias_one = full_grad_kernel(ids, first, mgrad, w_project, mixed_sum)
    project_grad = lax.psum_scatter(project_part, "dp", scatter_dimension=0, tiled=True)
    branches = branches_kernel(ids, context, w_merge, hidden, w_shrink, n_tensor, after=(project_part,))
    summed = [branches[0]] + [flip(branches[k], "tensor", k, n_tensor) for k in range(n_tensor - 1, 0, -1)]
    pgrad, expand_sum = shrink_back_kernel(ids, seed, w_shrink, slope, after=(branches[0],))
    expand_part, gain_two, bias_two = full_grad_kernel(ids, second, pgrad, w_expand, expand_sum, spare=128)

    def slots(values):
        return jnp.pad(values, ((0, 0), (0, depth - values.shape[1]))).reshape(width)

    narrow = [
        jnp.sum(cotangent.astype(F32), axis=0),
        slots(expand_sum.reshape(n_dp, -1)),
        slots(jnp.transpose(mixed_sum.reshape(heads, n_dp, -1), (1, 0, 2)).reshape(n_dp, -1)),
    ]
    narrow = jnp.pad(jnp.stack(narrow, axis=1), ((0, 0), (4, 128 - 4 - len(narrow))))
    expand_part = spare_kernel(ids, expand_part, [gain_one, bias_one, gain_two, bias_two], narrow)
    expand_grad = lax.psum_scatter(expand_part, "dp", scatter_dimension=0, tiled=True)
    (joint_grad,) = widen_kernel(ids, joint_grad, after=(expand_part,))
    shrink_grad, merging_grad = joint_grad[:hidden_width], joint_grad[hidden_width:]
    gains = jnp.stack([vectors[0], vectors[2]])
    back = []
    last = joint_grad
    half = n_tensor // 2
    for start, count in ((half + 1, half - 1), (1, half), (0, 1)):
        made = back_kernel(ids, mgrad, w_project, pgrad, w_expand, gains, start, count, n_tensor, after=(last,))
        back.append([flip(made[k], "tensor", start + k, n_tensor) if start else made[k] for k in range(count - 1, -1, -1)])
        last = made[0]
        if len(back) == 1:
            (project_grad,) = widen_kernel(ids, project_grad, after=(last,))
            last = layer_output = output_kernel(ids, layer_input, summed, vectors, after=(project_grad,), lag=165)
    far = total_kernel(ids, back[0] + back[2], after=(last,), lag=4)
    expand_grad, sums = widen_kernel(ids, expand_grad, spare=128, after=(far,))
    input_grad = input_kernel(ids, layer_input, cotangent, back[1] + [far], after=(expand_grad,), lag=160)

    sums = jnp.transpose(sums[:, :7] + sums[:, 64:71])
    norms = sums[:5]
    norms = norms + sum(flip(norms, "tensor", k, n_tensor) for k in range(1, n_tensor))
    gain_one, bias_one, gain_two, bias_two, seed_sum = norms
    gain_one = (gain_one - firstbias.astype(F32) * bias_one) / firstgain.astype(F32)
    gain_two = (gain_two - secondbias.astype(F32) * bias_two) / secondgain.astype(F32)
    expandbias_grad = sums[5, : expandbias.shape[0]]
    projbias_grad = sums[6, : projbias.size].reshape(projbias.shape)
    return (
        layer_output,
        input_grad,
        gain_one,
        bias_one,
        gain_two,
        bias_two,
        project_grad.reshape(project.shape),
        projbias_grad,
        merging_grad,
        seed_sum,
        expand_grad,
        expandbias_grad,
        shrink_grad,
        seed_sum,
    )


def solution(mesh):
    specs = (
        P(("dp", "tensor"), None),
        P(("dp", "tensor"), None),
        P("dp"),
        P("dp"),
        P("dp"),
        P("dp"),
        P("dp", "tensor", None),
        P("tensor", "dp"),
        P("tensor", "dp"),
        P("dp"),
        P("dp", "tensor"),
        P(("tensor", "dp")),
        P("tensor", "dp"),
        P("dp"),
    )
    return jax.shard_map(body, mesh=mesh, in_specs=specs, out_specs=specs, check_vma=False)
```

```python
import jax
import jax.numpy as jnp
from jax import lax
from jax.experimental import pallas as pl
from jax.experimental.pallas import tpu as pltpu
from jax.sharding import PartitionSpec as P

HEAD_DIM = 256
ROTARY = 64
LENGTH = 2048
EPSILON = 1e-05
BIG = -1e30
F32 = jnp.float32
BF16 = jnp.bfloat16
DIMS = {
    "NN": (((1,), (0,)), ((), ())),
    "NT": (((1,), (1,)), ((), ())),
    "TN": (((0,), (0,)), ((), ())),
}


def product(left, right, mode):
    return lax.dot_general(left, right, DIMS[mode], preferred_element_type=F32)


def params():
    return pltpu.CompilerParams(vmem_limit_bytes=56 << 20)


def cost(lag):
    return pl.CostEstimate(flops=int(lag * 1e9), bytes_accessed=0, transcendentals=0)


def tile_of(width, most):
    best = 128
    for size in range(128, most + 1, 128):
        if width % size == 0:
            best = size
    return best


def call(kernel, ids, grid, in_specs, out_specs, out_shape, args, name, scratch=(), after=(), kept=(), lag=0.05):
    count = len(args)
    unread = tuple(kept) + tuple(after)

    def run(ids_ref, *refs):
        kernel(ids_ref, *refs[:count], *refs[count + len(unread) :])

    return pl.pallas_call(
        run,
        grid_spec=pltpu.PrefetchScalarGridSpec(
            num_scalar_prefetch=1,
            grid=grid,
            in_specs=list(in_specs) + [pl.BlockSpec(memory_space=pl.ANY)] * len(unread),
            out_specs=out_specs,
            scratch_shapes=list(scratch),
        ),
        out_shape=out_shape,
        input_output_aliases={1 + count + k: k for k in range(len(kept))},
        compiler_params=params(),
        cost_estimate=cost(lag),
        name=name,
    )(ids, *args, *unread)


def group(pieces, unit):
    blocks, filled = [], unit
    for number, piece in enumerate(pieces):
        if filled == unit:
            blocks.append([])
            filled = 0
        blocks[-1].append((number, filled))
        filled += piece.shape[0]
    return blocks


def norm_kernel(ids, pieces, vectors, unit, start, total, kept=(), after=(), lag=0.05):
    width = pieces[0].shape[1]
    blocks = group(pieces, unit)

    def kernel(ids_ref, *refs):
        vec = refs[len(pieces)]
        first_ref, second_ref = refs[len(pieces) + 1 :]
        for step, block in enumerate(blocks):

            @pl.when(pl.program_id(0) == step)
            def _(block=block):
                for number, row in block:
                    rows = slice(row, row + pieces[number].shape[0])
                    data = refs[number][...].astype(F32)
                    centre = data - jnp.mean(data, axis=-1, keepdims=True)
                    spread = jnp.mean(centre * centre, axis=-1, keepdims=True)
                    scaled = centre * lax.rsqrt(spread + EPSILON)
                    first_ref[rows, :] = (scaled * vec[0:1, :] + vec[1:2, :]).astype(BF16)
                    second_ref[rows, :] = (scaled * vec[2:3, :] + vec[3:4, :]).astype(BF16)

    out = pl.BlockSpec((unit, width), lambda i, ids: (start + i, 0))
    shape = jax.ShapeDtypeStruct((total * unit, width), BF16)
    return call(
        kernel,
        ids,
        (len(blocks),),
        [pl.BlockSpec(array.shape, lambda i, ids: (0, 0)) for array in (*pieces, vectors)],
        [out, out],
        [shape, shape],
        (*pieces, vectors),
        kept=kept,
        after=after,
        lag=lag,
        name="norm",
    )


def rotate(block, cos, sin_low, sin_high, sign):
    lead = block[:, :128]
    turned = (
        lead * cos
        + sign * (pltpu.roll(lead, 96, 1) * sin_low + pltpu.roll(lead, 32, 1) * sin_high)
    )
    return jnp.concatenate([turned, block[:, 128:]], axis=1)


def mixed_kernel(ids, first, weight, place, bias, tables, start, count, blocks, kept=(), after=(), lag=0.05):
    rows, depth = first.shape
    heads = bias.shape[1] // (3 * HEAD_DIM)
    unit = rows // blocks
    wide = 3 * HEAD_DIM

    def kernel(ids_ref, a_ref, *refs):
        b_ref, cos, low, high, out_ref = refs[3:]
        for part in range(3):
            here = slice(part * HEAD_DIM, (part + 1) * HEAD_DIM)
            value = product(a_ref[...], refs[part][...], "NN") + b_ref[:, here]
            if part < 2:
                value = rotate(value, cos[...], low[...], high[...], 1.0)
            out_ref[:, here] = value.astype(BF16)

    table = pl.BlockSpec((unit, 128), lambda j, i, ids: (ids[0] ^ (start + i), 0))
    return call(
        kernel,
        ids,
        (heads, count),
        [
            pl.BlockSpec((unit, depth), lambda j, i, ids: (start + i, 0)),
            *[
                pl.BlockSpec((depth, HEAD_DIM), lambda j, i, ids, part=part: (0, place // HEAD_DIM + 3 * j + part))
                for part in range(3)
            ],
            pl.BlockSpec((1, wide), lambda j, i, ids: (0, j)),
            table,
            table,
            table,
        ],
        [pl.BlockSpec((unit, wide), lambda j, i, ids: (start + i, j))],
        [jax.ShapeDtypeStruct((rows, heads * wide), BF16)],
        (first, weight, weight, weight, bias, *tables),
        kept=kept,
        after=after,
        lag=lag,
        name="mixed",
    )


def attend_kernel(ids, mixed, blocks, after=(), lag=0.05):
    rows, width = mixed.shape
    heads = width // (3 * HEAD_DIM)
    unit = rows // blocks
    lanes = range(0, unit, 128)
    scale = HEAD_DIM ** (-0.5)

    def kernel(ids_ref, x_ref, ctx_ref, lse_ref):
        me = ids_ref[0]

        def place(block):
            return pl.ds(pl.multiple_of((me ^ block) * unit, unit), unit)

        def head_of(block, head):
            at = 3 * HEAD_DIM * head
            query = x_ref[place(block), at : at + HEAD_DIM] * jnp.asarray(scale, BF16)
            tiles = []
            for other in range(block + 1):
                scores = product(query, x_ref[place(other), at + HEAD_DIM : at + 2 * HEAD_DIM], "NT")
                if other == block:
                    row_at = lax.broadcasted_iota(jnp.int32, scores.shape, 0)
                    col_at = lax.broadcasted_iota(jnp.int32, scores.shape, 1)
                    scores = jnp.where(col_at <= row_at, scores, BIG)
                tiles.append(scores)
            top = None
            for scores in tiles:
                for lane in lanes:
                    piece = scores[:, lane : lane + 128]
                    top = piece if top is None else jnp.maximum(top, piece)
            top = jnp.max(top, axis=1, keepdims=True)
            total = acc = None
            for other, scores in enumerate(tiles):
                weight = jnp.exp(scores - top)
                for lane in lanes:
                    piece = weight[:, lane : lane + 128]
                    total = piece if total is None else total + piece
                value = x_ref[place(other), at + 2 * HEAD_DIM : at + 3 * HEAD_DIM]
                made = product(weight.astype(BF16), value, "NN")
                acc = made if acc is None else acc + made
            total = jnp.sum(total, axis=1, keepdims=True)
            ctx_ref[:, HEAD_DIM * head : HEAD_DIM * (head + 1)] = (acc / total).astype(BF16)
            log_total = jnp.broadcast_to(top + jnp.log(total), (unit, 128))
            lse_ref[head, 0] = jnp.transpose(log_total)[:8]

        for block in range(blocks):

            @pl.when(pl.program_id(0) == block)
            def _(block=block):
                for head in range(heads):
                    head_of(block, head)

    return call(
        kernel,
        ids,
        (blocks,),
        [pl.BlockSpec((rows, width), lambda b, ids: (0, 0))],
        [
            pl.BlockSpec((unit, heads * HEAD_DIM), lambda b, ids: (ids[0] ^ b, 0)),
            pl.BlockSpec((heads, 1, 8, unit), lambda b, ids: (0, b, 0, 0)),
        ],
        [
            jax.ShapeDtypeStruct((rows, heads * HEAD_DIM), BF16),
            jax.ShapeDtypeStruct((heads, blocks, 8, unit), F32),
        ],
        (mixed,),
        after=after,
        lag=lag,
        name="attend",
    )


def attend_back_kernel(ids, mixed, grad, context, lse, tables, blocks, after=(), lag=0.05):
    rows, width = mixed.shape
    heads = width // (3 * HEAD_DIM)
    unit = rows // blocks
    scale = HEAD_DIM ** (-0.5)

    def kernel(ids_ref, x_ref, g_ref, c_ref, lse_ref, cos, low, high, out_ref, sum_ref, dk_s, dv_s):
        me = ids_ref[0]

        def place(block):
            return pl.ds(pl.multiple_of((me ^ block) * unit, unit), unit)

        def head_of(block, head):
            at = 3 * HEAD_DIM * head
            cols = slice(HEAD_DIM * head, HEAD_DIM * (head + 1))
            query = x_ref[place(block), at : at + HEAD_DIM] * jnp.asarray(scale, BF16)
            seed = g_ref[place(block), cols]
            inner = jnp.sum(seed.astype(F32) * c_ref[place(block), cols].astype(F32), axis=1, keepdims=True)
            inner = jnp.transpose(jnp.broadcast_to(inner, (unit, 128)))[:1]
            log_total = lse_ref[head, 0][:1]
            dquery = None
            for other in reversed(range(block + 1)):
                key = x_ref[place(other), at + HEAD_DIM : at + 2 * HEAD_DIM]
                value = x_ref[place(other), at + 2 * HEAD_DIM : at + 3 * HEAD_DIM]
                prob = jnp.exp(product(key, query, "NT") - log_total)
                if other == block:
                    key_at = lax.broadcasted_iota(jnp.int32, prob.shape, 0)
                    row_at = lax.broadcasted_iota(jnp.int32, prob.shape, 1)
                    prob = jnp.where(key_at <= row_at, prob, 0.0)
                dscore = (prob * (product(value, seed, "NT") - inner)).astype(BF16)
                dvalue = product(prob.astype(BF16), seed, "NN")
                dkey = product(dscore, query, "NN")
                if block < blocks - 1:
                    dvalue = dvalue + dv_s[head, other]
                    dkey = dkey + dk_s[head, other]
                if other < block:
                    dv_s[head, other] = dvalue
                    dk_s[head, other] = dkey
                else:
                    done = (dkey, dvalue)
                made = product(dscore, key, "TN")
                dquery = made if dquery is None else dquery + made
            dquery = rotate(dquery * scale, cos[...], low[...], high[...], -1.0)
            dkey = rotate(done[0], cos[...], low[...], high[...], -1.0)
            for part, value in enumerate((dquery, dkey, done[1])):
                cols = slice(at + part * HEAD_DIM, at + (part + 1) * HEAD_DIM)
                rounded = value.astype(BF16)
                out_ref[:, cols] = rounded
                column = jnp.sum(rounded.astype(F32), axis=0, keepdims=True)
                if block < blocks - 1:
                    column = column + sum_ref[:, cols]
                sum_ref[:, cols] = column

        for turn in range(blocks):

            @pl.when(pl.program_id(0) == turn)
            def _(turn=turn):
                for head in range(heads):
                    head_of(blocks - 1 - turn, head)

    def whole(cols):
        return pl.BlockSpec((rows, cols), lambda b, ids: (0, 0))

    table = pl.BlockSpec((unit, 128), lambda b, ids: (blocks - 1 - b, 0))
    return call(
        kernel,
        ids,
        (blocks,),
        [
            whole(width),
            whole(heads * HEAD_DIM),
            whole(heads * HEAD_DIM),
            pl.BlockSpec((heads, 1, 8, unit), lambda b, ids: (0, blocks - 1 - b, 0, 0)),
            table,
            table,
            table,
        ],
        [
            pl.BlockSpec((unit, width), lambda b, ids: (ids[0] ^ (blocks - 1 - b), 0)),
            pl.BlockSpec((1, width), lambda b, ids: (0, 0)),
        ],
        [jax.ShapeDtypeStruct((rows, width), BF16), jax.ShapeDtypeStruct((1, width), F32)],
        (mixed, grad, context, lse, *tables),
        scratch=[
            pltpu.VMEM((heads, blocks, unit, HEAD_DIM), F32),
            pltpu.VMEM((heads, blocks, unit, HEAD_DIM), F32),
        ],
        after=after,
        lag=lag,
        name="attend_back",
    )


def expand_kernel(ids, second, weight, bias, after=(), lag=0.05):
    rows, depth = second.shape
    width = bias.shape[1]
    tall, wide = tile_of(rows, 1024), tile_of(width, 1024)
    unit = tile_of(wide, 512)

    def kernel(ids_ref, a_ref, w_ref, b_ref, hidden_ref, slope_ref):
        for part in range(wide // unit):
            here = slice(part * unit, (part + 1) * unit)
            pre = product(a_ref[...], w_ref[:, here], "NN") + b_ref[:, here]
            phi = 0.5 + 0.5 * lax.erf(pre * 0.7071067811865476)
            hidden_ref[:, here] = (pre * phi).astype(BF16)
            slope = phi + pre * (jnp.exp(-0.5 * pre * pre) * 0.3989422804014327)
            slope_ref[:, here] = slope.astype(BF16)

    out = pl.BlockSpec((tall, wide), lambda i, j, ids: (i, j))
    shape = jax.ShapeDtypeStruct((rows, width), BF16)
    return call(
        kernel,
        ids,
        (rows // tall, width // wide),
        [
            pl.BlockSpec((tall, depth), lambda i, j, ids: (i, 0)),
            pl.BlockSpec((depth, wide), lambda i, j, ids: (0, j)),
            pl.BlockSpec((1, wide), lambda i, j, ids: (0, j)),
        ],
        [out, out],
        [shape, shape],
        (second, weight, bias),
        after=after,
        lag=lag,
        name="expand",
    )


def stack_kernel(ids, pieces, unit, after=(), lag=0.05):
    width = pieces[0].shape[1]
    blocks = group(pieces, unit)

    def kernel(ids_ref, *refs):
        for step, block in enumerate(blocks):

            @pl.when(pl.program_id(0) == step)
            def _(block=block):
                for number, row in block:
                    refs[-1][row : row + pieces[number].shape[0], :] = refs[number][...]

    return call(
        kernel,
        ids,
        (len(blocks),),
        [pl.BlockSpec(piece.shape, lambda i, ids: (0, 0)) for piece in pieces],
        pl.BlockSpec((unit, width), lambda i, ids: (i, 0)),
        jax.ShapeDtypeStruct((len(blocks) * unit, width), BF16),
        tuple(pieces),
        after=after,
        lag=lag,
        name="stack",
    )


def shrink_back_kernel(ids, seed, weight, slope, after=(), lag=0.05):
    rows, depth = seed.shape
    width = slope.shape[1]
    tall, wide = tile_of(rows, 1024), tile_of(width, 1024)
    unit = tile_of(wide, 512)

    def kernel(ids_ref, a_ref, w_ref, s_ref, out_ref, sum_ref):
        @pl.when(pl.program_id(1) == 0)
        def _():
            sum_ref[...] = jnp.zeros_like(sum_ref)

        for part in range(wide // unit):
            here = slice(part * unit, (part + 1) * unit)
            grad = product(a_ref[...], w_ref[here, :], "NT") * s_ref[:, here].astype(F32)
            rounded = grad.astype(BF16)
            out_ref[:, here] = rounded
            sum_ref[:, here] += jnp.sum(rounded.astype(F32), axis=0, keepdims=True)

    tile = pl.BlockSpec((tall, wide), lambda j, i, ids: (i, j))
    return call(
        kernel,
        ids,
        (width // wide, rows // tall),
        [
            pl.BlockSpec((tall, depth), lambda j, i, ids: (i, 0)),
            pl.BlockSpec((wide, depth), lambda j, i, ids: (j, 0)),
            tile,
        ],
        [tile, pl.BlockSpec((1, wide), lambda j, i, ids: (0, j))],
        [jax.ShapeDtypeStruct((rows, width), BF16), jax.ShapeDtypeStruct((1, width), F32)],
        (seed, weight, slope),
        after=after,
        lag=lag,
        name="shrink_back",
    )


def merge_kernel(ids, seed, context, weight, place, start, span, blocks, after=(), lag=0.05):
    rows, depth = seed.shape
    width = context.shape[1]
    unit = rows // blocks

    def kernel(ids_ref, g_ref, c_ref, w_ref, back_ref, out_ref, acc_s):
        step = pl.program_id(0)
        back_ref[...] = product(g_ref[...], w_ref[...], "NT").astype(BF16)
        made = product(g_ref[...], c_ref[...], "TN")

        @pl.when(step == 0)
        def _():
            acc_s[...] = made

        @pl.when((step > 0) & (step < blocks - 1))
        def _():
            acc_s[...] += made

        @pl.when(step == blocks - 1)
        def _():
            out_ref[...] = (acc_s[...] + made).astype(BF16)

    tile = pl.BlockSpec((unit, width), lambda i, ids: (i, 0))
    return call(
        kernel,
        ids,
        (blocks,),
        [
            pl.BlockSpec((unit, depth), lambda i, ids: (i, 0)),
            tile,
            pl.BlockSpec((width, depth), lambda i, ids: (place // width, 0)),
        ],
        [tile, pl.BlockSpec((depth, width), lambda i, ids: (0, start // width))],
        [jax.ShapeDtypeStruct((rows, width), BF16), jax.ShapeDtypeStruct((depth, span), BF16)],
        (seed, context, weight),
        scratch=[pltpu.VMEM((depth, width), F32)],
        after=after,
        lag=lag,
        name="merge",
    )


def branches_kernel(ids, context, hidden, weight, blocks, after=(), lag=0.05):
    rows, deep_b = hidden.shape
    depth, deep_a = weight.shape[1], context.shape[1]
    tall, wide = rows // blocks, tile_of(depth, 1024)
    unit = tile_of(wide, 512)

    def kernel(ids_ref, a_ref, m_ref, h_ref, s_ref, *out_refs):
        for block, out_ref in enumerate(out_refs):

            @pl.when(pl.program_id(1) == block)
            def _(out_ref=out_ref):
                for part in range(wide // unit):
                    here = slice(part * unit, (part + 1) * unit)
                    value = product(h_ref[...], s_ref[:, here], "NN")
                    value = value + product(a_ref[...], m_ref[:, here], "NN")
                    out_ref[:, here] = value.astype(BF16)

    return call(
        kernel,
        ids,
        (depth // wide, blocks),
        [
            pl.BlockSpec((tall, deep_a), lambda j, i, ids: (i, 0)),
            pl.BlockSpec((deep_a, wide), lambda j, i, ids: (deep_b // deep_a, j)),
            pl.BlockSpec((tall, deep_b), lambda j, i, ids: (i, 0)),
            pl.BlockSpec((deep_b, wide), lambda j, i, ids: (0, j)),
        ],
        [pl.BlockSpec((tall, wide), lambda j, i, ids: (0, j))] * blocks,
        [jax.ShapeDtypeStruct((tall, depth), BF16)] * blocks,
        (context, weight, hidden, weight),
        after=after,
        lag=lag,
        name="branches",
    )


def back_kernel(ids, left_a, left_b, right, scales, start, count, blocks, after=(), lag=0.05):
    rows = left_a.shape[0] // blocks
    width = right.shape[0]
    deep_a, deep_b = left_a.shape[1], left_b.shape[1]
    wide = tile_of(width, 512)
    unit = tile_of(wide, 512)

    def kernel(ids_ref, a_ref, b_ref, c_ref, d_ref, s_ref, *out_refs):
        for block, out_ref in enumerate(out_refs):

            @pl.when(pl.program_id(1) == block)
            def _(out_ref=out_ref):
                for part in range(wide // unit):
                    here = slice(part * unit, (part + 1) * unit)
                    one = product(a_ref[...], b_ref[here, :], "NT") * s_ref[0:1, here]
                    two = product(c_ref[...], d_ref[here, :], "NT") * s_ref[1:2, here]
                    out_ref[:, here] = (one + two).astype(BF16)

    return call(
        kernel,
        ids,
        (width // wide, count),
        [
            pl.BlockSpec((rows, deep_a), lambda j, i, ids: (start + i, 0)),
            pl.BlockSpec((pl.Element(wide), pl.Element(deep_a)), lambda j, i, ids: (j * wide, deep_b)),
            pl.BlockSpec((rows, deep_b), lambda j, i, ids: (start + i, 0)),
            pl.BlockSpec((wide, deep_b), lambda j, i, ids: (j, 0)),
            pl.BlockSpec((2, wide), lambda j, i, ids: (0, j)),
        ],
        [pl.BlockSpec((rows, wide), lambda j, i, ids: (0, j))] * count,
        [jax.ShapeDtypeStruct((rows, width), BF16)] * count,
        (left_a, right, left_b, right, scales),
        after=after,
        lag=lag,
        name="back",
    )


def full_grad_kernel(ids, left, right, weight=None, total=None, place=0, spare=0, start=0, span=0, kept=(), after=(), lag=0.05):
    rows, depth = left.shape
    width = right.shape[1]
    tall, wide = tile_of(depth, 1024), tile_of(width, 512 if span else 1024)
    unit = tile_of(wide, 512)
    summed = weight is not None

    def kernel(ids_ref, a_ref, b_ref, *refs):
        out_ref = refs[2 if summed else 0]
        if summed:

            @pl.when(pl.program_id(1) == 0)
            def _():
                refs[3][...] = jnp.zeros_like(refs[3])
                refs[4][...] = jnp.zeros_like(refs[4])

        for part in range(wide // unit):
            here = slice(part * unit, (part + 1) * unit)
            value = product(a_ref[...], b_ref[:, here], "TN")
            out_ref[:, here] = value.astype(BF16)
            if summed:
                held = refs[0][:, here].astype(F32)
                one, two = held * value, held * refs[1][:, here]
                refs[3][...] += sum(one[:, lane : lane + 128] for lane in range(0, unit, 128))
                refs[4][...] += sum(two[:, lane : lane + 128] for lane in range(0, unit, 128))

    tile = pl.BlockSpec((tall, wide), lambda i, j, ids: (i, j))
    in_specs = [
        pl.BlockSpec((rows, tall), lambda i, j, ids: (0, i)),
        pl.BlockSpec((rows, wide), lambda i, j, ids: (0, j)),
    ]
    out_specs = [pl.BlockSpec((tall, wide), lambda i, j, ids: (i, start // wide + j))]
    out_shape = [jax.ShapeDtypeStruct((depth, span or width + spare), BF16)]
    args = (left, right)
    if summed:
        args += (weight, total)
        in_specs += [
            pl.BlockSpec((tall, wide), lambda i, j, ids: (i, place // wide + j)),
            pl.BlockSpec((1, wide), lambda i, j, ids: (0, j)),
        ]
        out_specs += [pl.BlockSpec((tall, 128), lambda i, j, ids: (i, 0))] * 2
        out_shape += [jax.ShapeDtypeStruct((depth, 128), F32)] * 2
    return call(
        kernel,
        ids,
        (depth // tall, width // wide),
        in_specs,
        out_specs,
        out_shape,
        args,
        kept=kept,
        after=after,
        lag=lag,
        name="full_grad",
    )


def sums_kernel(ids, wide, rows, after=(), lag=0.05):
    depth = rows.shape[1]
    count = len(wide)

    def kernel(ids_ref, *refs):
        lane = lax.broadcasted_iota(jnp.int32, (depth, 128), 1)
        value = jnp.zeros((depth, 128), F32)
        for number, ref in enumerate(refs[:count]):
            value = jnp.where(lane == number, jnp.sum(ref[...], axis=1, keepdims=True), value)
        refs[-1][...] = refs[count][...] + jnp.transpose(value)[:8]

    def whole(shape):
        return pl.BlockSpec(shape, lambda i, ids: (0, 0))

    return call(
        kernel,
        ids,
        (1,),
        [whole((depth, 128))] * count + [whole((8, depth))],
        whole((8, depth)),
        jax.ShapeDtypeStruct((8, depth), F32),
        (*wide, rows),
        after=after,
        lag=lag,
        name="sums",
    )


def spare_kernel(ids, kept, parts, after=(), lag=0.05):
    depth = kept.shape[0]

    def kernel(ids_ref, *refs):
        total = refs[0][...]
        for ref in refs[1:-1]:
            total = total + ref[...]
        value = jnp.transpose(jnp.concatenate([total, jnp.zeros((120, depth), F32)], axis=0))
        lane = lax.broadcasted_iota(jnp.int32, (depth, 128), 1)
        rounded = value.astype(BF16).astype(F32)
        rest = pltpu.roll(value - rounded, 64, 1)
        refs[-1][...] = jnp.where(lane < 64, rounded, rest).astype(BF16)

    return call(
        kernel,
        ids,
        (1,),
        [pl.BlockSpec((8, depth), lambda i, ids: (0, 0))] * len(parts),
        [pl.BlockSpec((depth, 128), lambda i, ids: (0, kept.shape[1] // 128 - 1))],
        [jax.ShapeDtypeStruct(kept.shape, BF16)],
        tuple(parts),
        kept=(kept,),
        after=after,
        lag=lag,
        name="spare",
    )[0]


def output_kernel(ids, rows, parts, vectors, after=(), lag=0.05):
    count, width = rows.shape

    def kernel(ids_ref, x_ref, vec, *refs):
        total = refs[0][...].astype(F32)
        for ref in refs[1:-1]:
            total = total + ref[...].astype(F32)
        refs[-1][...] = (x_ref[...].astype(F32) + total + (vec[4:5, :] + vec[5:6, :])).astype(BF16)

    unit = tile_of(count, 256)
    tile = pl.BlockSpec((unit, width), lambda i, ids: (i, 0))
    return call(
        kernel,
        ids,
        (count // unit,),
        [tile, pl.BlockSpec(vectors.shape, lambda i, ids: (0, 0))] + [tile] * len(parts),
        tile,
        jax.ShapeDtypeStruct((count, width), BF16),
        (rows, vectors, *parts),
        after=after,
        lag=lag,
        name="output",
    )


def widen_kernel(ids, rows, widths, after=(), lag=0.05):
    count = rows.shape[0]
    specs, shapes, place = [], [], 0
    for width in widths:
        specs.append(pl.BlockSpec((pl.Element(count), pl.Element(width)), lambda i, ids, place=place: (0, place)))
        shapes.append(jax.ShapeDtypeStruct((count, width), F32))
        place += width

    def kernel(ids_ref, *refs):
        for in_ref, out_ref in zip(refs[: len(specs)], refs[len(specs) :]):
            out_ref[...] = in_ref[...].astype(F32)

    return call(
        kernel,
        ids,
        (1,),
        specs,
        [pl.BlockSpec(shape.shape, lambda i, ids: (0, 0)) for shape in shapes],
        shapes,
        (rows,) * len(specs),
        after=after,
        lag=lag,
        name="widen",
    )


def total_kernel(ids, parts, after=(), lag=0.05):
    rows, width = parts[0].shape

    def kernel(ids_ref, *refs):
        total = refs[0][...].astype(F32)
        for ref in refs[1:-1]:
            total = total + ref[...].astype(F32)
        refs[-1][...] = total

    unit = min(rows, 256)
    tile = pl.BlockSpec((unit, width), lambda i, ids: (i, 0))
    return call(
        kernel,
        ids,
        (rows // unit,),
        [tile] * len(parts),
        tile,
        jax.ShapeDtypeStruct((rows, width), F32),
        tuple(parts),
        after=after,
        lag=lag,
        name="total",
    )


def input_kernel(ids, rows, seed, parts, after=(), lag=0.05):
    count, width = rows.shape

    def kernel(ids_ref, x_ref, g_ref, *refs):
        back = refs[0][...].astype(F32)
        for ref in refs[1:-1]:
            back = back + ref[...].astype(F32)
        data = x_ref[...].astype(F32)
        centre = data - jnp.mean(data, axis=-1, keepdims=True)
        rstd = lax.rsqrt(jnp.mean(centre * centre, axis=-1, keepdims=True) + EPSILON)
        scaled = centre * rstd
        inner = jnp.mean(back * scaled, axis=-1, keepdims=True)
        back = back - jnp.mean(back, axis=-1, keepdims=True) - scaled * inner
        refs[-1][...] = g_ref[...].astype(F32) + rstd * back

    unit = tile_of(count, 256)
    tile = pl.BlockSpec((unit, width), lambda i, ids: (i, 0))
    return call(
        kernel,
        ids,
        (count // unit,),
        [tile] * (2 + len(parts)),
        tile,
        jax.ShapeDtypeStruct((count, width), F32),
        (rows, seed, *parts),
        after=after,
        lag=lag,
        name="input",
    )


def rotary_tables(length):
    position = jnp.arange(length, dtype=F32)[:, None]
    lane = jnp.arange(128)
    half = ROTARY // 2
    frequency = 10000.0 ** (-2.0 * (lane % half).astype(F32) / ROTARY)
    angles = position * frequency[None, :]
    sine = jnp.sin(angles)
    return (
        jnp.where(lane < ROTARY, jnp.cos(angles), 1.0),
        jnp.where(lane < half, -sine, 0.0),
        jnp.where((lane >= half) & (lane < ROTARY), sine, 0.0),
    )


def flip(value, axis, bit, size):
    return lax.ppermute(value, axis, [(i, i ^ bit) for i in range(size)])


def sum_over(value, axis, size):
    bit = 1
    while bit < size:
        value = value + flip(value, axis, bit, size)
        bit *= 2
    return value


def half_kernel(ids, rows, number, after=(), lag=0.05):
    count, width = rows.shape[0] // 2, rows.shape[1]

    def kernel(ids_ref, in_ref, out_ref):
        out_ref[...] = in_ref[...]

    return call(
        kernel,
        ids,
        (1,),
        [pl.BlockSpec((count, width), lambda i, ids: (number, 0))],
        pl.BlockSpec((count, width), lambda i, ids: (0, 0)),
        jax.ShapeDtypeStruct((count, width), BF16),
        (rows,),
        after=after,
        lag=lag,
        name="half",
    )


def gather_rows(ids, rows, size, after=()):
    if size != 4:
        return [rows] + [flip(rows, "tensor", k, size) for k in range(1, size)]
    one = flip(rows, "tensor", 1, size)
    two = flip(rows, "tensor", 2, size)
    upper = flip(half_kernel(ids, two, 0, after), "tensor", 1, size)
    lower = flip(half_kernel(ids, one, 1, after), "tensor", 2, size)
    return [rows, one, two, upper, lower]


def body(
    layer_input,
    cotangent,
    firstgain,
    firstbias,
    secondgain,
    secondbias,
    project,
    projbias,
    merging,
    mergebias,
    expand,
    expandbias,
    shrink,
    shrinkbias,
):
    n_dp, n_tensor = lax.axis_size("dp"), lax.axis_size("tensor")
    dp_at, tensor_at = lax.axis_index("dp"), lax.axis_index("tensor")
    chip, core = dp_at // 2, dp_at % 2
    bits = [(chip >> bit) & 1 for bit in range((n_dp // 2).bit_length() - 1)]
    ids = jnp.stack([tensor_at, core, *bits]).astype(jnp.int32)
    own_count, width = layer_input.shape
    group_count = own_count * n_tensor
    assert group_count == LENGTH
    depth = width // n_dp
    heads = project.shape[1]
    mixed_width = heads * 3 * HEAD_DIM
    hidden_width = expand.shape[1]

    packed = jnp.concatenate(
        [firstgain, firstbias, secondgain, secondbias, mergebias, shrinkbias, expandbias, projbias.reshape(-1)]
    )
    slots = jnp.where(jnp.arange(n_dp)[:, None] == dp_at, packed[None, :], jnp.zeros((), BF16))
    slots = sum_over(slots, "dp", n_dp).astype(F32)
    vectors = jnp.transpose(slots[:, : 6 * depth].reshape(n_dp, 6, depth), (1, 0, 2)).reshape(6, width)
    at = 6 * depth
    part = hidden_width // n_dp
    b_expand = slots[:, at : at + part].reshape(1, hidden_width)
    at += part
    b_project = jnp.transpose(slots[:, at:].reshape(n_dp, heads, -1), (1, 0, 2)).reshape(1, mixed_width)

    tables = rotary_tables(LENGTH)
    own_project = project.reshape(depth, mixed_width)
    w_in = lax.all_gather(jnp.concatenate([expand, own_project], axis=1), "dp", axis=0, tiled=True)
    w_out = lax.all_gather(jnp.concatenate([shrink, merging], axis=0), "dp", axis=1, tiled=True)

    unit = own_count
    rows_pieces = gather_rows(ids, layer_input, n_tensor, (vectors, tables[0]))
    near, far = (rows_pieces[:-1], rows_pieces[-1:]) if n_tensor != 4 else (rows_pieces[:3], rows_pieces[3:])
    pair = norm_kernel(ids, near, vectors, unit, 0, n_tensor)
    later = stack_kernel(ids, [cotangent], unit, after=(pair[0], *far))
    seed_pieces = [later] + [flip(later, "tensor", k, n_tensor) for k in range(n_tensor - 1, 0, -1)]
    first, second = norm_kernel(ids, far, vectors, unit, n_tensor - 1, n_tensor, kept=pair, after=(later,))
    hidden, slope = expand_kernel(ids, second, w_in, b_expand)
    (mixed,) = mixed_kernel(
        ids, first, w_in, hidden_width, b_project, tables, 0, n_tensor, n_tensor, after=(hidden,)
    )
    seed = stack_kernel(ids, seed_pieces[:1] + seed_pieces[:0:-1], unit, after=(mixed,))
    (shrink_part,) = full_grad_kernel(ids, hidden, seed)
    shrink_grad = lax.psum_scatter(shrink_part, "dp", scatter_dimension=1, tiled=True)
    context, lse = attend_kernel(ids, mixed, n_tensor, after=(shrink_part,))
    branches = branches_kernel(ids, context, hidden, w_out, n_tensor)
    summed = [branches[0]] + [flip(branches[k], "tensor", k, n_tensor) for k in range(n_tensor - 1, 0, -1)]
    pgrad, expand_sum = shrink_back_kernel(ids, seed, w_out, slope, after=(branches[0],))
    expand_part, gain_two, bias_two = full_grad_kernel(ids, second, pgrad, w_in, expand_sum)
    expand_grad = lax.psum_scatter(expand_part, "dp", scatter_dimension=0, tiled=True)

    merge_width = merging.shape[0]
    joint = mixed_width + merge_width + 128
    cgrad, part = merge_kernel(ids, seed, context, w_out, hidden_width, mixed_width, joint, 2, after=(expand_part,))
    mgrad, mixed_sum = attend_back_kernel(ids, mixed, cgrad, context, lse, tables, n_tensor)
    project_part, gain_one, bias_one = full_grad_kernel(
        ids, first, mgrad, w_in, mixed_sum, place=hidden_width, span=joint, kept=(part,)
    )
    (shrink_grad,) = widen_kernel(ids, shrink_grad, [shrink.shape[1]], after=(project_part,))

    def slots(values):
        return jnp.pad(values, ((0, 0), (0, depth - values.shape[1]))).reshape(1, width)

    seed_sum = jnp.sum(cotangent.astype(F32), axis=0, keepdims=True)
    over_all = jnp.pad(seed_sum, ((4, 3), (0, 0)))
    over_all = sums_kernel(ids, [gain_one, bias_one, gain_two, bias_two], over_all, after=(shrink_grad,))
    over_dp = [
        slots(expand_sum.reshape(n_dp, -1)),
        slots(jnp.transpose(mixed_sum.reshape(heads, n_dp, -1), (1, 0, 2)).reshape(n_dp, -1)),
    ]
    over_dp = jnp.pad(jnp.concatenate(over_dp, axis=0), ((5, 1), (0, 0)))
    over_tensor = [over_all] + [flip(over_all, "tensor", k, n_tensor) for k in range(n_tensor - 1, 0, -1)]

    gains = jnp.stack([vectors[0], vectors[2]])
    back = []
    last = over_all
    half = n_tensor // 2
    for start, count in ((half + 1, half - 1), (1, half), (0, 1)):
        made = back_kernel(ids, mgrad, pgrad, w_in, gains, start, count, n_tensor, after=(last,))
        back.append([flip(made[k], "tensor", start + k, n_tensor) if start else made[k] for k in range(count - 1, -1, -1)])
        last = made[0]
        if len(back) == 1:
            layer_output = output_kernel(ids, layer_input, summed, vectors, after=(last,), lag=160)
            last = spare_kernel(ids, project_part, over_tensor + [over_dp], after=(layer_output,))
            project_grad = lax.psum_scatter(last, "dp", scatter_dimension=0, tiled=True)
    (expand_grad,) = widen_kernel(ids, expand_grad, [hidden_width], after=(last,))
    far = total_kernel(ids, back[0] + back[2], after=(expand_grad,), lag=8)
    input_grad = input_kernel(ids, layer_input, cotangent, back[1] + [far], lag=162)
    project_grad, merging_grad, sums = widen_kernel(
        ids, project_grad, [mixed_width, merge_width, 128], after=(input_grad,)
    )
    sums = jnp.transpose(sums[:, :7] + sums[:, 64:71])
    gain_one, bias_one, gain_two, bias_two, seed_sum = sums[:5]
    gain_one = (gain_one - firstbias.astype(F32) * bias_one) / firstgain.astype(F32)
    gain_two = (gain_two - secondbias.astype(F32) * bias_two) / secondgain.astype(F32)
    expandbias_grad = sums[5, : expandbias.shape[0]]
    projbias_grad = sums[6, : projbias.size].reshape(projbias.shape)
    return (
        layer_output,
        input_grad,
        gain_one,
        bias_one,
        gain_two,
        bias_two,
        project_grad.reshape(project.shape),
        projbias_grad,
        jnp.transpose(merging_grad),
        seed_sum,
        expand_grad,
        expandbias_grad,
        shrink_grad,
        seed_sum,
    )


def solution(mesh):
    specs = (
        P(("dp", "tensor"), None),
        P(("dp", "tensor"), None),
        P("dp"),
        P("dp"),
        P("dp"),
        P("dp"),
        P("dp", "tensor", None),
        P("tensor", "dp"),
        P("tensor", "dp"),
        P("dp"),
        P("dp", "tensor"),
        P(("tensor", "dp")),
        P("tensor", "dp"),
        P("dp"),
    )
    return jax.shard_map(body, mesh=mesh, in_specs=specs, out_specs=specs, check_vma=False)
```

```python
import jax
import jax.numpy as jnp
from jax import lax
from jax.experimental import pallas as pl
from jax.experimental.pallas import tpu as pltpu
from jax.sharding import PartitionSpec as P

HEAD_DIM = 256
ROTARY = 64
LENGTH = 2048
EPSILON = 1e-05
BIG = -1e30
SUMS = 7
F32 = jnp.float32
BF16 = jnp.bfloat16
DIMS = {
    "NN": (((1,), (0,)), ((), ())),
    "NT": (((1,), (1,)), ((), ())),
    "TN": (((0,), (0,)), ((), ())),
}


def product(left, right, mode):
    return lax.dot_general(left, right, DIMS[mode], preferred_element_type=F32)


def params():
    return pltpu.CompilerParams(vmem_limit_bytes=56 << 20)


def cost(lag):
    return pl.CostEstimate(flops=int(lag * 1e9), bytes_accessed=0, transcendentals=0)


def tile_of(width, most):
    best = 128
    for size in range(128, most + 1, 128):
        if width % size == 0:
            best = size
    return best


def call(kernel, ids, grid, in_specs, out_specs, out_shape, args, name, scratch=(), after=(), kept=(), lag=0.05):
    count = len(args)
    unread = tuple(kept) + tuple(after)

    def run(ids_ref, *refs):
        kernel(ids_ref, *refs[:count], *refs[count + len(unread) :])

    return pl.pallas_call(
        run,
        grid_spec=pltpu.PrefetchScalarGridSpec(
            num_scalar_prefetch=1,
            grid=grid,
            in_specs=list(in_specs) + [pl.BlockSpec(memory_space=pl.ANY)] * len(unread),
            out_specs=out_specs,
            scratch_shapes=list(scratch),
        ),
        out_shape=out_shape,
        input_output_aliases={1 + count + k: k for k in range(len(kept))},
        compiler_params=params(),
        cost_estimate=cost(lag),
        name=name,
    )(ids, *args, *unread)


def group(pieces, unit):
    blocks, filled = [], unit
    for number, piece in enumerate(pieces):
        if filled == unit:
            blocks.append([])
            filled = 0
        blocks[-1].append((number, filled))
        filled += piece.shape[0]
    return blocks


def norm_kernel(ids, pieces, vectors, unit, start, total, kept=(), after=(), lag=0.05):
    width = pieces[0].shape[1]
    blocks = group(pieces, unit)

    def kernel(ids_ref, *refs):
        vec = refs[len(pieces)]
        first_ref, second_ref = refs[len(pieces) + 1 :]
        for step, block in enumerate(blocks):

            @pl.when(pl.program_id(0) == step)
            def _(block=block):
                for number, row in block:
                    rows = slice(row, row + pieces[number].shape[0])
                    data = refs[number][...].astype(F32)
                    centre = data - jnp.mean(data, axis=-1, keepdims=True)
                    spread = jnp.mean(centre * centre, axis=-1, keepdims=True)
                    scaled = centre * lax.rsqrt(spread + EPSILON)
                    first_ref[rows, :] = (scaled * vec[0:1, :] + vec[1:2, :]).astype(BF16)
                    second_ref[rows, :] = (scaled * vec[2:3, :] + vec[3:4, :]).astype(BF16)

    out = pl.BlockSpec((unit, width), lambda i, ids: (start + i, 0))
    shape = jax.ShapeDtypeStruct((total * unit, width), BF16)
    return call(
        kernel,
        ids,
        (len(blocks),),
        [pl.BlockSpec(array.shape, lambda i, ids: (0, 0)) for array in (*pieces, vectors)],
        [out, out],
        [shape, shape],
        (*pieces, vectors),
        kept=kept,
        after=after,
        lag=lag,
        name="norm",
    )


def rotate(block, table, sign):
    cos, sin_low, sin_high = table[:, :128], table[:, 128:256], table[:, 256:]
    lead = block[:, :128]
    turned = (
        lead * cos
        + sign * (pltpu.roll(lead, 96, 1) * sin_low + pltpu.roll(lead, 32, 1) * sin_high)
    )
    return jnp.concatenate([turned, block[:, 128:]], axis=1)


def mixed_kernel(ids, first, weight, place, bias, tables, blocks, after=(), lag=0.05):
    rows, depth = first.shape
    heads = bias.shape[1] // (3 * HEAD_DIM)
    unit = rows // blocks
    wide = 3 * HEAD_DIM

    def kernel(ids_ref, a_ref, w_ref, b_ref, low_ref, high_ref, out_ref):
        for part in range(3):
            here = slice(part * HEAD_DIM, (part + 1) * HEAD_DIM)
            value = product(a_ref[...], w_ref[:, here], "NN") + b_ref[:, here]
            if part < 2:
                value = rotate(value, jnp.concatenate([low_ref[...], high_ref[...]], axis=0), 1.0)
            out_ref[:, here] = value.astype(BF16)

    def table(block):
        return pl.BlockSpec((unit, 3 * 128), lambda j, i, ids: (ids[0] ^ (2 * i + block), 0))

    return call(
        kernel,
        ids,
        (heads, blocks // 2),
        [
            pl.BlockSpec((2 * unit, depth), lambda j, i, ids: (i, 0)),
            pl.BlockSpec((pl.Element(depth), pl.Element(wide)), lambda j, i, ids: (0, pl.multiple_of(place + wide * j, 128))),
            pl.BlockSpec((1, wide), lambda j, i, ids: (0, j)),
            table(0),
            table(1),
        ],
        pl.BlockSpec((2 * unit, wide), lambda j, i, ids: (i, j)),
        jax.ShapeDtypeStruct((rows, heads * wide), BF16),
        (first, weight, bias, tables, tables),
        after=after,
        lag=lag,
        name="mixed",
    )


def attend_kernel(ids, mixed, blocks, after=(), lag=0.05):
    rows, width = mixed.shape
    heads = width // (3 * HEAD_DIM)
    unit = rows // blocks
    lanes = range(0, unit, 128)
    scale = HEAD_DIM ** (-0.5)

    def kernel(ids_ref, x_ref, ctx_ref, lse_ref):
        me = ids_ref[0]

        def place(block):
            return pl.ds(pl.multiple_of((me ^ block) * unit, unit), unit)

        def head_of(block, head):
            at = 3 * HEAD_DIM * head
            query = x_ref[place(block), at : at + HEAD_DIM] * jnp.asarray(scale, BF16)
            tiles = []
            for other in range(block + 1):
                scores = product(query, x_ref[place(other), at + HEAD_DIM : at + 2 * HEAD_DIM], "NT")
                if other == block:
                    row_at = lax.broadcasted_iota(jnp.int32, scores.shape, 0)
                    col_at = lax.broadcasted_iota(jnp.int32, scores.shape, 1)
                    scores = jnp.where(col_at <= row_at, scores, BIG)
                tiles.append(scores)
            top = None
            for scores in tiles:
                for lane in lanes:
                    piece = scores[:, lane : lane + 128]
                    top = piece if top is None else jnp.maximum(top, piece)
            top = jnp.max(top, axis=1, keepdims=True)
            total = acc = None
            for other, scores in enumerate(tiles):
                weight = jnp.exp(scores - top)
                for lane in lanes:
                    piece = weight[:, lane : lane + 128]
                    total = piece if total is None else total + piece
                value = x_ref[place(other), at + 2 * HEAD_DIM : at + 3 * HEAD_DIM]
                made = product(weight.astype(BF16), value, "NN")
                acc = made if acc is None else acc + made
            total = jnp.sum(total, axis=1, keepdims=True)
            ctx_ref[:, HEAD_DIM * head : HEAD_DIM * (head + 1)] = (acc / total).astype(BF16)
            log_total = jnp.broadcast_to(top + jnp.log(total), (unit, 128))
            lse_ref[head, 0] = jnp.transpose(log_total)[:8]

        for block in range(blocks):

            @pl.when(pl.program_id(0) == block)
            def _(block=block):
                for head in range(heads):
                    head_of(block, head)

    return call(
        kernel,
        ids,
        (blocks,),
        [pl.BlockSpec((rows, width), lambda b, ids: (0, 0))],
        [
            pl.BlockSpec((unit, heads * HEAD_DIM), lambda b, ids: (ids[0] ^ b, 0)),
            pl.BlockSpec((heads, 1, 8, unit), lambda b, ids: (0, b, 0, 0)),
        ],
        [
            jax.ShapeDtypeStruct((rows, heads * HEAD_DIM), BF16),
            jax.ShapeDtypeStruct((heads, blocks, 8, unit), F32),
        ],
        (mixed,),
        after=after,
        lag=lag,
        name="attend",
    )


def attend_back_kernel(ids, mixed, grad, context, lse, tables, blocks, after=(), lag=0.05):
    rows, width = mixed.shape
    heads = width // (3 * HEAD_DIM)
    unit = rows // blocks
    scale = HEAD_DIM ** (-0.5)

    def kernel(ids_ref, x_ref, g_ref, c_ref, lse_ref, t_ref, out_ref, sum_ref, dk_s, dv_s):
        me = ids_ref[0]

        def place(block):
            return pl.ds(pl.multiple_of((me ^ block) * unit, unit), unit)

        def head_of(block, head):
            at = 3 * HEAD_DIM * head
            cols = slice(HEAD_DIM * head, HEAD_DIM * (head + 1))
            query = x_ref[place(block), at : at + HEAD_DIM] * jnp.asarray(scale, BF16)
            seed = g_ref[place(block), cols]
            inner = jnp.sum(seed.astype(F32) * c_ref[place(block), cols].astype(F32), axis=1, keepdims=True)
            inner = jnp.transpose(jnp.broadcast_to(inner, (unit, 128)))[:1]
            log_total = lse_ref[head, 0][:1]
            dquery = None
            for other in reversed(range(block + 1)):
                key = x_ref[place(other), at + HEAD_DIM : at + 2 * HEAD_DIM]
                value = x_ref[place(other), at + 2 * HEAD_DIM : at + 3 * HEAD_DIM]
                prob = jnp.exp(product(key, query, "NT") - log_total)
                if other == block:
                    key_at = lax.broadcasted_iota(jnp.int32, prob.shape, 0)
                    row_at = lax.broadcasted_iota(jnp.int32, prob.shape, 1)
                    prob = jnp.where(key_at <= row_at, prob, 0.0)
                dscore = (prob * (product(value, seed, "NT") - inner)).astype(BF16)
                dvalue = product(prob.astype(BF16), seed, "NN")
                dkey = product(dscore, query, "NN")
                if block < blocks - 1:
                    dvalue = dvalue + dv_s[head, other]
                    dkey = dkey + dk_s[head, other]
                if other < block:
                    dv_s[head, other] = dvalue
                    dk_s[head, other] = dkey
                else:
                    done = (dkey, dvalue)
                made = product(dscore, key, "TN")
                dquery = made if dquery is None else dquery + made
            dquery = rotate(dquery * scale, t_ref[...], -1.0)
            dkey = rotate(done[0], t_ref[...], -1.0)
            for part, value in enumerate((dquery, dkey, done[1])):
                cols = slice(at + part * HEAD_DIM, at + (part + 1) * HEAD_DIM)
                rounded = value.astype(BF16)
                out_ref[:, cols] = rounded
                column = jnp.sum(rounded.astype(F32), axis=0, keepdims=True)
                if block < blocks - 1:
                    column = column + sum_ref[:, cols]
                sum_ref[:, cols] = column

        for turn in range(blocks):

            @pl.when(pl.program_id(0) == turn)
            def _(turn=turn):
                for head in range(heads):
                    head_of(blocks - 1 - turn, head)

    def whole(cols):
        return pl.BlockSpec((rows, cols), lambda b, ids: (0, 0))

    table = pl.BlockSpec((unit, 3 * 128), lambda b, ids: (blocks - 1 - b, 0))
    return call(
        kernel,
        ids,
        (blocks,),
        [
            whole(width),
            whole(heads * HEAD_DIM),
            whole(heads * HEAD_DIM),
            pl.BlockSpec((heads, 1, 8, unit), lambda b, ids: (0, blocks - 1 - b, 0, 0)),
            table,
        ],
        [
            pl.BlockSpec((unit, width), lambda b, ids: (ids[0] ^ (blocks - 1 - b), 0)),
            pl.BlockSpec((1, width), lambda b, ids: (0, 0)),
        ],
        [jax.ShapeDtypeStruct((rows, width), BF16), jax.ShapeDtypeStruct((1, width), F32)],
        (mixed, grad, context, lse, tables),
        scratch=[
            pltpu.VMEM((heads, blocks, unit, HEAD_DIM), F32),
            pltpu.VMEM((heads, blocks, unit, HEAD_DIM), F32),
        ],
        after=after,
        lag=lag,
        name="attend_back",
    )


def expand_kernel(ids, second, weight, bias, after=(), lag=0.05):
    rows, depth = second.shape
    width = bias.shape[1]
    tall, wide = tile_of(rows, 1024), tile_of(width, 1024)
    unit = tile_of(wide, 512)

    def kernel(ids_ref, a_ref, w_ref, b_ref, hidden_ref, slope_ref):
        for part in range(wide // unit):
            here = slice(part * unit, (part + 1) * unit)
            pre = product(a_ref[...], w_ref[:, here], "NN") + b_ref[:, here]
            phi = 0.5 + 0.5 * lax.erf(pre * 0.7071067811865476)
            hidden_ref[:, here] = (pre * phi).astype(BF16)
            slope = phi + pre * (jnp.exp(-0.5 * pre * pre) * 0.3989422804014327)
            slope_ref[:, here] = slope.astype(BF16)

    out = pl.BlockSpec((tall, wide), lambda i, j, ids: (i, j))
    shape = jax.ShapeDtypeStruct((rows, width), BF16)
    return call(
        kernel,
        ids,
        (rows // tall, width // wide),
        [
            pl.BlockSpec((tall, depth), lambda i, j, ids: (i, 0)),
            pl.BlockSpec((depth, wide), lambda i, j, ids: (0, j)),
            pl.BlockSpec((1, wide), lambda i, j, ids: (0, j)),
        ],
        [out, out],
        [shape, shape],
        (second, weight, bias),
        after=after,
        lag=lag,
        name="expand",
    )


def stack_kernel(ids, pieces, unit, after=(), lag=0.05):
    width = pieces[0].shape[1]
    blocks = group(pieces, unit)

    def kernel(ids_ref, *refs):
        for step, block in enumerate(blocks):

            @pl.when(pl.program_id(0) == step)
            def _(block=block):
                for number, row in block:
                    refs[-1][row : row + pieces[number].shape[0], :] = refs[number][...]

    return call(
        kernel,
        ids,
        (len(blocks),),
        [pl.BlockSpec(piece.shape, lambda i, ids: (0, 0)) for piece in pieces],
        pl.BlockSpec((unit, width), lambda i, ids: (i, 0)),
        jax.ShapeDtypeStruct((len(blocks) * unit, width), BF16),
        tuple(pieces),
        after=after,
        lag=lag,
        name="stack",
    )


def shrink_back_kernel(ids, seed, weight, slope, after=(), lag=0.05):
    rows, depth = seed.shape
    width = slope.shape[1]
    tall, wide = tile_of(rows, 1024), tile_of(width, 1024)
    unit = tile_of(wide, 512)

    def kernel(ids_ref, a_ref, w_ref, s_ref, out_ref, sum_ref):
        @pl.when(pl.program_id(1) == 0)
        def _():
            sum_ref[...] = jnp.zeros_like(sum_ref)

        for part in range(wide // unit):
            here = slice(part * unit, (part + 1) * unit)
            grad = product(a_ref[...], w_ref[here, :], "NT") * s_ref[:, here].astype(F32)
            rounded = grad.astype(BF16)
            out_ref[:, here] = rounded
            sum_ref[:, here] += jnp.sum(rounded.astype(F32), axis=0, keepdims=True)

    tile = pl.BlockSpec((tall, wide), lambda j, i, ids: (i, j))
    return call(
        kernel,
        ids,
        (width // wide, rows // tall),
        [
            pl.BlockSpec((tall, depth), lambda j, i, ids: (i, 0)),
            pl.BlockSpec((wide, depth), lambda j, i, ids: (j, 0)),
            tile,
        ],
        [tile, pl.BlockSpec((1, wide), lambda j, i, ids: (0, j))],
        [jax.ShapeDtypeStruct((rows, width), BF16), jax.ShapeDtypeStruct((1, width), F32)],
        (seed, weight, slope),
        after=after,
        lag=lag,
        name="shrink_back",
    )


def merge_kernel(ids, seed, context, weight, place, start, span, blocks, after=(), lag=0.05):
    rows, depth = seed.shape
    width = context.shape[1]
    unit = rows // blocks

    def kernel(ids_ref, g_ref, c_ref, w_ref, back_ref, out_ref, acc_s):
        step = pl.program_id(0)
        back_ref[...] = product(g_ref[...], w_ref[...], "NT").astype(BF16)
        made = product(g_ref[...], c_ref[...], "TN")

        @pl.when(step == 0)
        def _():
            acc_s[...] = made

        @pl.when((step > 0) & (step < blocks - 1))
        def _():
            acc_s[...] += made

        @pl.when(step == blocks - 1)
        def _():
            out_ref[...] = (acc_s[...] + made).astype(BF16)

    tile = pl.BlockSpec((unit, width), lambda i, ids: (i, 0))
    return call(
        kernel,
        ids,
        (blocks,),
        [
            pl.BlockSpec((unit, depth), lambda i, ids: (i, 0)),
            tile,
            pl.BlockSpec((width, depth), lambda i, ids: (place // width, 0)),
        ],
        [tile, pl.BlockSpec((depth, width), lambda i, ids: (0, start // width))],
        [jax.ShapeDtypeStruct((rows, width), BF16), jax.ShapeDtypeStruct((depth, span), BF16)],
        (seed, context, weight),
        scratch=[pltpu.VMEM((depth, width), F32)],
        after=after,
        lag=lag,
        name="merge",
    )


def branches_kernel(ids, context, hidden, weight, blocks, after=(), lag=0.05):
    rows, deep_b = hidden.shape
    depth, deep_a = weight.shape[1], context.shape[1]
    tall, wide = rows // blocks, tile_of(depth, 1024)
    unit = tile_of(wide, 512)

    def kernel(ids_ref, a_ref, m_ref, h_ref, s_ref, *out_refs):
        for block in range(0, blocks, 2):

            @pl.when(pl.program_id(1) == block // 2)
            def _(block=block):
                for part in range(wide // unit):
                    here = slice(part * unit, (part + 1) * unit)
                    value = product(h_ref[...], s_ref[:, here], "NN")
                    value = value + product(a_ref[...], m_ref[:, here], "NN")
                    out_refs[block][:, here] = value[:tall].astype(BF16)
                    out_refs[block + 1][:, here] = value[tall:].astype(BF16)

    return call(
        kernel,
        ids,
        (depth // wide, blocks // 2),
        [
            pl.BlockSpec((2 * tall, deep_a), lambda j, i, ids: (i, 0)),
            pl.BlockSpec((deep_a, wide), lambda j, i, ids: (deep_b // deep_a, j)),
            pl.BlockSpec((2 * tall, deep_b), lambda j, i, ids: (i, 0)),
            pl.BlockSpec((deep_b, wide), lambda j, i, ids: (0, j)),
        ],
        [pl.BlockSpec((tall, wide), lambda j, i, ids: (0, j))] * blocks,
        [jax.ShapeDtypeStruct((tall, depth), BF16)] * blocks,
        (context, weight, hidden, weight),
        after=after,
        lag=lag,
        name="branches",
    )


def back_kernel(ids, left_a, left_b, right, scales, start, count, blocks, after=(), lag=0.05):
    rows = left_a.shape[0] // blocks
    width = right.shape[0]
    deep_a, deep_b = left_a.shape[1], left_b.shape[1]
    wide = tile_of(width, 512 if count == 1 else 1024)
    unit = tile_of(wide, 512)

    def kernel(ids_ref, a_ref, b_ref, c_ref, d_ref, s_ref, *out_refs):
        for block, out_ref in enumerate(out_refs):

            @pl.when(pl.program_id(1) == block)
            def _(out_ref=out_ref):
                for part in range(wide // unit):
                    here = slice(part * unit, (part + 1) * unit)
                    one = product(a_ref[...], b_ref[here, :], "NT") * s_ref[0:1, here]
                    two = product(c_ref[...], d_ref[here, :], "NT") * s_ref[1:2, here]
                    out_ref[:, here] = (one + two).astype(BF16)

    return call(
        kernel,
        ids,
        (width // wide, count),
        [
            pl.BlockSpec((rows, deep_a), lambda j, i, ids: (start + i, 0)),
            pl.BlockSpec((pl.Element(wide), pl.Element(deep_a)), lambda j, i, ids: (j * wide, deep_b)),
            pl.BlockSpec((rows, deep_b), lambda j, i, ids: (start + i, 0)),
            pl.BlockSpec((wide, deep_b), lambda j, i, ids: (j, 0)),
            pl.BlockSpec((2, wide), lambda j, i, ids: (0, j)),
        ],
        [pl.BlockSpec((rows, wide), lambda j, i, ids: (0, j))] * count,
        [jax.ShapeDtypeStruct((rows, width), BF16)] * count,
        (left_a, right, left_b, right, scales),
        after=after,
        lag=lag,
        name="back",
    )


def piece_grad_kernel(ids, left, pieces, after=(), lag=0.05):
    rows, width = left.shape
    unit, depth = pieces[0].shape
    tall, wide = tile_of(width, 1024), tile_of(depth, 1024)
    cut = tile_of(wide, 512)

    def kernel(ids_ref, a_ref, *refs):
        grad_ref, right_ref = refs[len(pieces) :]
        for part in range(wide // cut):
            here = slice(part * cut, (part + 1) * cut)
            total = None
            for number in range(len(pieces)):
                made = product(a_ref[number * unit : (number + 1) * unit, :], refs[number][:, here], "TN")
                total = made if total is None else total + made
            grad_ref[:, here] = total.astype(BF16)

        @pl.when(pl.program_id(1) == 0)
        def _():
            for number in range(len(pieces)):
                right_ref[number * unit : (number + 1) * unit, :] = refs[number][...]

    return call(
        kernel,
        ids,
        (depth // wide, width // tall),
        [pl.BlockSpec((rows, tall), lambda j, i, ids: (0, i))]
        + [pl.BlockSpec((unit, wide), lambda j, i, ids: (0, j))] * len(pieces),
        [
            pl.BlockSpec((tall, wide), lambda j, i, ids: (i, j)),
            pl.BlockSpec((rows, wide), lambda j, i, ids: (0, j)),
        ],
        [jax.ShapeDtypeStruct((width, depth), BF16), jax.ShapeDtypeStruct((rows, depth), BF16)],
        (left, *pieces),
        after=after,
        lag=lag,
        name="piece_grad",
    )


def full_grad_kernel(ids, left, right, weight=None, total=None, place=0, spare=0, start=0, span=0, kept=(), after=(), lag=0.05):
    rows, depth = left.shape
    width = right.shape[1]
    tall, wide = (tile_of(depth, 512), width) if span else (tile_of(depth, 1024), tile_of(width, 1024))
    unit = tile_of(wide, 512)
    summed = weight is not None

    def kernel(ids_ref, a_ref, b_ref, *refs):
        out_ref = refs[2 if summed else 0]
        if summed:

            @pl.when(pl.program_id(1) == 0)
            def _():
                refs[3][...] = jnp.zeros_like(refs[3])
                refs[4][...] = jnp.zeros_like(refs[4])

        for part in range(wide // unit):
            here = slice(part * unit, (part + 1) * unit)
            value = product(a_ref[...], b_ref[:, here], "TN")
            out_ref[:, here] = value.astype(BF16)
            if summed:
                held = refs[0][:, here].astype(F32)
                one, two = held * value, held * refs[1][:, here]
                refs[3][...] += sum(one[:, lane : lane + 128] for lane in range(0, unit, 128))
                refs[4][...] += sum(two[:, lane : lane + 128] for lane in range(0, unit, 128))

    tile = pl.BlockSpec((tall, wide), lambda i, j, ids: (i, j))
    in_specs = [
        pl.BlockSpec((rows, tall), lambda i, j, ids: (0, i)),
        pl.BlockSpec((rows, wide), lambda i, j, ids: (0, j)),
    ]
    out_specs = [pl.BlockSpec((tall, wide), lambda i, j, ids: (i, start // wide + j))]
    out_shape = [jax.ShapeDtypeStruct((depth, span or width + spare), BF16)]
    args = (left, right)
    if summed:
        args += (weight, total)
        in_specs += [
            pl.BlockSpec((pl.Element(tall), pl.Element(wide)), lambda i, j, ids: (i * tall, pl.multiple_of(place + j * wide, 128))),
            pl.BlockSpec((1, wide), lambda i, j, ids: (0, j)),
        ]
        out_specs += [pl.BlockSpec((tall, 128), lambda i, j, ids: (i, 0))] * 2
        out_shape += [jax.ShapeDtypeStruct((depth, 128), F32)] * 2
    return call(
        kernel,
        ids,
        (depth // tall, width // wide),
        in_specs,
        out_specs,
        out_shape,
        args,
        kept=kept,
        after=after,
        lag=lag,
        name="full_grad",
    )


def sums_kernel(ids, wide, rows, after=(), lag=0.05):
    depth = rows.shape[1]
    count = len(wide)

    def kernel(ids_ref, *refs):
        total = refs[count][...]
        for number, ref in enumerate(refs[:count]):
            row = lax.broadcasted_iota(jnp.int32, (8, 128), 0)
            pick = jnp.where(row == number, 1.0, 0.0).astype(BF16)
            high = ref[...].astype(BF16)
            rest = (ref[...] - high.astype(F32)).astype(BF16)
            total = total + product(pick, high, "NT") + product(pick, rest, "NT")
        refs[-1][...] = total

    def whole(shape):
        return pl.BlockSpec(shape, lambda i, ids: (0, 0))

    return call(
        kernel,
        ids,
        (1,),
        [whole((depth, 128))] * count + [whole((8, depth))],
        whole((8, depth)),
        jax.ShapeDtypeStruct((8, depth), F32),
        (*wide, rows),
        after=after,
        lag=lag,
        name="sums",
    )


def spare_kernel(ids, kept, parts, slots, after=(), lag=0.05):
    depth = kept.shape[0]

    def kernel(ids_ref, *refs):
        total = refs[0][...]
        for ref in refs[1:-1]:
            total = total + ref[...]
        rounded = total.astype(BF16).astype(F32)
        row = lax.broadcasted_iota(jnp.int32, (128, depth), 0)
        value = jnp.zeros((128, depth), F32)
        for number in range(SUMS):
            place = number * slots + ids_ref[1]
            value = jnp.where(row == place, rounded[number : number + 1], value)
            if SUMS * slots <= 64:
                value = jnp.where(row == place + 64, (total - rounded)[number : number + 1], value)
        refs[-1][...] = jnp.transpose(value).astype(BF16)

    return call(
        kernel,
        ids,
        (1,),
        [pl.BlockSpec((8, depth), lambda i, ids: (0, 0))] * len(parts),
        [pl.BlockSpec((depth, 128), lambda i, ids: (0, kept.shape[1] // 128 - 1))],
        [jax.ShapeDtypeStruct(kept.shape, BF16)],
        tuple(parts),
        kept=(kept,),
        after=after,
        lag=lag,
        name="spare",
    )[0]


def output_kernel(ids, rows, parts, vectors, after=(), lag=0.05):
    count, width = rows.shape

    def kernel(ids_ref, x_ref, vec, *refs):
        total = refs[0][...].astype(F32)
        for ref in refs[1:-1]:
            total = total + ref[...].astype(F32)
        refs[-1][...] = (x_ref[...].astype(F32) + total + (vec[4:5, :] + vec[5:6, :])).astype(BF16)

    unit = tile_of(count, 256)
    tile = pl.BlockSpec((unit, width), lambda i, ids: (i, 0))
    return call(
        kernel,
        ids,
        (count // unit,),
        [tile, pl.BlockSpec(vectors.shape, lambda i, ids: (0, 0))] + [tile] * len(parts),
        tile,
        jax.ShapeDtypeStruct((count, width), BF16),
        (rows, vectors, *parts),
        after=after,
        lag=lag,
        name="output",
    )


def widen_kernel(ids, rows, widths, after=(), lag=0.05):
    count = rows.shape[0]
    specs, shapes, place = [], [], 0
    for width in widths:
        specs.append(pl.BlockSpec((pl.Element(count), pl.Element(width)), lambda i, ids, place=place: (0, place)))
        shapes.append(jax.ShapeDtypeStruct((count, width), F32))
        place += width

    def kernel(ids_ref, *refs):
        for in_ref, out_ref in zip(refs[: len(specs)], refs[len(specs) :]):
            out_ref[...] = in_ref[...].astype(F32)

    return call(
        kernel,
        ids,
        (1,),
        specs,
        [pl.BlockSpec(shape.shape, lambda i, ids: (0, 0)) for shape in shapes],
        shapes,
        (rows,) * len(specs),
        after=after,
        lag=lag,
        name="widen",
    )


def finish_kernel(ids, rows, widths, heads, slots, after=(), lag=0.05):
    count = rows.shape[0]
    one, two = widths
    each = one // heads

    def kernel(ids_ref, in_ref, one_ref, two_ref, sums_ref):
        for head in range(heads):
            one_ref[:, head, :] = in_ref[:, head * each : (head + 1) * each].astype(F32)
        two_ref[...] = jnp.transpose(in_ref[:, one : one + two].astype(F32))
        number = lax.broadcasted_iota(jnp.int32, (8, 128), 0)
        lane = lax.broadcasted_iota(jnp.int32, (8, 128), 1)
        if SUMS * slots <= 64:
            lane = lane % 64
        mine = (lane // slots == number) & (number < SUMS)
        sums_ref[...] = product(jnp.where(mine, 1.0, 0.0).astype(BF16), in_ref[:, one + two :], "NT")

    def whole(shape):
        return pl.BlockSpec(shape, lambda i, ids: (0,) * len(shape))

    shapes = [(count, heads, each), (two, count), (8, count)]
    return call(
        kernel,
        ids,
        (1,),
        [whole(rows.shape)],
        [whole(shape) for shape in shapes],
        [jax.ShapeDtypeStruct(shape, F32) for shape in shapes],
        (rows,),
        after=after,
        lag=lag,
        name="finish",
    )


def total_kernel(ids, parts, after=(), lag=0.05):
    rows, width = parts[0].shape

    def kernel(ids_ref, *refs):
        total = refs[0][...].astype(F32)
        for ref in refs[1:-1]:
            total = total + ref[...].astype(F32)
        refs[-1][...] = total

    unit = min(rows, 256)
    tile = pl.BlockSpec((unit, width), lambda i, ids: (i, 0))
    return call(
        kernel,
        ids,
        (rows // unit,),
        [tile] * len(parts),
        tile,
        jax.ShapeDtypeStruct((rows, width), F32),
        tuple(parts),
        after=after,
        lag=lag,
        name="total",
    )


def input_kernel(ids, rows, seed, parts, after=(), lag=0.05):
    count, width = rows.shape

    def kernel(ids_ref, x_ref, g_ref, *refs):
        back = refs[0][...].astype(F32)
        for ref in refs[1:-1]:
            back = back + ref[...].astype(F32)
        data = x_ref[...].astype(F32)
        centre = data - jnp.mean(data, axis=-1, keepdims=True)
        rstd = lax.rsqrt(jnp.mean(centre * centre, axis=-1, keepdims=True) + EPSILON)
        scaled = centre * rstd
        inner = jnp.mean(back * scaled, axis=-1, keepdims=True)
        back = back - jnp.mean(back, axis=-1, keepdims=True) - scaled * inner
        refs[-1][...] = g_ref[...].astype(F32) + rstd * back

    unit = tile_of(count, 256)
    tile = pl.BlockSpec((unit, width), lambda i, ids: (i, 0))
    return call(
        kernel,
        ids,
        (count // unit,),
        [tile] * (2 + len(parts)),
        tile,
        jax.ShapeDtypeStruct((count, width), F32),
        (rows, seed, *parts),
        after=after,
        lag=lag,
        name="input",
    )


def rotary_tables(length):
    position = jnp.arange(length, dtype=F32)[:, None]
    lane = jnp.arange(128)
    half = ROTARY // 2
    frequency = 10000.0 ** (-2.0 * (lane % half).astype(F32) / ROTARY)
    angles = position * frequency[None, :]
    sine = jnp.sin(angles)
    tables = (
        jnp.where(lane < ROTARY, jnp.cos(angles), 1.0),
        jnp.where(lane < half, -sine, 0.0),
        jnp.where((lane >= half) & (lane < ROTARY), sine, 0.0),
    )
    return jnp.concatenate(tables, axis=1)


def flip(value, axis, bit, size):
    return lax.ppermute(value, axis, [(i, i ^ bit) for i in range(size)])


def sum_over(value, axis, size):
    bit = 1
    while bit < size:
        value = value + flip(value, axis, bit, size)
        bit *= 2
    return value


def half_kernel(ids, rows, number, after=(), lag=0.05):
    count, width = rows.shape[0] // 2, rows.shape[1]

    def kernel(ids_ref, in_ref, out_ref):
        out_ref[...] = in_ref[...]

    return call(
        kernel,
        ids,
        (1,),
        [pl.BlockSpec((count, width), lambda i, ids: (number, 0))],
        pl.BlockSpec((count, width), lambda i, ids: (0, 0)),
        jax.ShapeDtypeStruct((count, width), BF16),
        (rows,),
        after=after,
        lag=lag,
        name="half",
    )


def gather_rows(ids, rows, size, after=()):
    if size != 4:
        return [rows] + [flip(rows, "tensor", k, size) for k in range(1, size)]
    one = flip(rows, "tensor", 1, size)
    two = flip(rows, "tensor", 2, size)
    upper = flip(half_kernel(ids, two, 0, after), "tensor", 1, size)
    lower = flip(half_kernel(ids, one, 1, after), "tensor", 2, size)
    return [rows, one, two, upper, lower]


def body(
    layer_input,
    cotangent,
    firstgain,
    firstbias,
    secondgain,
    secondbias,
    project,
    projbias,
    merging,
    mergebias,
    expand,
    expandbias,
    shrink,
    shrinkbias,
):
    n_dp, n_tensor = lax.axis_size("dp"), lax.axis_size("tensor")
    dp_at, tensor_at = lax.axis_index("dp"), lax.axis_index("tensor")
    assert SUMS * n_dp <= 128
    ids = jnp.stack([tensor_at, dp_at]).astype(jnp.int32)
    own_count, width = layer_input.shape
    group_count = own_count * n_tensor
    assert group_count == LENGTH
    depth = width // n_dp
    heads = project.shape[1]
    mixed_width = heads * 3 * HEAD_DIM
    hidden_width = expand.shape[1]

    packed = jnp.concatenate(
        [firstgain, firstbias, secondgain, secondbias, mergebias, shrinkbias, expandbias, projbias.reshape(-1)]
    )
    slots = jnp.where(jnp.arange(n_dp)[:, None] == dp_at, packed[None, :], jnp.zeros((), BF16))
    slots = sum_over(slots, "dp", n_dp).astype(F32)
    vectors = jnp.transpose(slots[:, : 6 * depth].reshape(n_dp, 6, depth), (1, 0, 2)).reshape(6, width)
    at = 6 * depth
    part = hidden_width // n_dp
    b_expand = slots[:, at : at + part].reshape(1, hidden_width)
    at += part
    b_project = jnp.transpose(slots[:, at:].reshape(n_dp, heads, -1), (1, 0, 2)).reshape(1, mixed_width)

    tables = rotary_tables(LENGTH)
    own_project = project.reshape(depth, mixed_width)
    w_in = lax.all_gather(jnp.concatenate([expand, own_project], axis=1), "dp", axis=0, tiled=True)
    w_out = lax.all_gather(jnp.concatenate([shrink, merging], axis=0), "dp", axis=1, tiled=True)

    unit = own_count
    rows_pieces = gather_rows(ids, layer_input, n_tensor, (vectors, tables))
    near, far = (rows_pieces[:-1], rows_pieces[-1:]) if n_tensor != 4 else (rows_pieces[:3], rows_pieces[3:])
    pair = norm_kernel(ids, near, vectors, unit, 0, n_tensor)
    later = stack_kernel(ids, [cotangent], unit, after=(pair[0], *far))
    seed_pieces = [later] + [flip(later, "tensor", k, n_tensor) for k in range(n_tensor - 1, 0, -1)]
    first, second = norm_kernel(ids, far, vectors, unit, n_tensor - 1, n_tensor, kept=pair, after=(later,))
    hidden, slope = expand_kernel(ids, second, w_in, b_expand)
    mixed = mixed_kernel(ids, first, w_in, hidden_width, b_project, tables, n_tensor, after=(hidden,))
    shrink_part, seed = piece_grad_kernel(ids, hidden, seed_pieces[:1] + seed_pieces[:0:-1], after=(mixed,))
    shrink_grad = lax.psum_scatter(shrink_part, "dp", scatter_dimension=1, tiled=True)
    context, lse = attend_kernel(ids, mixed, n_tensor, after=(shrink_part,))
    branches = branches_kernel(ids, context, hidden, w_out, n_tensor)
    summed = [branches[0]] + [flip(branches[k], "tensor", k, n_tensor) for k in range(n_tensor - 1, 0, -1)]
    pgrad, expand_sum = shrink_back_kernel(ids, seed, w_out, slope, after=(branches[0],))
    expand_part, gain_two, bias_two = full_grad_kernel(ids, second, pgrad, w_in, expand_sum)
    expand_grad = lax.psum_scatter(expand_part, "dp", scatter_dimension=0, tiled=True)

    merge_width = merging.shape[0]
    joint = mixed_width + merge_width + 128
    cgrad, part = merge_kernel(ids, seed, context, w_out, hidden_width, mixed_width, joint, 2, after=(expand_part,))
    mgrad, mixed_sum = attend_back_kernel(ids, mixed, cgrad, context, lse, tables, n_tensor)
    project_part, gain_one, bias_one = full_grad_kernel(
        ids, first, mgrad, w_in, mixed_sum, place=hidden_width, span=joint, kept=(part,)
    )

    def slots(values):
        return jnp.pad(values, ((0, 0), (0, depth - values.shape[1]))).reshape(1, width)

    seed_sum = jnp.sum(cotangent.astype(F32), axis=0, keepdims=True)
    over_all = jnp.pad(seed_sum, ((4, 3), (0, 0)))
    over_all = sums_kernel(ids, [gain_one, bias_one, gain_two, bias_two], over_all)
    over_dp = [
        slots(expand_sum.reshape(n_dp, -1)),
        slots(jnp.transpose(mixed_sum.reshape(heads, n_dp, -1), (1, 0, 2)).reshape(n_dp, -1)),
    ]
    over_dp = jnp.pad(jnp.concatenate(over_dp, axis=0), ((5, 1), (0, 0)))
    over_tensor = [over_all] + [flip(over_all, "tensor", k, n_tensor) for k in range(n_tensor - 1, 0, -1)]

    gains = jnp.stack([vectors[0], vectors[2]])
    back = []
    last = over_all
    half = n_tensor // 2
    for start, count in ((half + 1, half - 1), (1, half), (0, 1)):
        made = back_kernel(ids, mgrad, pgrad, w_in, gains, start, count, n_tensor, after=(last,))
        back.append([flip(made[k], "tensor", start + k, n_tensor) if start else made[k] for k in range(count - 1, -1, -1)])
        last = made[0]
        if len(back) == 1:
            layer_output = output_kernel(ids, layer_input, summed, vectors, after=(last,), lag=160)
            last = spare_kernel(ids, project_part, over_tensor + [over_dp], n_dp, after=(layer_output,))
            project_grad = lax.psum_scatter(last, "dp", scatter_dimension=0, tiled=True)
            (shrink_grad,) = widen_kernel(ids, shrink_grad, [shrink.shape[1]], after=(last,), lag=0.05)
            last = shrink_grad
    (expand_grad,) = widen_kernel(ids, expand_grad, [hidden_width], after=(last,))
    far = total_kernel(ids, back[0] + back[2], after=(expand_grad,), lag=8)
    input_grad = input_kernel(ids, layer_input, cotangent, back[1] + [far], lag=162)
    project_grad, merging_grad, sums = finish_kernel(
        ids, project_grad, [mixed_width, merge_width], heads, n_dp, after=(input_grad,)
    )
    gain_one, bias_one, gain_two, bias_two, seed_sum = sums[:5]
    gain_one = (gain_one - firstbias.astype(F32) * bias_one) / firstgain.astype(F32)
    gain_two = (gain_two - secondbias.astype(F32) * bias_two) / secondgain.astype(F32)
    expandbias_grad = sums[5, : expandbias.shape[0]]
    projbias_grad = sums[6, : projbias.size].reshape(projbias.shape)
    return (
        layer_output,
        input_grad,
        gain_one,
        bias_one,
        gain_two,
        bias_two,
        project_grad,
        projbias_grad,
        merging_grad,
        seed_sum,
        expand_grad,
        expandbias_grad,
        shrink_grad,
        seed_sum,
    )


def solution(mesh):
    specs = (
        P(("dp", "tensor"), None),
        P(("dp", "tensor"), None),
        P("dp"),
        P("dp"),
        P("dp"),
        P("dp"),
        P("dp", "tensor", None),
        P("tensor", "dp"),
        P("tensor", "dp"),
        P("dp"),
        P("dp", "tensor"),
        P(("tensor", "dp")),
        P("tensor", "dp"),
        P("dp"),
    )
    return jax.shard_map(body, mesh=mesh, in_specs=specs, out_specs=specs, check_vma=False)
```

```python
import jax
import jax.numpy as jnp
from jax import lax
from jax.experimental import pallas as pl
from jax.experimental.pallas import tpu as pltpu
from jax.sharding import PartitionSpec as P

HEAD_DIM = 256
ROTARY = 64
LENGTH = 2048
EPSILON = 1e-05
BIG = -1e30
SUMS = 7
F32 = jnp.float32
BF16 = jnp.bfloat16
DIMS = {
    "NN": (((1,), (0,)), ((), ())),
    "NT": (((1,), (1,)), ((), ())),
    "TN": (((0,), (0,)), ((), ())),
}


def product(left, right, mode):
    return lax.dot_general(left, right, DIMS[mode], preferred_element_type=F32)


def params():
    return pltpu.CompilerParams(vmem_limit_bytes=56 << 20)


def cost(lag):
    return pl.CostEstimate(flops=int(lag * 1e9), bytes_accessed=0, transcendentals=0)


def tile_of(width, most):
    best = 128
    for size in range(128, most + 1, 128):
        if width % size == 0:
            best = size
    return best


def call(kernel, ids, grid, in_specs, out_specs, out_shape, args, name, scratch=(), after=(), kept=(), lag=0.05):
    count = len(args)
    unread = tuple(kept) + tuple(after)

    def run(ids_ref, *refs):
        kernel(ids_ref, *refs[:count], *refs[count + len(unread) :])

    return pl.pallas_call(
        run,
        grid_spec=pltpu.PrefetchScalarGridSpec(
            num_scalar_prefetch=1,
            grid=grid,
            in_specs=list(in_specs) + [pl.BlockSpec(memory_space=pl.ANY)] * len(unread),
            out_specs=out_specs,
            scratch_shapes=list(scratch),
        ),
        out_shape=out_shape,
        input_output_aliases={1 + count + k: k for k in range(len(kept))},
        compiler_params=params(),
        cost_estimate=cost(lag),
        name=name,
    )(ids, *args, *unread)


def group(pieces, unit):
    blocks, filled = [], unit
    for number, piece in enumerate(pieces):
        if filled == unit:
            blocks.append([])
            filled = 0
        blocks[-1].append((number, filled))
        filled += piece.shape[0]
    return blocks


def norm_kernel(ids, pieces, vectors, unit, start, total, kept=(), after=(), lag=0.05):
    width = pieces[0].shape[1]
    blocks = group(pieces, unit)

    def kernel(ids_ref, *refs):
        vec = refs[len(pieces)]
        first_ref, second_ref = refs[len(pieces) + 1 :]
        for step, block in enumerate(blocks):

            @pl.when(pl.program_id(0) == step)
            def _(block=block):
                for number, row in block:
                    rows = slice(row, row + pieces[number].shape[0])
                    data = refs[number][...].astype(F32)
                    centre = data - jnp.mean(data, axis=-1, keepdims=True)
                    spread = jnp.mean(centre * centre, axis=-1, keepdims=True)
                    scaled = centre * lax.rsqrt(spread + EPSILON)
                    first_ref[rows, :] = (scaled * vec[0:1, :] + vec[1:2, :]).astype(BF16)
                    second_ref[rows, :] = (scaled * vec[2:3, :] + vec[3:4, :]).astype(BF16)

    out = pl.BlockSpec((unit, width), lambda i, ids: (start + i, 0))
    shape = jax.ShapeDtypeStruct((total * unit, width), BF16)
    return call(
        kernel,
        ids,
        (len(blocks),),
        [pl.BlockSpec(array.shape, lambda i, ids: (0, 0)) for array in (*pieces, vectors)],
        [out, out],
        [shape, shape],
        (*pieces, vectors),
        kept=kept,
        after=after,
        lag=lag,
        name="norm",
    )


def rotate(block, table, sign):
    cos, sin_low, sin_high = table[:, :128], table[:, 128:256], table[:, 256:]
    lead = block[:, :128]
    turned = (
        lead * cos
        + sign * (pltpu.roll(lead, 96, 1) * sin_low + pltpu.roll(lead, 32, 1) * sin_high)
    )
    return jnp.concatenate([turned, block[:, 128:]], axis=1)


def mixed_kernel(ids, first, weight, place, bias, tables, blocks, after=(), lag=0.05):
    rows, depth = first.shape
    heads = bias.shape[1] // (3 * HEAD_DIM)
    unit = rows // blocks
    wide = 3 * HEAD_DIM

    def kernel(ids_ref, a_ref, w_ref, b_ref, low_ref, high_ref, out_ref):
        for part in range(3):
            here = slice(part * HEAD_DIM, (part + 1) * HEAD_DIM)
            value = product(a_ref[...], w_ref[:, here], "NN") + b_ref[:, here]
            if part < 2:
                value = rotate(value, jnp.concatenate([low_ref[...], high_ref[...]], axis=0), 1.0)
            out_ref[:, here] = value.astype(BF16)

    def table(block):
        return pl.BlockSpec((unit, 3 * 128), lambda j, i, ids: (ids[0] ^ (2 * i + block), 0))

    return call(
        kernel,
        ids,
        (heads, blocks // 2),
        [
            pl.BlockSpec((2 * unit, depth), lambda j, i, ids: (i, 0)),
            pl.BlockSpec((pl.Element(depth), pl.Element(wide)), lambda j, i, ids: (0, pl.multiple_of(place + wide * j, 128))),
            pl.BlockSpec((1, wide), lambda j, i, ids: (0, j)),
            table(0),
            table(1),
        ],
        pl.BlockSpec((2 * unit, wide), lambda j, i, ids: (i, j)),
        jax.ShapeDtypeStruct((rows, heads * wide), BF16),
        (first, weight, bias, tables, tables),
        after=after,
        lag=lag,
        name="mixed",
    )


def attend_kernel(ids, mixed, blocks, after=(), lag=0.05):
    rows, width = mixed.shape
    heads = width // (3 * HEAD_DIM)
    unit = rows // blocks
    lanes = range(0, unit, 128)
    scale = HEAD_DIM ** (-0.5)

    def kernel(ids_ref, x_ref, ctx_ref, lse_ref):
        me = ids_ref[0]

        def place(block):
            return pl.ds(pl.multiple_of((me ^ block) * unit, unit), unit)

        def head_of(block, head):
            at = 3 * HEAD_DIM * head
            query = x_ref[place(block), at : at + HEAD_DIM] * jnp.asarray(scale, BF16)
            tiles = []
            for other in range(block + 1):
                scores = product(query, x_ref[place(other), at + HEAD_DIM : at + 2 * HEAD_DIM], "NT")
                if other == block:
                    row_at = lax.broadcasted_iota(jnp.int32, scores.shape, 0)
                    col_at = lax.broadcasted_iota(jnp.int32, scores.shape, 1)
                    scores = jnp.where(col_at <= row_at, scores, BIG)
                tiles.append(scores)
            top = None
            for scores in tiles:
                for lane in lanes:
                    piece = scores[:, lane : lane + 128]
                    top = piece if top is None else jnp.maximum(top, piece)
            top = jnp.max(top, axis=1, keepdims=True)
            total = acc = None
            for other, scores in enumerate(tiles):
                weight = jnp.exp(scores - top)
                for lane in lanes:
                    piece = weight[:, lane : lane + 128]
                    total = piece if total is None else total + piece
                value = x_ref[place(other), at + 2 * HEAD_DIM : at + 3 * HEAD_DIM]
                made = product(weight.astype(BF16), value, "NN")
                acc = made if acc is None else acc + made
            total = jnp.sum(total, axis=1, keepdims=True)
            ctx_ref[:, HEAD_DIM * head : HEAD_DIM * (head + 1)] = (acc / total).astype(BF16)
            log_total = jnp.broadcast_to(top + jnp.log(total), (unit, 128))
            lse_ref[head, 0] = jnp.transpose(log_total)[:8]

        for block in range(blocks):

            @pl.when(pl.program_id(0) == block)
            def _(block=block):
                for head in range(heads):
                    head_of(block, head)

    return call(
        kernel,
        ids,
        (blocks,),
        [pl.BlockSpec((rows, width), lambda b, ids: (0, 0))],
        [
            pl.BlockSpec((unit, heads * HEAD_DIM), lambda b, ids: (ids[0] ^ b, 0)),
            pl.BlockSpec((heads, 1, 8, unit), lambda b, ids: (0, b, 0, 0)),
        ],
        [
            jax.ShapeDtypeStruct((rows, heads * HEAD_DIM), BF16),
            jax.ShapeDtypeStruct((heads, blocks, 8, unit), F32),
        ],
        (mixed,),
        after=after,
        lag=lag,
        name="attend",
    )


def attend_back_kernel(ids, mixed, grad, context, lse, tables, blocks, after=(), lag=0.05):
    rows, width = mixed.shape
    heads = width // (3 * HEAD_DIM)
    unit = rows // blocks
    scale = HEAD_DIM ** (-0.5)

    def kernel(ids_ref, x_ref, g_ref, c_ref, lse_ref, t_ref, out_ref, sum_ref, dk_s, dv_s):
        me = ids_ref[0]

        def place(block):
            return pl.ds(pl.multiple_of((me ^ block) * unit, unit), unit)

        def head_of(block, head):
            at = 3 * HEAD_DIM * head
            cols = slice(HEAD_DIM * head, HEAD_DIM * (head + 1))
            query = x_ref[place(block), at : at + HEAD_DIM] * jnp.asarray(scale, BF16)
            seed = g_ref[place(block), cols]
            inner = jnp.sum(seed.astype(F32) * c_ref[place(block), cols].astype(F32), axis=1, keepdims=True)
            inner = jnp.transpose(jnp.broadcast_to(inner, (unit, 128)))[:1]
            log_total = lse_ref[head, 0][:1]
            dquery = None
            for other in reversed(range(block + 1)):
                key = x_ref[place(other), at + HEAD_DIM : at + 2 * HEAD_DIM]
                value = x_ref[place(other), at + 2 * HEAD_DIM : at + 3 * HEAD_DIM]
                prob = jnp.exp(product(key, query, "NT") - log_total)
                if other == block:
                    key_at = lax.broadcasted_iota(jnp.int32, prob.shape, 0)
                    row_at = lax.broadcasted_iota(jnp.int32, prob.shape, 1)
                    prob = jnp.where(key_at <= row_at, prob, 0.0)
                dscore = (prob * (product(value, seed, "NT") - inner)).astype(BF16)
                dvalue = product(prob.astype(BF16), seed, "NN")
                dkey = product(dscore, query, "NN")
                if block < blocks - 1:
                    dvalue = dvalue + dv_s[head, other]
                    dkey = dkey + dk_s[head, other]
                if other < block:
                    dv_s[head, other] = dvalue
                    dk_s[head, other] = dkey
                else:
                    done = (dkey, dvalue)
                made = product(dscore, key, "TN")
                dquery = made if dquery is None else dquery + made
            dquery = rotate(dquery * scale, t_ref[...], -1.0)
            dkey = rotate(done[0], t_ref[...], -1.0)
            for part, value in enumerate((dquery, dkey, done[1])):
                cols = slice(at + part * HEAD_DIM, at + (part + 1) * HEAD_DIM)
                rounded = value.astype(BF16)
                out_ref[:, cols] = rounded
                column = jnp.sum(rounded.astype(F32), axis=0, keepdims=True)
                if block < blocks - 1:
                    column = column + sum_ref[:, cols]
                sum_ref[:, cols] = column

        for turn in range(blocks):

            @pl.when(pl.program_id(0) == turn)
            def _(turn=turn):
                for head in range(heads):
                    head_of(blocks - 1 - turn, head)

    def whole(cols):
        return pl.BlockSpec((rows, cols), lambda b, ids: (0, 0))

    table = pl.BlockSpec((unit, 3 * 128), lambda b, ids: (blocks - 1 - b, 0))
    return call(
        kernel,
        ids,
        (blocks,),
        [
            whole(width),
            whole(heads * HEAD_DIM),
            whole(heads * HEAD_DIM),
            pl.BlockSpec((heads, 1, 8, unit), lambda b, ids: (0, blocks - 1 - b, 0, 0)),
            table,
        ],
        [
            pl.BlockSpec((unit, width), lambda b, ids: (ids[0] ^ (blocks - 1 - b), 0)),
            pl.BlockSpec((1, width), lambda b, ids: (0, 0)),
        ],
        [jax.ShapeDtypeStruct((rows, width), BF16), jax.ShapeDtypeStruct((1, width), F32)],
        (mixed, grad, context, lse, tables),
        scratch=[
            pltpu.VMEM((heads, blocks, unit, HEAD_DIM), F32),
            pltpu.VMEM((heads, blocks, unit, HEAD_DIM), F32),
        ],
        after=after,
        lag=lag,
        name="attend_back",
    )


def expand_kernel(ids, second, weight, bias, after=(), lag=0.05):
    rows, depth = second.shape
    width = bias.shape[1]
    tall, wide = tile_of(rows, 1024), tile_of(width, 1024)
    unit = tile_of(wide, 512)

    def kernel(ids_ref, a_ref, w_ref, b_ref, hidden_ref, slope_ref):
        for part in range(wide // unit):
            here = slice(part * unit, (part + 1) * unit)
            pre = product(a_ref[...], w_ref[:, here], "NN") + b_ref[:, here]
            phi = 0.5 + 0.5 * lax.erf(pre * 0.7071067811865476)
            hidden_ref[:, here] = (pre * phi).astype(BF16)
            slope = phi + pre * (jnp.exp(-0.5 * pre * pre) * 0.3989422804014327)
            slope_ref[:, here] = slope.astype(BF16)

    out = pl.BlockSpec((tall, wide), lambda i, j, ids: (i, j))
    shape = jax.ShapeDtypeStruct((rows, width), BF16)
    return call(
        kernel,
        ids,
        (rows // tall, width // wide),
        [
            pl.BlockSpec((tall, depth), lambda i, j, ids: (i, 0)),
            pl.BlockSpec((depth, wide), lambda i, j, ids: (0, j)),
            pl.BlockSpec((1, wide), lambda i, j, ids: (0, j)),
        ],
        [out, out],
        [shape, shape],
        (second, weight, bias),
        after=after,
        lag=lag,
        name="expand",
    )


def stack_kernel(ids, pieces, unit, after=(), lag=0.05):
    width = pieces[0].shape[1]
    blocks = group(pieces, unit)

    def kernel(ids_ref, *refs):
        for step, block in enumerate(blocks):

            @pl.when(pl.program_id(0) == step)
            def _(block=block):
                for number, row in block:
                    refs[-1][row : row + pieces[number].shape[0], :] = refs[number][...]

    return call(
        kernel,
        ids,
        (len(blocks),),
        [pl.BlockSpec(piece.shape, lambda i, ids: (0, 0)) for piece in pieces],
        pl.BlockSpec((unit, width), lambda i, ids: (i, 0)),
        jax.ShapeDtypeStruct((len(blocks) * unit, width), BF16),
        tuple(pieces),
        after=after,
        lag=lag,
        name="stack",
    )


def shrink_back_kernel(ids, seed, weight, slope, after=(), lag=0.05):
    rows, depth = seed.shape
    width = slope.shape[1]
    tall, wide = tile_of(rows, 1024), tile_of(width, 1024)
    unit = tile_of(wide, 512)

    def kernel(ids_ref, a_ref, w_ref, s_ref, out_ref, sum_ref):
        @pl.when(pl.program_id(1) == 0)
        def _():
            sum_ref[...] = jnp.zeros_like(sum_ref)

        for part in range(wide // unit):
            here = slice(part * unit, (part + 1) * unit)
            grad = product(a_ref[...], w_ref[here, :], "NT") * s_ref[:, here].astype(F32)
            rounded = grad.astype(BF16)
            out_ref[:, here] = rounded
            sum_ref[:, here] += jnp.sum(rounded.astype(F32), axis=0, keepdims=True)

    tile = pl.BlockSpec((tall, wide), lambda j, i, ids: (i, j))
    return call(
        kernel,
        ids,
        (width // wide, rows // tall),
        [
            pl.BlockSpec((tall, depth), lambda j, i, ids: (i, 0)),
            pl.BlockSpec((wide, depth), lambda j, i, ids: (j, 0)),
            tile,
        ],
        [tile, pl.BlockSpec((1, wide), lambda j, i, ids: (0, j))],
        [jax.ShapeDtypeStruct((rows, width), BF16), jax.ShapeDtypeStruct((1, width), F32)],
        (seed, weight, slope),
        after=after,
        lag=lag,
        name="shrink_back",
    )


def plain_kernel(ids, left, right, place, width, after=(), lag=0.05):
    rows, depth = left.shape
    tall = tile_of(rows, 1024)

    def kernel(ids_ref, a_ref, b_ref, out_ref):
        out_ref[...] = product(a_ref[...], b_ref[...], "NT").astype(BF16)

    return call(
        kernel,
        ids,
        (rows // tall,),
        [
            pl.BlockSpec((tall, depth), lambda i, ids: (i, 0)),
            pl.BlockSpec((width, depth), lambda i, ids: (place // width, 0)),
        ],
        pl.BlockSpec((tall, width), lambda i, ids: (i, 0)),
        jax.ShapeDtypeStruct((rows, width), BF16),
        (left, right),
        after=after,
        lag=lag,
        name="plain",
    )


def branches_kernel(ids, context, hidden, weight, blocks, after=(), lag=0.05):
    rows, deep_b = hidden.shape
    depth, deep_a = weight.shape[1], context.shape[1]
    tall, wide = rows // blocks, tile_of(depth, 1024)
    unit = tile_of(wide, 512)

    def kernel(ids_ref, a_ref, m_ref, h_ref, s_ref, *out_refs):
        for block in range(0, blocks, 2):

            @pl.when(pl.program_id(1) == block // 2)
            def _(block=block):
                for part in range(wide // unit):
                    here = slice(part * unit, (part + 1) * unit)
                    value = product(h_ref[...], s_ref[:, here], "NN")
                    value = value + product(a_ref[...], m_ref[:, here], "NN")
                    out_refs[block][:, here] = value[:tall].astype(BF16)
                    out_refs[block + 1][:, here] = value[tall:].astype(BF16)

    return call(
        kernel,
        ids,
        (depth // wide, blocks // 2),
        [
            pl.BlockSpec((2 * tall, deep_a), lambda j, i, ids: (i, 0)),
            pl.BlockSpec((deep_a, wide), lambda j, i, ids: (deep_b // deep_a, j)),
            pl.BlockSpec((2 * tall, deep_b), lambda j, i, ids: (i, 0)),
            pl.BlockSpec((deep_b, wide), lambda j, i, ids: (0, j)),
        ],
        [pl.BlockSpec((tall, wide), lambda j, i, ids: (0, j))] * blocks,
        [jax.ShapeDtypeStruct((tall, depth), BF16)] * blocks,
        (context, weight, hidden, weight),
        after=after,
        lag=lag,
        name="branches",
    )


def back_kernel(ids, left_a, left_b, right, scales, start, count, blocks, after=(), lag=0.05):
    rows = left_a.shape[0] // blocks
    width = right.shape[0]
    deep_a, deep_b = left_a.shape[1], left_b.shape[1]
    wide = tile_of(width, 512 if count == 1 else 1024)
    unit = tile_of(wide, 512)

    def kernel(ids_ref, a_ref, b_ref, c_ref, d_ref, s_ref, *out_refs):
        for block, out_ref in enumerate(out_refs):

            @pl.when(pl.program_id(1) == block)
            def _(out_ref=out_ref):
                for part in range(wide // unit):
                    here = slice(part * unit, (part + 1) * unit)
                    one = product(a_ref[...], b_ref[here, :], "NT") * s_ref[0:1, here]
                    two = product(c_ref[...], d_ref[here, :], "NT") * s_ref[1:2, here]
                    out_ref[:, here] = (one + two).astype(BF16)

    return call(
        kernel,
        ids,
        (width // wide, count),
        [
            pl.BlockSpec((rows, deep_a), lambda j, i, ids: (start + i, 0)),
            pl.BlockSpec((pl.Element(wide), pl.Element(deep_a)), lambda j, i, ids: (j * wide, deep_b)),
            pl.BlockSpec((rows, deep_b), lambda j, i, ids: (start + i, 0)),
            pl.BlockSpec((wide, deep_b), lambda j, i, ids: (j, 0)),
            pl.BlockSpec((2, wide), lambda j, i, ids: (0, j)),
        ],
        [pl.BlockSpec((rows, wide), lambda j, i, ids: (0, j))] * count,
        [jax.ShapeDtypeStruct((rows, width), BF16)] * count,
        (left_a, right, left_b, right, scales),
        after=after,
        lag=lag,
        name="back",
    )


def piece_grad_kernel(ids, left, pieces, after=(), lag=0.05):
    rows, width = left.shape
    unit, depth = pieces[0].shape
    tall, wide = tile_of(width, 1024), tile_of(depth, 1024)
    cut = tile_of(wide, 512)

    def kernel(ids_ref, a_ref, *refs):
        grad_ref, right_ref = refs[len(pieces) :]
        for part in range(wide // cut):
            here = slice(part * cut, (part + 1) * cut)
            total = None
            for number in range(len(pieces)):
                made = product(a_ref[number * unit : (number + 1) * unit, :], refs[number][:, here], "TN")
                total = made if total is None else total + made
            grad_ref[:, here] = total.astype(BF16)

        @pl.when(pl.program_id(1) == 0)
        def _():
            for number in range(len(pieces)):
                right_ref[number * unit : (number + 1) * unit, :] = refs[number][...]

    return call(
        kernel,
        ids,
        (depth // wide, width // tall),
        [pl.BlockSpec((rows, tall), lambda j, i, ids: (0, i))]
        + [pl.BlockSpec((unit, wide), lambda j, i, ids: (0, j))] * len(pieces),
        [
            pl.BlockSpec((tall, wide), lambda j, i, ids: (i, j)),
            pl.BlockSpec((rows, wide), lambda j, i, ids: (0, j)),
        ],
        [jax.ShapeDtypeStruct((width, depth), BF16), jax.ShapeDtypeStruct((rows, depth), BF16)],
        (left, *pieces),
        after=after,
        lag=lag,
        name="piece_grad",
    )


def full_grad_kernel(ids, left, right, weight=None, total=None, place=0, spare=0, start=0, span=0, kept=(), after=(), lag=0.05):
    rows, depth = left.shape
    width = right.shape[1]
    tall, wide = (tile_of(depth, 512), width) if span else (tile_of(depth, 1024), tile_of(width, 1024))
    unit = tile_of(wide, 512)
    summed = weight is not None

    def kernel(ids_ref, a_ref, b_ref, *refs):
        out_ref = refs[2 if summed else 0]
        if summed:

            @pl.when(pl.program_id(1) == 0)
            def _():
                refs[3][...] = jnp.zeros_like(refs[3])
                refs[4][...] = jnp.zeros_like(refs[4])

        for part in range(wide // unit):
            here = slice(part * unit, (part + 1) * unit)
            value = product(a_ref[...], b_ref[:, here], "TN")
            out_ref[:, here] = value.astype(BF16)
            if summed:
                held = refs[0][:, here].astype(F32)
                one, two = held * value, held * refs[1][:, here]
                refs[3][...] += sum(one[:, lane : lane + 128] for lane in range(0, unit, 128))
                refs[4][...] += sum(two[:, lane : lane + 128] for lane in range(0, unit, 128))

    tile = pl.BlockSpec((tall, wide), lambda i, j, ids: (i, j))
    in_specs = [
        pl.BlockSpec((rows, tall), lambda i, j, ids: (0, i)),
        pl.BlockSpec((rows, wide), lambda i, j, ids: (0, j)),
    ]
    out_specs = [pl.BlockSpec((tall, wide), lambda i, j, ids: (i, start // wide + j))]
    out_shape = [jax.ShapeDtypeStruct((depth, span or width + spare), BF16)]
    args = (left, right)
    if summed:
        args += (weight, total)
        in_specs += [
            pl.BlockSpec((pl.Element(tall), pl.Element(wide)), lambda i, j, ids: (i * tall, pl.multiple_of(place + j * wide, 128))),
            pl.BlockSpec((1, wide), lambda i, j, ids: (0, j)),
        ]
        out_specs += [pl.BlockSpec((tall, 128), lambda i, j, ids: (i, 0))] * 2
        out_shape += [jax.ShapeDtypeStruct((depth, 128), F32)] * 2
    return call(
        kernel,
        ids,
        (depth // tall, width // wide),
        in_specs,
        out_specs,
        out_shape,
        args,
        kept=kept,
        after=after,
        lag=lag,
        name="full_grad",
    )


def sums_kernel(ids, wide, rows, after=(), lag=0.05):
    depth = rows.shape[1]
    count = len(wide)

    def kernel(ids_ref, *refs):
        total = refs[count][...]
        for number, ref in enumerate(refs[:count]):
            row = lax.broadcasted_iota(jnp.int32, (8, 128), 0)
            pick = jnp.where(row == number, 1.0, 0.0).astype(BF16)
            high = ref[...].astype(BF16)
            rest = (ref[...] - high.astype(F32)).astype(BF16)
            total = total + product(pick, high, "NT") + product(pick, rest, "NT")
        refs[-1][...] = total

    def whole(shape):
        return pl.BlockSpec(shape, lambda i, ids: (0, 0))

    return call(
        kernel,
        ids,
        (1,),
        [whole((depth, 128))] * count + [whole((8, depth))],
        whole((8, depth)),
        jax.ShapeDtypeStruct((8, depth), F32),
        (*wide, rows),
        after=after,
        lag=lag,
        name="sums",
    )


def spare_kernel(ids, kept, parts, slots, after=(), lag=0.05):
    depth = kept.shape[0]

    def kernel(ids_ref, *refs):
        total = refs[0][...]
        for ref in refs[1:-1]:
            total = total + ref[...]
        rounded = total.astype(BF16).astype(F32)
        row = lax.broadcasted_iota(jnp.int32, (128, depth), 0)
        value = jnp.zeros((128, depth), F32)
        for number in range(SUMS):
            place = number * slots + ids_ref[1]
            value = jnp.where(row == place, rounded[number : number + 1], value)
            if SUMS * slots <= 64:
                value = jnp.where(row == place + 64, (total - rounded)[number : number + 1], value)
        refs[-1][...] = jnp.transpose(value).astype(BF16)

    return call(
        kernel,
        ids,
        (1,),
        [pl.BlockSpec((8, depth), lambda i, ids: (0, 0))] * len(parts),
        [pl.BlockSpec((depth, 128), lambda i, ids: (0, kept.shape[1] // 128 - 1))],
        [jax.ShapeDtypeStruct(kept.shape, BF16)],
        tuple(parts),
        kept=(kept,),
        after=after,
        lag=lag,
        name="spare",
    )[0]


def output_kernel(ids, rows, parts, vectors, after=(), lag=0.05):
    count, width = rows.shape

    def kernel(ids_ref, x_ref, vec, *refs):
        total = refs[0][...].astype(F32)
        for ref in refs[1:-1]:
            total = total + ref[...].astype(F32)
        refs[-1][...] = (x_ref[...].astype(F32) + total + (vec[4:5, :] + vec[5:6, :])).astype(BF16)

    unit = tile_of(count, 256)
    tile = pl.BlockSpec((unit, width), lambda i, ids: (i, 0))
    return call(
        kernel,
        ids,
        (count // unit,),
        [tile, pl.BlockSpec(vectors.shape, lambda i, ids: (0, 0))] + [tile] * len(parts),
        tile,
        jax.ShapeDtypeStruct((count, width), BF16),
        (rows, vectors, *parts),
        after=after,
        lag=lag,
        name="output",
    )


def widen_kernel(ids, rows, widths, after=(), lag=0.05):
    count = rows.shape[0]
    specs, shapes, place = [], [], 0
    for width in widths:
        specs.append(pl.BlockSpec((pl.Element(count), pl.Element(width)), lambda i, ids, place=place: (0, place)))
        shapes.append(jax.ShapeDtypeStruct((count, width), F32))
        place += width

    def kernel(ids_ref, *refs):
        for in_ref, out_ref in zip(refs[: len(specs)], refs[len(specs) :]):
            out_ref[...] = in_ref[...].astype(F32)

    return call(
        kernel,
        ids,
        (1,),
        specs,
        [pl.BlockSpec(shape.shape, lambda i, ids: (0, 0)) for shape in shapes],
        shapes,
        (rows,) * len(specs),
        after=after,
        lag=lag,
        name="widen",
    )


def finish_kernel(ids, rows, widths, heads, slots, scales, last, after=(), lag=0.05):
    count = rows.shape[0]
    one, two = widths
    each = one // heads

    def kernel(ids_ref, in_ref, v_ref, one_ref, two_ref, *sum_refs):
        for head in range(heads):
            one_ref[:, head, :] = in_ref[:, head * each : (head + 1) * each].astype(F32)
        two_ref[...] = jnp.transpose(in_ref[:, one : one + two].astype(F32))
        number = lax.broadcasted_iota(jnp.int32, (8, 128), 0)
        lane = lax.broadcasted_iota(jnp.int32, (8, 128), 1)
        if SUMS * slots <= 64:
            lane = lane % 64
        mine = (lane // slots == number) & (number < SUMS)
        sums = product(jnp.where(mine, 1.0, 0.0).astype(BF16), in_ref[:, one + two :], "NT")
        for number, sum_ref in zip((0, 1, 2, 3, 4, 4, 5, 6), sum_refs):
            value = sums[number : number + 1]
            if number in (0, 2):
                value = (value - v_ref[number + 1 : number + 2, :] * sums[number + 1 : number + 2]) / v_ref[number : number + 1, :]
            wide = sum_ref.shape[1]
            for row in range(sum_ref.shape[0]):
                sum_ref[row : row + 1, :] = value[:, row * wide : (row + 1) * wide]

    def whole(shape):
        return pl.BlockSpec(shape, lambda i, ids: (0,) * len(shape))

    shapes = [(count, heads, each), (two, count)] + [(1, count)] * 6 + last
    return call(
        kernel,
        ids,
        (1,),
        [whole(rows.shape), whole(scales.shape)],
        [whole(shape) for shape in shapes],
        [jax.ShapeDtypeStruct(shape, F32) for shape in shapes],
        (rows, scales),
        after=after,
        lag=lag,
        name="finish",
    )


def total_kernel(ids, parts, after=(), lag=0.05):
    rows, width = parts[0].shape

    def kernel(ids_ref, *refs):
        total = refs[0][...].astype(F32)
        for ref in refs[1:-1]:
            total = total + ref[...].astype(F32)
        refs[-1][...] = total

    unit = min(rows, 256)
    tile = pl.BlockSpec((unit, width), lambda i, ids: (i, 0))
    return call(
        kernel,
        ids,
        (rows // unit,),
        [tile] * len(parts),
        tile,
        jax.ShapeDtypeStruct((rows, width), F32),
        tuple(parts),
        after=after,
        lag=lag,
        name="total",
    )


def input_kernel(ids, rows, seed, parts, after=(), lag=0.05):
    count, width = rows.shape

    def kernel(ids_ref, x_ref, g_ref, *refs):
        back = refs[0][...].astype(F32)
        for ref in refs[1:-1]:
            back = back + ref[...].astype(F32)
        data = x_ref[...].astype(F32)
        centre = data - jnp.mean(data, axis=-1, keepdims=True)
        rstd = lax.rsqrt(jnp.mean(centre * centre, axis=-1, keepdims=True) + EPSILON)
        scaled = centre * rstd
        inner = jnp.mean(back * scaled, axis=-1, keepdims=True)
        back = back - jnp.mean(back, axis=-1, keepdims=True) - scaled * inner
        refs[-1][...] = g_ref[...].astype(F32) + rstd * back

    unit = tile_of(count, 256)
    tile = pl.BlockSpec((unit, width), lambda i, ids: (i, 0))
    return call(
        kernel,
        ids,
        (count // unit,),
        [tile] * (2 + len(parts)),
        tile,
        jax.ShapeDtypeStruct((count, width), F32),
        (rows, seed, *parts),
        after=after,
        lag=lag,
        name="input",
    )


def rotary_tables(length):
    position = jnp.arange(length, dtype=F32)[:, None]
    lane = jnp.arange(128)
    half = ROTARY // 2
    frequency = 10000.0 ** (-2.0 * (lane % half).astype(F32) / ROTARY)
    angles = position * frequency[None, :]
    sine = jnp.sin(angles)
    tables = (
        jnp.where(lane < ROTARY, jnp.cos(angles), 1.0),
        jnp.where(lane < half, -sine, 0.0),
        jnp.where((lane >= half) & (lane < ROTARY), sine, 0.0),
    )
    return jnp.concatenate(tables, axis=1)


def flip(value, axis, bit, size):
    return lax.ppermute(value, axis, [(i, i ^ bit) for i in range(size)])


def sum_over(value, axis, size):
    bit = 1
    while bit < size:
        value = value + flip(value, axis, bit, size)
        bit *= 2
    return value


def half_kernel(ids, rows, number, after=(), lag=0.05):
    count, width = rows.shape[0] // 2, rows.shape[1]

    def kernel(ids_ref, in_ref, out_ref):
        out_ref[...] = in_ref[...]

    return call(
        kernel,
        ids,
        (1,),
        [pl.BlockSpec((count, width), lambda i, ids: (number, 0))],
        pl.BlockSpec((count, width), lambda i, ids: (0, 0)),
        jax.ShapeDtypeStruct((count, width), BF16),
        (rows,),
        after=after,
        lag=lag,
        name="half",
    )


def gather_rows(ids, rows, size, after=()):
    if size != 4:
        return [rows] + [flip(rows, "tensor", k, size) for k in range(1, size)]
    one = flip(rows, "tensor", 1, size)
    two = flip(rows, "tensor", 2, size)
    upper = flip(half_kernel(ids, two, 0, after), "tensor", 1, size)
    lower = flip(half_kernel(ids, one, 1, after), "tensor", 2, size)
    return [rows, one, two, upper, lower]


def body(
    layer_input,
    cotangent,
    firstgain,
    firstbias,
    secondgain,
    secondbias,
    project,
    projbias,
    merging,
    mergebias,
    expand,
    expandbias,
    shrink,
    shrinkbias,
):
    n_dp, n_tensor = lax.axis_size("dp"), lax.axis_size("tensor")
    dp_at, tensor_at = lax.axis_index("dp"), lax.axis_index("tensor")
    assert SUMS * n_dp <= 128
    ids = jnp.stack([tensor_at, dp_at]).astype(jnp.int32)
    own_count, width = layer_input.shape
    group_count = own_count * n_tensor
    assert group_count == LENGTH
    depth = width // n_dp
    heads = project.shape[1]
    mixed_width = heads * 3 * HEAD_DIM
    hidden_width = expand.shape[1]

    packed = jnp.concatenate(
        [firstgain, firstbias, secondgain, secondbias, mergebias, shrinkbias, expandbias, projbias.reshape(-1)]
    )
    slots = jnp.where(jnp.arange(n_dp)[:, None] == dp_at, packed[None, :], jnp.zeros((), BF16))
    slots = sum_over(slots, "dp", n_dp).astype(F32)
    vectors = jnp.transpose(slots[:, : 6 * depth].reshape(n_dp, 6, depth), (1, 0, 2)).reshape(6, width)
    at = 6 * depth
    part = hidden_width // n_dp
    b_expand = slots[:, at : at + part].reshape(1, hidden_width)
    at += part
    b_project = jnp.transpose(slots[:, at:].reshape(n_dp, heads, -1), (1, 0, 2)).reshape(1, mixed_width)

    tables = rotary_tables(LENGTH)
    own_project = project.reshape(depth, mixed_width)
    w_in = lax.all_gather(jnp.concatenate([expand, own_project], axis=1), "dp", axis=0, tiled=True)
    w_out = lax.all_gather(jnp.concatenate([shrink, merging], axis=0), "dp", axis=1, tiled=True)

    unit = own_count
    rows_pieces = gather_rows(ids, layer_input, n_tensor, (vectors, tables))
    near, far = (rows_pieces[:-1], rows_pieces[-1:]) if n_tensor != 4 else (rows_pieces[:3], rows_pieces[3:])
    pair = norm_kernel(ids, near, vectors, unit, 0, n_tensor)
    later = stack_kernel(ids, [cotangent], unit, after=(pair[0], *far))
    seed_pieces = [later] + [flip(later, "tensor", k, n_tensor) for k in range(n_tensor - 1, 0, -1)]
    first, second = norm_kernel(ids, far, vectors, unit, n_tensor - 1, n_tensor, kept=pair, after=(later,))
    hidden, slope = expand_kernel(ids, second, w_in, b_expand)
    mixed = mixed_kernel(ids, first, w_in, hidden_width, b_project, tables, n_tensor, after=(hidden,))
    shrink_part, seed = piece_grad_kernel(ids, hidden, seed_pieces[:1] + seed_pieces[:0:-1], after=(mixed,))
    shrink_grad = lax.psum_scatter(shrink_part, "dp", scatter_dimension=1, tiled=True)
    context, lse = attend_kernel(ids, mixed, n_tensor, after=(shrink_part,))
    merge_width = merging.shape[0]
    joint = mixed_width + merge_width + 128
    part = full_grad_kernel(ids, seed, context, start=mixed_width, span=joint)
    branches = branches_kernel(ids, context, hidden, w_out, n_tensor, after=part)
    summed = [branches[0]] + [flip(branches[k], "tensor", k, n_tensor) for k in range(n_tensor - 1, 0, -1)]
    pgrad, expand_sum = shrink_back_kernel(ids, seed, w_out, slope, after=(branches[0],))
    expand_part, gain_two, bias_two = full_grad_kernel(ids, second, pgrad, w_in, expand_sum)
    expand_grad = lax.psum_scatter(expand_part, "dp", scatter_dimension=0, tiled=True)
    cgrad = plain_kernel(ids, seed, w_out, hidden_width, merge_width, after=(expand_part,))
    mgrad, mixed_sum = attend_back_kernel(ids, mixed, cgrad, context, lse, tables, n_tensor)
    project_part, gain_one, bias_one = full_grad_kernel(
        ids, first, mgrad, w_in, mixed_sum, place=hidden_width, span=joint, kept=part
    )

    def slots(values):
        return jnp.pad(values, ((0, 0), (0, depth - values.shape[1]))).reshape(1, width)

    seed_sum = jnp.sum(cotangent.astype(F32), axis=0, keepdims=True)
    over_all = jnp.pad(seed_sum, ((4, 3), (0, 0)))
    over_all = sums_kernel(ids, [gain_one, bias_one, gain_two, bias_two], over_all)
    over_dp = [
        slots(expand_sum.reshape(n_dp, -1)),
        slots(jnp.transpose(mixed_sum.reshape(heads, n_dp, -1), (1, 0, 2)).reshape(n_dp, -1)),
    ]
    over_dp = jnp.pad(jnp.concatenate(over_dp, axis=0), ((5, 1), (0, 0)))
    over_tensor = [over_all] + [flip(over_all, "tensor", k, n_tensor) for k in range(n_tensor - 1, 0, -1)]

    gains = jnp.stack([vectors[0], vectors[2]])
    back = []
    last = over_all
    half = n_tensor // 2
    for start, count in ((half + 1, half - 1), (1, half), (0, 1)):
        made = back_kernel(ids, mgrad, pgrad, w_in, gains, start, count, n_tensor, after=(last,))
        back.append([flip(made[k], "tensor", start + k, n_tensor) if start else made[k] for k in range(count - 1, -1, -1)])
        last = made[0]
        if len(back) == 1:
            layer_output = output_kernel(ids, layer_input, summed, vectors, after=(last,), lag=160)
            last = spare_kernel(ids, project_part, over_tensor + [over_dp], n_dp, after=(layer_output,))
            project_grad = lax.psum_scatter(last, "dp", scatter_dimension=0, tiled=True)
            (shrink_grad,) = widen_kernel(ids, shrink_grad, [shrink.shape[1]], after=(last,), lag=0.05)
            last = shrink_grad
    (expand_grad,) = widen_kernel(ids, expand_grad, [hidden_width], after=(last,))
    far = total_kernel(ids, back[0] + back[2], after=(expand_grad,), lag=8)
    input_grad = input_kernel(ids, layer_input, cotangent, back[1] + [far], lag=162)
    scales = jnp.stack([firstgain, firstbias, secondgain, secondbias]).astype(F32)
    project_grad, merging_grad, *sums = finish_kernel(
        ids, project_grad, [mixed_width, merge_width], heads, n_dp, scales, [(1, expandbias.shape[0]), projbias.shape], after=(input_grad,)
    )
    projbias_grad = sums.pop()
    gain_one, bias_one, gain_two, bias_two, seed_sum, seed_sum_again, expandbias_grad = [value[0] for value in sums]
    return (
        layer_output,
        input_grad,
        gain_one,
        bias_one,
        gain_two,
        bias_two,
        project_grad,
        projbias_grad,
        merging_grad,
        seed_sum,
        expand_grad,
        expandbias_grad,
        shrink_grad,
        seed_sum_again,
    )


def solution(mesh):
    specs = (
        P(("dp", "tensor"), None),
        P(("dp", "tensor"), None),
        P("dp"),
        P("dp"),
        P("dp"),
        P("dp"),
        P("dp", "tensor", None),
        P("tensor", "dp"),
        P("tensor", "dp"),
        P("dp"),
        P("dp", "tensor"),
        P(("tensor", "dp")),
        P("tensor", "dp"),
        P("dp"),
    )
    return jax.shard_map(body, mesh=mesh, in_specs=specs, out_specs=specs, check_vma=False)
```

```python
import jax
import jax.numpy as jnp
from jax import lax
from jax.experimental import pallas as pl
from jax.experimental.pallas import tpu as pltpu
from jax.sharding import PartitionSpec as P

HEAD_DIM = 256
ROTARY = 64
LENGTH = 2048
EPSILON = 1e-05
BIG = -1e30
F32 = jnp.float32
BF16 = jnp.bfloat16
DIMS = {
    "NN": (((1,), (0,)), ((), ())),
    "NT": (((1,), (1,)), ((), ())),
    "TN": (((0,), (0,)), ((), ())),
}


def product(left, right, mode):
    return lax.dot_general(left, right, DIMS[mode], preferred_element_type=F32)


def params():
    return pltpu.CompilerParams(vmem_limit_bytes=56 << 20)


def cost(lag):
    return pl.CostEstimate(flops=int(lag * 1e9), bytes_accessed=0, transcendentals=0)


def tile_of(width, most):
    best = 128
    for size in range(128, most + 1, 128):
        if width % size == 0:
            best = size
    return best


def call(kernel, ids, grid, in_specs, out_specs, out_shape, args, name, scratch=(), after=(), kept=(), lag=0.05):
    count = len(args)
    unread = tuple(kept) + tuple(after)

    def run(ids_ref, *refs):
        kernel(ids_ref, *refs[:count], *refs[count + len(unread) :])

    return pl.pallas_call(
        run,
        grid_spec=pltpu.PrefetchScalarGridSpec(
            num_scalar_prefetch=1,
            grid=grid,
            in_specs=list(in_specs) + [pl.BlockSpec(memory_space=pl.ANY)] * len(unread),
            out_specs=out_specs,
            scratch_shapes=list(scratch),
        ),
        out_shape=out_shape,
        input_output_aliases={1 + count + k: k for k in range(len(kept))},
        compiler_params=params(),
        cost_estimate=cost(lag),
        name=name,
    )(ids, *args, *unread)


def group(pieces, unit):
    blocks, filled = [], unit
    for number, piece in enumerate(pieces):
        if filled == unit:
            blocks.append([])
            filled = 0
        blocks[-1].append((number, filled))
        filled += piece.shape[0]
    return blocks


def norm_kernel(ids, pieces, vectors, unit, start, total, kept=(), after=(), lag=0.05):
    width = pieces[0].shape[1]
    blocks = group(pieces, unit)

    def kernel(ids_ref, *refs):
        vec = refs[len(pieces)]
        first_ref, second_ref = refs[len(pieces) + 1 :]
        for step, block in enumerate(blocks):

            @pl.when(pl.program_id(0) == step)
            def _(block=block):
                for number, row in block:
                    rows = slice(row, row + pieces[number].shape[0])
                    data = refs[number][...].astype(F32)
                    centre = data - jnp.mean(data, axis=-1, keepdims=True)
                    spread = jnp.mean(centre * centre, axis=-1, keepdims=True)
                    scaled = centre * lax.rsqrt(spread + EPSILON)
                    first_ref[rows, :] = (scaled * vec[0:1, :] + vec[1:2, :]).astype(BF16)
                    second_ref[rows, :] = (scaled * vec[2:3, :] + vec[3:4, :]).astype(BF16)

    out = pl.BlockSpec((unit, width), lambda i, ids: (start + i, 0))
    shape = jax.ShapeDtypeStruct((total * unit, width), BF16)
    return call(
        kernel,
        ids,
        (len(blocks),),
        [pl.BlockSpec(array.shape, lambda i, ids: (0, 0)) for array in (*pieces, vectors)],
        [out, out],
        [shape, shape],
        (*pieces, vectors),
        kept=kept,
        after=after,
        lag=lag,
        name="norm",
    )


def rotate(block, table, sign):
    cos, sin_low, sin_high = table[:, :128], table[:, 128:256], table[:, 256:]
    lead = block[:, :128]
    turned = (
        lead * cos
        + sign * (pltpu.roll(lead, 96, 1) * sin_low + pltpu.roll(lead, 32, 1) * sin_high)
    )
    return jnp.concatenate([turned, block[:, 128:]], axis=1)


def mixed_kernel(ids, first, weight, place, bias, tables, blocks, after=(), lag=0.05):
    rows, depth = first.shape
    heads = bias.shape[1] // (3 * HEAD_DIM)
    unit = rows // blocks
    wide = 3 * HEAD_DIM

    def kernel(ids_ref, a_ref, w_ref, b_ref, low_ref, high_ref, out_ref):
        for part in range(3):
            here = slice(part * HEAD_DIM, (part + 1) * HEAD_DIM)
            value = product(a_ref[...], w_ref[:, here], "NN") + b_ref[:, here]
            if part < 2:
                value = rotate(value, jnp.concatenate([low_ref[...], high_ref[...]], axis=0), 1.0)
            out_ref[:, here] = value.astype(BF16)

    def table(block):
        return pl.BlockSpec((unit, 3 * 128), lambda j, i, ids: (ids[0] ^ (2 * i + block), 0))

    return call(
        kernel,
        ids,
        (heads, blocks // 2),
        [
            pl.BlockSpec((2 * unit, depth), lambda j, i, ids: (i, 0)),
            pl.BlockSpec((pl.Element(depth), pl.Element(wide)), lambda j, i, ids: (0, pl.multiple_of(place + wide * j, 128))),
            pl.BlockSpec((1, wide), lambda j, i, ids: (0, j)),
            table(0),
            table(1),
        ],
        pl.BlockSpec((2 * unit, wide), lambda j, i, ids: (i, j)),
        jax.ShapeDtypeStruct((rows, heads * wide), BF16),
        (first, weight, bias, tables, tables),
        after=after,
        lag=lag,
        name="mixed",
    )


def attend_kernel(ids, mixed, blocks, after=(), lag=0.05):
    rows, width = mixed.shape
    heads = width // (3 * HEAD_DIM)
    unit = rows // blocks
    lanes = range(0, unit, 128)
    scale = HEAD_DIM ** (-0.5)

    def kernel(ids_ref, x_ref, ctx_ref, lse_ref):
        me = ids_ref[0]

        def place(block):
            return pl.ds(pl.multiple_of((me ^ block) * unit, unit), unit)

        def head_of(block, head):
            at = 3 * HEAD_DIM * head
            query = x_ref[place(block), at : at + HEAD_DIM] * jnp.asarray(scale, BF16)
            tiles = []
            for other in range(block + 1):
                scores = product(query, x_ref[place(other), at + HEAD_DIM : at + 2 * HEAD_DIM], "NT")
                if other == block:
                    row_at = lax.broadcasted_iota(jnp.int32, scores.shape, 0)
                    col_at = lax.broadcasted_iota(jnp.int32, scores.shape, 1)
                    scores = jnp.where(col_at <= row_at, scores, BIG)
                tiles.append(scores)
            top = None
            for scores in tiles:
                for lane in lanes:
                    piece = scores[:, lane : lane + 128]
                    top = piece if top is None else jnp.maximum(top, piece)
            top = jnp.max(top, axis=1, keepdims=True)
            total = acc = None
            for other, scores in enumerate(tiles):
                weight = jnp.exp(scores - top)
                for lane in lanes:
                    piece = weight[:, lane : lane + 128]
                    total = piece if total is None else total + piece
                value = x_ref[place(other), at + 2 * HEAD_DIM : at + 3 * HEAD_DIM]
                made = product(weight.astype(BF16), value, "NN")
                acc = made if acc is None else acc + made
            total = jnp.sum(total, axis=1, keepdims=True)
            ctx_ref[:, HEAD_DIM * head : HEAD_DIM * (head + 1)] = (acc / total).astype(BF16)
            log_total = jnp.broadcast_to(top + jnp.log(total), (unit, 128))
            lse_ref[head, 0] = jnp.transpose(log_total)[:8]

        for block in range(blocks):

            @pl.when(pl.program_id(0) == block)
            def _(block=block):
                for head in range(heads):
                    head_of(block, head)

    return call(
        kernel,
        ids,
        (blocks,),
        [pl.BlockSpec((rows, width), lambda b, ids: (0, 0))],
        [
            pl.BlockSpec((unit, heads * HEAD_DIM), lambda b, ids: (ids[0] ^ b, 0)),
            pl.BlockSpec((heads, 1, 8, unit), lambda b, ids: (0, b, 0, 0)),
        ],
        [
            jax.ShapeDtypeStruct((rows, heads * HEAD_DIM), BF16),
            jax.ShapeDtypeStruct((heads, blocks, 8, unit), F32),
        ],
        (mixed,),
        after=after,
        lag=lag,
        name="attend",
    )


def attend_back_kernel(ids, mixed, grad, context, lse, tables, blocks, after=(), lag=0.05):
    rows, width = mixed.shape
    heads = width // (3 * HEAD_DIM)
    unit = rows // blocks
    scale = HEAD_DIM ** (-0.5)

    def kernel(ids_ref, x_ref, g_ref, c_ref, lse_ref, t_ref, out_ref, sum_ref, dk_s, dv_s):
        me = ids_ref[0]

        def place(block):
            return pl.ds(pl.multiple_of((me ^ block) * unit, unit), unit)

        def head_of(block, head):
            at = 3 * HEAD_DIM * head
            cols = slice(HEAD_DIM * head, HEAD_DIM * (head + 1))
            query = x_ref[place(block), at : at + HEAD_DIM] * jnp.asarray(scale, BF16)
            seed = g_ref[place(block), cols]
            inner = jnp.sum(seed.astype(F32) * c_ref[place(block), cols].astype(F32), axis=1, keepdims=True)
            inner = jnp.transpose(jnp.broadcast_to(inner, (unit, 128)))[:1]
            log_total = lse_ref[head, 0][:1]
            dquery = None
            for other in reversed(range(block + 1)):
                key = x_ref[place(other), at + HEAD_DIM : at + 2 * HEAD_DIM]
                value = x_ref[place(other), at + 2 * HEAD_DIM : at + 3 * HEAD_DIM]
                prob = jnp.exp(product(key, query, "NT") - log_total)
                if other == block:
                    key_at = lax.broadcasted_iota(jnp.int32, prob.shape, 0)
                    row_at = lax.broadcasted_iota(jnp.int32, prob.shape, 1)
                    prob = jnp.where(key_at <= row_at, prob, 0.0)
                dscore = (prob * (product(value, seed, "NT") - inner)).astype(BF16)
                dvalue = product(prob.astype(BF16), seed, "NN")
                dkey = product(dscore, query, "NN")
                if block < blocks - 1:
                    dvalue = dvalue + dv_s[head, other]
                    dkey = dkey + dk_s[head, other]
                if other < block:
                    dv_s[head, other] = dvalue
                    dk_s[head, other] = dkey
                else:
                    done = (dkey, dvalue)
                made = product(dscore, key, "TN")
                dquery = made if dquery is None else dquery + made
            dquery = rotate(dquery * scale, t_ref[...], -1.0)
            dkey = rotate(done[0], t_ref[...], -1.0)
            for part, value in enumerate((dquery, dkey, done[1])):
                cols = slice(at + part * HEAD_DIM, at + (part + 1) * HEAD_DIM)
                rounded = value.astype(BF16)
                out_ref[:, cols] = rounded
                column = jnp.sum(rounded.astype(F32), axis=0, keepdims=True)
                if block < blocks - 1:
                    column = column + sum_ref[:, cols]
                sum_ref[:, cols] = column

        for turn in range(blocks):

            @pl.when(pl.program_id(0) == turn)
            def _(turn=turn):
                for head in range(heads):
                    head_of(blocks - 1 - turn, head)

    def whole(cols):
        return pl.BlockSpec((rows, cols), lambda b, ids: (0, 0))

    table = pl.BlockSpec((unit, 3 * 128), lambda b, ids: (blocks - 1 - b, 0))
    return call(
        kernel,
        ids,
        (blocks,),
        [
            whole(width),
            whole(heads * HEAD_DIM),
            whole(heads * HEAD_DIM),
            pl.BlockSpec((heads, 1, 8, unit), lambda b, ids: (0, blocks - 1 - b, 0, 0)),
            table,
        ],
        [
            pl.BlockSpec((unit, width), lambda b, ids: (ids[0] ^ (blocks - 1 - b), 0)),
            pl.BlockSpec((1, width), lambda b, ids: (0, 0)),
        ],
        [jax.ShapeDtypeStruct((rows, width), BF16), jax.ShapeDtypeStruct((1, width), F32)],
        (mixed, grad, context, lse, tables),
        scratch=[
            pltpu.VMEM((heads, blocks, unit, HEAD_DIM), F32),
            pltpu.VMEM((heads, blocks, unit, HEAD_DIM), F32),
        ],
        after=after,
        lag=lag,
        name="attend_back",
    )


def expand_kernel(ids, second, weight, bias, after=(), lag=0.05):
    rows, depth = second.shape
    width = bias.shape[1]
    tall, wide = tile_of(rows, 1024), tile_of(width, 1024)
    unit = tile_of(wide, 512)

    def kernel(ids_ref, a_ref, w_ref, b_ref, hidden_ref, slope_ref):
        for part in range(wide // unit):
            here = slice(part * unit, (part + 1) * unit)
            pre = product(a_ref[...], w_ref[:, here], "NN") + b_ref[:, here]
            phi = 0.5 + 0.5 * lax.erf(pre * 0.7071067811865476)
            hidden_ref[:, here] = (pre * phi).astype(BF16)
            slope = phi + pre * (jnp.exp(-0.5 * pre * pre) * 0.3989422804014327)
            slope_ref[:, here] = slope.astype(BF16)

    out = pl.BlockSpec((tall, wide), lambda i, j, ids: (i, j))
    shape = jax.ShapeDtypeStruct((rows, width), BF16)
    return call(
        kernel,
        ids,
        (rows // tall, width // wide),
        [
            pl.BlockSpec((tall, depth), lambda i, j, ids: (i, 0)),
            pl.BlockSpec((depth, wide), lambda i, j, ids: (0, j)),
            pl.BlockSpec((1, wide), lambda i, j, ids: (0, j)),
        ],
        [out, out],
        [shape, shape],
        (second, weight, bias),
        after=after,
        lag=lag,
        name="expand",
    )


def stack_kernel(ids, pieces, unit, after=(), lag=0.05):
    width = pieces[0].shape[1]
    blocks = group(pieces, unit)

    def kernel(ids_ref, *refs):
        for step, block in enumerate(blocks):

            @pl.when(pl.program_id(0) == step)
            def _(block=block):
                for number, row in block:
                    refs[-1][row : row + pieces[number].shape[0], :] = refs[number][...]

    return call(
        kernel,
        ids,
        (len(blocks),),
        [pl.BlockSpec(piece.shape, lambda i, ids: (0, 0)) for piece in pieces],
        pl.BlockSpec((unit, width), lambda i, ids: (i, 0)),
        jax.ShapeDtypeStruct((len(blocks) * unit, width), BF16),
        tuple(pieces),
        after=after,
        lag=lag,
        name="stack",
    )


def shrink_back_kernel(ids, seed, weight, slope, after=(), lag=0.05):
    rows, depth = seed.shape
    width = slope.shape[1]
    tall, wide = tile_of(rows, 1024), tile_of(width, 1024)
    unit = tile_of(wide, 512)

    def kernel(ids_ref, a_ref, w_ref, s_ref, out_ref, sum_ref):
        @pl.when(pl.program_id(1) == 0)
        def _():
            sum_ref[...] = jnp.zeros_like(sum_ref)

        for part in range(wide // unit):
            here = slice(part * unit, (part + 1) * unit)
            grad = product(a_ref[...], w_ref[here, :], "NT") * s_ref[:, here].astype(F32)
            rounded = grad.astype(BF16)
            out_ref[:, here] = rounded
            sum_ref[:, here] += jnp.sum(rounded.astype(F32), axis=0, keepdims=True)

    tile = pl.BlockSpec((tall, wide), lambda j, i, ids: (i, j))
    return call(
        kernel,
        ids,
        (width // wide, rows // tall),
        [
            pl.BlockSpec((tall, depth), lambda j, i, ids: (i, 0)),
            pl.BlockSpec((wide, depth), lambda j, i, ids: (j, 0)),
            tile,
        ],
        [tile, pl.BlockSpec((1, wide), lambda j, i, ids: (0, j))],
        [jax.ShapeDtypeStruct((rows, width), BF16), jax.ShapeDtypeStruct((1, width), F32)],
        (seed, weight, slope),
        after=after,
        lag=lag,
        name="shrink_back",
    )


def plain_kernel(ids, left, right, place, width, after=(), lag=0.05):
    rows, depth = left.shape
    tall = tile_of(rows, 1024)

    def kernel(ids_ref, a_ref, b_ref, out_ref):
        out_ref[...] = product(a_ref[...], b_ref[...], "NT").astype(BF16)

    return call(
        kernel,
        ids,
        (rows // tall,),
        [
            pl.BlockSpec((tall, depth), lambda i, ids: (i, 0)),
            pl.BlockSpec((width, depth), lambda i, ids: (place // width, 0)),
        ],
        pl.BlockSpec((tall, width), lambda i, ids: (i, 0)),
        jax.ShapeDtypeStruct((rows, width), BF16),
        (left, right),
        after=after,
        lag=lag,
        name="plain",
    )


def branches_kernel(ids, context, hidden, weight, blocks, after=(), lag=0.05):
    rows, deep_b = hidden.shape
    depth, deep_a = weight.shape[1], context.shape[1]
    tall, wide = rows // blocks, tile_of(depth, 1024)
    unit = tile_of(wide, 512)

    def kernel(ids_ref, a_ref, m_ref, h_ref, s_ref, *out_refs):
        for block in range(0, blocks, 2):

            @pl.when(pl.program_id(1) == block // 2)
            def _(block=block):
                for part in range(wide // unit):
                    here = slice(part * unit, (part + 1) * unit)
                    value = product(h_ref[...], s_ref[:, here], "NN")
                    value = value + product(a_ref[...], m_ref[:, here], "NN")
                    out_refs[block][:, here] = value[:tall].astype(BF16)
                    out_refs[block + 1][:, here] = value[tall:].astype(BF16)

    return call(
        kernel,
        ids,
        (depth // wide, blocks // 2),
        [
            pl.BlockSpec((2 * tall, deep_a), lambda j, i, ids: (i, 0)),
            pl.BlockSpec((deep_a, wide), lambda j, i, ids: (deep_b // deep_a, j)),
            pl.BlockSpec((2 * tall, deep_b), lambda j, i, ids: (i, 0)),
            pl.BlockSpec((deep_b, wide), lambda j, i, ids: (0, j)),
        ],
        [pl.BlockSpec((tall, wide), lambda j, i, ids: (0, j))] * blocks,
        [jax.ShapeDtypeStruct((tall, depth), BF16)] * blocks,
        (context, weight, hidden, weight),
        after=after,
        lag=lag,
        name="branches",
    )


def back_kernel(ids, left_a, left_b, right, scales, start, count, blocks, after=(), lag=0.05):
    rows = left_a.shape[0] // blocks
    width = right.shape[0]
    deep_a, deep_b = left_a.shape[1], left_b.shape[1]
    wide = tile_of(width, 512 if count == 1 else 1024)
    unit = tile_of(wide, 512)

    def kernel(ids_ref, a_ref, b_ref, c_ref, d_ref, s_ref, *out_refs):
        for block, out_ref in enumerate(out_refs):

            @pl.when(pl.program_id(1) == block)
            def _(out_ref=out_ref):
                for part in range(wide // unit):
                    here = slice(part * unit, (part + 1) * unit)
                    one = product(a_ref[...], b_ref[here, :], "NT") * s_ref[0:1, here]
                    two = product(c_ref[...], d_ref[here, :], "NT") * s_ref[1:2, here]
                    out_ref[:, here] = (one + two).astype(BF16)

    return call(
        kernel,
        ids,
        (width // wide, count),
        [
            pl.BlockSpec((rows, deep_a), lambda j, i, ids: (start + i, 0)),
            pl.BlockSpec((pl.Element(wide), pl.Element(deep_a)), lambda j, i, ids: (j * wide, deep_b)),
            pl.BlockSpec((rows, deep_b), lambda j, i, ids: (start + i, 0)),
            pl.BlockSpec((wide, deep_b), lambda j, i, ids: (j, 0)),
            pl.BlockSpec((2, wide), lambda j, i, ids: (0, j)),
        ],
        [pl.BlockSpec((rows, wide), lambda j, i, ids: (0, j))] * count,
        [jax.ShapeDtypeStruct((rows, width), BF16)] * count,
        (left_a, right, left_b, right, scales),
        after=after,
        lag=lag,
        name="back",
    )


def piece_grad_kernel(ids, left, pieces, after=(), lag=0.05):
    rows, width = left.shape
    unit, depth = pieces[0].shape
    tall, wide = tile_of(width, 1024), tile_of(depth, 1024)
    cut = tile_of(wide, 512)

    def kernel(ids_ref, a_ref, *refs):
        grad_ref, right_ref = refs[len(pieces) :]
        for part in range(wide // cut):
            here = slice(part * cut, (part + 1) * cut)
            total = None
            for number in range(len(pieces)):
                made = product(a_ref[number * unit : (number + 1) * unit, :], refs[number][:, here], "TN")
                total = made if total is None else total + made
            grad_ref[:, here] = total.astype(BF16)

        @pl.when(pl.program_id(1) == 0)
        def _():
            for number in range(len(pieces)):
                right_ref[number * unit : (number + 1) * unit, :] = refs[number][...]

    return call(
        kernel,
        ids,
        (depth // wide, width // tall),
        [pl.BlockSpec((rows, tall), lambda j, i, ids: (0, i))]
        + [pl.BlockSpec((unit, wide), lambda j, i, ids: (0, j))] * len(pieces),
        [
            pl.BlockSpec((tall, wide), lambda j, i, ids: (i, j)),
            pl.BlockSpec((rows, wide), lambda j, i, ids: (0, j)),
        ],
        [jax.ShapeDtypeStruct((width, depth), BF16), jax.ShapeDtypeStruct((rows, depth), BF16)],
        (left, *pieces),
        after=after,
        lag=lag,
        name="piece_grad",
    )


def full_grad_kernel(ids, left, right, weight=None, total=None, place=0, spare=0, start=0, span=0, kept=(), after=(), lag=0.05):
    rows, depth = left.shape
    width = right.shape[1]
    tall, wide = (tile_of(depth, 512), width) if span else (tile_of(depth, 1024), tile_of(width, 1024))
    unit = tile_of(wide, 512)
    summed = weight is not None

    def kernel(ids_ref, a_ref, b_ref, *refs):
        out_ref = refs[2 if summed else 0]
        if summed:

            @pl.when(pl.program_id(1) == 0)
            def _():
                refs[3][...] = jnp.zeros_like(refs[3])
                refs[4][...] = jnp.zeros_like(refs[4])

        for part in range(wide // unit):
            here = slice(part * unit, (part + 1) * unit)
            value = product(a_ref[...], b_ref[:, here], "TN")
            out_ref[:, here] = value.astype(BF16)
            if summed:
                held = refs[0][:, here].astype(F32)
                one, two = held * value, held * refs[1][:, here]
                refs[3][...] += sum(one[:, lane : lane + 128] for lane in range(0, unit, 128))
                refs[4][...] += sum(two[:, lane : lane + 128] for lane in range(0, unit, 128))

    tile = pl.BlockSpec((tall, wide), lambda i, j, ids: (i, j))
    in_specs = [
        pl.BlockSpec((rows, tall), lambda i, j, ids: (0, i)),
        pl.BlockSpec((rows, wide), lambda i, j, ids: (0, j)),
    ]
    out_specs = [pl.BlockSpec((tall, wide), lambda i, j, ids: (i, start // wide + j))]
    out_shape = [jax.ShapeDtypeStruct((depth, span or width + spare), BF16)]
    args = (left, right)
    if summed:
        args += (weight, total)
        in_specs += [
            pl.BlockSpec((pl.Element(tall), pl.Element(wide)), lambda i, j, ids: (i * tall, pl.multiple_of(place + j * wide, 128))),
            pl.BlockSpec((1, wide), lambda i, j, ids: (0, j)),
        ]
        out_specs += [pl.BlockSpec((tall, 128), lambda i, j, ids: (i, 0))] * 2
        out_shape += [jax.ShapeDtypeStruct((depth, 128), F32)] * 2
    return call(
        kernel,
        ids,
        (depth // tall, width // wide),
        in_specs,
        out_specs,
        out_shape,
        args,
        kept=kept,
        after=after,
        lag=lag,
        name="full_grad",
    )


def sums_kernel(ids, wide, rows, after=(), lag=0.05):
    depth = rows.shape[1]
    count = len(wide)

    def kernel(ids_ref, *refs):
        total = refs[count][...]
        for number, ref in enumerate(refs[:count]):
            row = lax.broadcasted_iota(jnp.int32, (8, 128), 0)
            pick = jnp.where(row == number, 1.0, 0.0).astype(BF16)
            high = ref[...].astype(BF16)
            rest = (ref[...] - high.astype(F32)).astype(BF16)
            total = total + product(pick, high, "NT") + product(pick, rest, "NT")
        refs[-1][...] = total

    def whole(shape):
        return pl.BlockSpec(shape, lambda i, ids: (0, 0))

    return call(
        kernel,
        ids,
        (1,),
        [whole((depth, 128))] * count + [whole((8, depth))],
        whole((8, depth)),
        jax.ShapeDtypeStruct((8, depth), F32),
        (*wide, rows),
        after=after,
        lag=lag,
        name="sums",
    )


def slots_kernel(ids, kept, parts, size, after=(), lag=0.05):
    count, width = parts[0].shape
    each = width // size

    def kernel(ids_ref, *refs):
        total = refs[0][...]
        for ref in refs[1 : len(parts)]:
            total = total + ref[...]
        held = refs[-1]
        held[...] = total
        for number in range(size):
            place = pl.multiple_of((ids_ref[1] ^ number) * each, 128)
            refs[len(parts) + 1 + number][...] = held[:, pl.ds(place, each)]

    return call(
        kernel,
        ids,
        (1,),
        [pl.BlockSpec((count, width), lambda i, ids: (0, 0))] * len(parts),
        [pl.BlockSpec(memory_space=pl.ANY)] + [pl.BlockSpec((count, each), lambda i, ids: (0, 0))] * size,
        [jax.ShapeDtypeStruct(kept.shape, BF16)] + [jax.ShapeDtypeStruct((count, each), F32)] * size,
        tuple(parts),
        scratch=[pltpu.VMEM((count, width), F32)],
        kept=(kept,),
        after=after,
        lag=lag,
        name="slots",
    )


def output_kernel(ids, rows, parts, vectors, after=(), lag=0.05):
    count, width = rows.shape

    def kernel(ids_ref, x_ref, vec, *refs):
        total = refs[0][...].astype(F32)
        for ref in refs[1:-1]:
            total = total + ref[...].astype(F32)
        refs[-1][...] = (x_ref[...].astype(F32) + total + (vec[4:5, :] + vec[5:6, :])).astype(BF16)

    unit = tile_of(count, 256)
    tile = pl.BlockSpec((unit, width), lambda i, ids: (i, 0))
    return call(
        kernel,
        ids,
        (count // unit,),
        [tile, pl.BlockSpec(vectors.shape, lambda i, ids: (0, 0))] + [tile] * len(parts),
        tile,
        jax.ShapeDtypeStruct((count, width), BF16),
        (rows, vectors, *parts),
        after=after,
        lag=lag,
        name="output",
    )


def widen_kernel(ids, rows, widths, after=(), lag=0.05):
    count = rows.shape[0]
    specs, shapes, place = [], [], 0
    for width in widths:
        specs.append(pl.BlockSpec((pl.Element(count), pl.Element(width)), lambda i, ids, place=place: (0, place)))
        shapes.append(jax.ShapeDtypeStruct((count, width), F32))
        place += width

    def kernel(ids_ref, *refs):
        for in_ref, out_ref in zip(refs[: len(specs)], refs[len(specs) :]):
            out_ref[...] = in_ref[...].astype(F32)

    return call(
        kernel,
        ids,
        (1,),
        specs,
        [pl.BlockSpec(shape.shape, lambda i, ids: (0, 0)) for shape in shapes],
        shapes,
        (rows,) * len(specs),
        after=after,
        lag=lag,
        name="widen",
    )


def finish_kernel(ids, rows, widths, heads, parts, scales, last, after=(), lag=0.05):
    count = rows.shape[0]
    one, two = widths
    each = one // heads

    def kernel(ids_ref, in_ref, v_ref, *refs):
        one_ref, two_ref, *sum_refs = refs[len(parts) :]
        for head in range(heads):
            one_ref[:, head, :] = in_ref[:, head * each : (head + 1) * each].astype(F32)
        two_ref[...] = jnp.transpose(in_ref[:, one : one + two].astype(F32))
        sums = refs[0][...]
        for ref in refs[1 : len(parts)]:
            sums = sums + ref[...]
        for number, sum_ref in zip((0, 1, 2, 3, 4, 4, 5, 6), sum_refs):
            value = sums[number : number + 1]
            if number in (0, 2):
                value = (value - v_ref[number + 1 : number + 2, :] * sums[number + 1 : number + 2]) / v_ref[number : number + 1, :]
            wide = sum_ref.shape[1]
            for row in range(sum_ref.shape[0]):
                sum_ref[row : row + 1, :] = value[:, row * wide : (row + 1) * wide]

    def whole(shape):
        return pl.BlockSpec(shape, lambda i, ids: (0,) * len(shape))

    shapes = [(count, heads, each), (two, count)] + [(1, count)] * 6 + last
    return call(
        kernel,
        ids,
        (1,),
        [whole(array.shape) for array in (rows, scales, *parts)],
        [whole(shape) for shape in shapes],
        [jax.ShapeDtypeStruct(shape, F32) for shape in shapes],
        (rows, scales, *parts),
        after=after,
        lag=lag,
        name="finish",
    )


def total_kernel(ids, parts, after=(), lag=0.05):
    rows, width = parts[0].shape

    def kernel(ids_ref, *refs):
        total = refs[0][...].astype(F32)
        for ref in refs[1:-1]:
            total = total + ref[...].astype(F32)
        refs[-1][...] = total

    unit = min(rows, 256)
    tile = pl.BlockSpec((unit, width), lambda i, ids: (i, 0))
    return call(
        kernel,
        ids,
        (rows // unit,),
        [tile] * len(parts),
        tile,
        jax.ShapeDtypeStruct((rows, width), F32),
        tuple(parts),
        after=after,
        lag=lag,
        name="total",
    )


def input_kernel(ids, rows, seed, parts, after=(), lag=0.05):
    count, width = rows.shape

    def kernel(ids_ref, x_ref, g_ref, *refs):
        back = refs[0][...].astype(F32)
        for ref in refs[1:-1]:
            back = back + ref[...].astype(F32)
        data = x_ref[...].astype(F32)
        centre = data - jnp.mean(data, axis=-1, keepdims=True)
        rstd = lax.rsqrt(jnp.mean(centre * centre, axis=-1, keepdims=True) + EPSILON)
        scaled = centre * rstd
        inner = jnp.mean(back * scaled, axis=-1, keepdims=True)
        back = back - jnp.mean(back, axis=-1, keepdims=True) - scaled * inner
        refs[-1][...] = g_ref[...].astype(F32) + rstd * back

    unit = tile_of(count, 256)
    tile = pl.BlockSpec((unit, width), lambda i, ids: (i, 0))
    return call(
        kernel,
        ids,
        (count // unit,),
        [tile] * (2 + len(parts)),
        tile,
        jax.ShapeDtypeStruct((count, width), F32),
        (rows, seed, *parts),
        after=after,
        lag=lag,
        name="input",
    )


def rotary_tables(length):
    position = jnp.arange(length, dtype=F32)[:, None]
    lane = jnp.arange(128)
    half = ROTARY // 2
    frequency = 10000.0 ** (-2.0 * (lane % half).astype(F32) / ROTARY)
    angles = position * frequency[None, :]
    sine = jnp.sin(angles)
    tables = (
        jnp.where(lane < ROTARY, jnp.cos(angles), 1.0),
        jnp.where(lane < half, -sine, 0.0),
        jnp.where((lane >= half) & (lane < ROTARY), sine, 0.0),
    )
    return jnp.concatenate(tables, axis=1)


def flip(value, axis, bit, size):
    return lax.ppermute(value, axis, [(i, i ^ bit) for i in range(size)])


def sum_over(value, axis, size):
    bit = 1
    while bit < size:
        value = value + flip(value, axis, bit, size)
        bit *= 2
    return value


def half_kernel(ids, rows, number, after=(), lag=0.05):
    count, width = rows.shape[0] // 2, rows.shape[1]

    def kernel(ids_ref, in_ref, out_ref):
        out_ref[...] = in_ref[...]

    return call(
        kernel,
        ids,
        (1,),
        [pl.BlockSpec((count, width), lambda i, ids: (number, 0))],
        pl.BlockSpec((count, width), lambda i, ids: (0, 0)),
        jax.ShapeDtypeStruct((count, width), BF16),
        (rows,),
        after=after,
        lag=lag,
        name="half",
    )


def gather_rows(ids, rows, size, after=()):
    if size != 4:
        return [rows] + [flip(rows, "tensor", k, size) for k in range(1, size)]
    one = flip(rows, "tensor", 1, size)
    two = flip(rows, "tensor", 2, size)
    upper = flip(half_kernel(ids, two, 0, after), "tensor", 1, size)
    lower = flip(half_kernel(ids, one, 1, after), "tensor", 2, size)
    return [rows, one, two, upper, lower]


def body(
    layer_input,
    cotangent,
    firstgain,
    firstbias,
    secondgain,
    secondbias,
    project,
    projbias,
    merging,
    mergebias,
    expand,
    expandbias,
    shrink,
    shrinkbias,
):
    n_dp, n_tensor = lax.axis_size("dp"), lax.axis_size("tensor")
    dp_at, tensor_at = lax.axis_index("dp"), lax.axis_index("tensor")
    ids = jnp.stack([tensor_at, dp_at]).astype(jnp.int32)
    own_count, width = layer_input.shape
    group_count = own_count * n_tensor
    assert group_count == LENGTH
    depth = width // n_dp
    heads = project.shape[1]
    mixed_width = heads * 3 * HEAD_DIM
    hidden_width = expand.shape[1]

    packed = jnp.concatenate(
        [firstgain, firstbias, secondgain, secondbias, mergebias, shrinkbias, expandbias, projbias.reshape(-1)]
    )
    slots = jnp.where(jnp.arange(n_dp)[:, None] == dp_at, packed[None, :], jnp.zeros((), BF16))
    slots = sum_over(slots, "dp", n_dp).astype(F32)
    vectors = jnp.transpose(slots[:, : 6 * depth].reshape(n_dp, 6, depth), (1, 0, 2)).reshape(6, width)
    at = 6 * depth
    part = hidden_width // n_dp
    b_expand = slots[:, at : at + part].reshape(1, hidden_width)
    at += part
    b_project = jnp.transpose(slots[:, at:].reshape(n_dp, heads, -1), (1, 0, 2)).reshape(1, mixed_width)

    tables = rotary_tables(LENGTH)
    own_project = project.reshape(depth, mixed_width)
    w_in = lax.all_gather(jnp.concatenate([expand, own_project], axis=1), "dp", axis=0, tiled=True)
    w_out = lax.all_gather(jnp.concatenate([shrink, merging], axis=0), "dp", axis=1, tiled=True)

    unit = own_count
    rows_pieces = gather_rows(ids, layer_input, n_tensor, (vectors, tables))
    near, far = (rows_pieces[:-1], rows_pieces[-1:]) if n_tensor != 4 else (rows_pieces[:3], rows_pieces[3:])
    pair = norm_kernel(ids, near, vectors, unit, 0, n_tensor)
    later = stack_kernel(ids, [cotangent], unit, after=(pair[0], *far))
    seed_pieces = [later] + [flip(later, "tensor", k, n_tensor) for k in range(n_tensor - 1, 0, -1)]
    first, second = norm_kernel(ids, far, vectors, unit, n_tensor - 1, n_tensor, kept=pair, after=(later,))
    hidden, slope = expand_kernel(ids, second, w_in, b_expand)
    mixed = mixed_kernel(ids, first, w_in, hidden_width, b_project, tables, n_tensor, after=(hidden,))
    shrink_part, seed = piece_grad_kernel(ids, hidden, seed_pieces[:1] + seed_pieces[:0:-1], after=(mixed,))
    shrink_grad = lax.psum_scatter(shrink_part, "dp", scatter_dimension=1, tiled=True)
    context, lse = attend_kernel(ids, mixed, n_tensor, after=(shrink_part,))
    merge_width = merging.shape[0]
    joint = mixed_width + merge_width
    part = full_grad_kernel(ids, seed, context, start=mixed_width, span=joint)
    branches = branches_kernel(ids, context, hidden, w_out, n_tensor, after=part)
    summed = [branches[0]] + [flip(branches[k], "tensor", k, n_tensor) for k in range(n_tensor - 1, 0, -1)]
    pgrad, expand_sum = shrink_back_kernel(ids, seed, w_out, slope, after=(branches[0],))
    expand_part, gain_two, bias_two = full_grad_kernel(ids, second, pgrad, w_in, expand_sum)
    expand_grad = lax.psum_scatter(expand_part, "dp", scatter_dimension=0, tiled=True)
    cgrad = plain_kernel(ids, seed, w_out, hidden_width, merge_width, after=(expand_part,))
    mgrad, mixed_sum = attend_back_kernel(ids, mixed, cgrad, context, lse, tables, n_tensor)
    project_part, gain_one, bias_one = full_grad_kernel(
        ids, first, mgrad, w_in, mixed_sum, place=hidden_width, span=joint, kept=part
    )

    def slots(values):
        return jnp.pad(values, ((0, 0), (0, depth - values.shape[1]))).reshape(1, width)

    seed_sum = jnp.sum(cotangent.astype(F32), axis=0, keepdims=True)
    over_all = jnp.pad(seed_sum, ((4, 3), (0, 0)))
    over_all = sums_kernel(ids, [gain_one, bias_one, gain_two, bias_two], over_all)
    over_dp = [
        slots(expand_sum.reshape(n_dp, -1)),
        slots(jnp.transpose(mixed_sum.reshape(heads, n_dp, -1), (1, 0, 2)).reshape(n_dp, -1)),
    ]
    over_dp = jnp.pad(jnp.concatenate(over_dp, axis=0), ((5, 1), (0, 0)))
    over_tensor = [over_all] + [flip(over_all, "tensor", k, n_tensor) for k in range(n_tensor - 1, 0, -1)]

    gains = jnp.stack([vectors[0], vectors[2]])
    back = []
    last = over_all
    half = n_tensor // 2
    for start, count in ((half + 1, half - 1), (1, half), (0, 1)):
        made = back_kernel(ids, mgrad, pgrad, w_in, gains, start, count, n_tensor, after=(last,))
        back.append([flip(made[k], "tensor", start + k, n_tensor) if start else made[k] for k in range(count - 1, -1, -1)])
        last = made[0]
        if len(back) == 1:
            layer_output = output_kernel(ids, layer_input, summed, vectors, after=(last,), lag=160)
            project_part, *sums = slots_kernel(ids, project_part, over_tensor + [over_dp], n_dp, after=(layer_output,))
            project_grad = lax.psum_scatter(project_part, "dp", scatter_dimension=0, tiled=True)
            (shrink_grad,) = widen_kernel(ids, shrink_grad, [shrink.shape[1]], after=(sums[0],))
            last = shrink_grad
    (expand_grad,) = widen_kernel(ids, expand_grad, [hidden_width], after=(last,))
    far = total_kernel(ids, back[0] + back[2], after=(expand_grad,), lag=8)
    input_grad = input_kernel(ids, layer_input, cotangent, back[1] + [far], lag=154)
    scales = jnp.stack([firstgain, firstbias, secondgain, secondbias]).astype(F32)
    sums = [sums[0]] + [flip(sums[k], "dp", k, n_dp) for k in range(1, n_dp)]
    project_grad, merging_grad, *sums = finish_kernel(
        ids, project_grad, [mixed_width, merge_width], heads, sums, scales, [(1, expandbias.shape[0]), projbias.shape], after=(input_grad,)
    )
    projbias_grad = sums.pop()
    gain_one, bias_one, gain_two, bias_two, seed_sum, seed_sum_again, expandbias_grad = [value[0] for value in sums]
    return (
        layer_output,
        input_grad,
        gain_one,
        bias_one,
        gain_two,
        bias_two,
        project_grad,
        projbias_grad,
        merging_grad,
        seed_sum,
        expand_grad,
        expandbias_grad,
        shrink_grad,
        seed_sum_again,
    )


def solution(mesh):
    specs = (
        P(("dp", "tensor"), None),
        P(("dp", "tensor"), None),
        P("dp"),
        P("dp"),
        P("dp"),
        P("dp"),
        P("dp", "tensor", None),
        P("tensor", "dp"),
        P("tensor", "dp"),
        P("dp"),
        P("dp", "tensor"),
        P(("tensor", "dp")),
        P("tensor", "dp"),
        P("dp"),
    )
    return jax.shard_map(body, mesh=mesh, in_specs=specs, out_specs=specs, check_vma=False)
```

```python
import jax
import jax.numpy as jnp
from jax import lax
from jax.experimental import pallas as pl
from jax.experimental.pallas import tpu as pltpu
from jax.sharding import PartitionSpec as P

HEAD_DIM = 256
ROTARY = 64
LENGTH = 2048
EPSILON = 1e-05
BIG = -1e30
F32 = jnp.float32
BF16 = jnp.bfloat16
DIMS = {
    "NN": (((1,), (0,)), ((), ())),
    "NT": (((1,), (1,)), ((), ())),
    "TN": (((0,), (0,)), ((), ())),
}


def product(left, right, mode):
    return lax.dot_general(left, right, DIMS[mode], preferred_element_type=F32)


def params():
    return pltpu.CompilerParams(vmem_limit_bytes=56 << 20)


def cost(lag):
    return pl.CostEstimate(flops=int(lag * 1e9), bytes_accessed=0, transcendentals=0)


def tile_of(width, most):
    best = 128
    for size in range(128, most + 1, 128):
        if width % size == 0:
            best = size
    return best


def call(kernel, ids, grid, in_specs, out_specs, out_shape, args, name, scratch=(), after=(), kept=(), lag=0.05):
    count = len(args)
    unread = tuple(kept) + tuple(after)

    def run(ids_ref, *refs):
        kernel(ids_ref, *refs[:count], *refs[count + len(unread) :])

    return pl.pallas_call(
        run,
        grid_spec=pltpu.PrefetchScalarGridSpec(
            num_scalar_prefetch=1,
            grid=grid,
            in_specs=list(in_specs) + [pl.BlockSpec(memory_space=pl.ANY)] * len(unread),
            out_specs=out_specs,
            scratch_shapes=list(scratch),
        ),
        out_shape=out_shape,
        input_output_aliases={1 + count + k: k for k in range(len(kept))},
        compiler_params=params(),
        cost_estimate=cost(lag),
        name=name,
    )(ids, *args, *unread)


def group(pieces, unit):
    blocks, filled = [], unit
    for number, piece in enumerate(pieces):
        if filled == unit:
            blocks.append([])
            filled = 0
        blocks[-1].append((number, filled))
        filled += piece.shape[0]
    return blocks


def norm_kernel(ids, pieces, vectors, unit, start, total, kept=(), after=(), lag=0.05):
    width = pieces[0].shape[1]
    blocks = group(pieces, unit)

    def kernel(ids_ref, *refs):
        vec = refs[len(pieces)]
        first_ref, second_ref = refs[len(pieces) + 1 :]
        for step, block in enumerate(blocks):

            @pl.when(pl.program_id(0) == step)
            def _(block=block):
                for number, row in block:
                    rows = slice(row, row + pieces[number].shape[0])
                    data = refs[number][...].astype(F32)
                    centre = data - jnp.mean(data, axis=-1, keepdims=True)
                    spread = jnp.mean(centre * centre, axis=-1, keepdims=True)
                    scaled = centre * lax.rsqrt(spread + EPSILON)
                    first_ref[rows, :] = (scaled * vec[0:1, :] + vec[1:2, :]).astype(BF16)
                    second_ref[rows, :] = (scaled * vec[2:3, :] + vec[3:4, :]).astype(BF16)

    out = pl.BlockSpec((unit, width), lambda i, ids: (start + i, 0))
    shape = jax.ShapeDtypeStruct((total * unit, width), BF16)
    return call(
        kernel,
        ids,
        (len(blocks),),
        [pl.BlockSpec(array.shape, lambda i, ids: (0, 0)) for array in (*pieces, vectors)],
        [out, out],
        [shape, shape],
        (*pieces, vectors),
        kept=kept,
        after=after,
        lag=lag,
        name="norm",
    )


def rotate(block, table, sign):
    cos, sin_low, sin_high = table[:, :128], table[:, 128:256], table[:, 256:]
    lead = block[:, :128]
    turned = (
        lead * cos
        + sign * (pltpu.roll(lead, 96, 1) * sin_low + pltpu.roll(lead, 32, 1) * sin_high)
    )
    return jnp.concatenate([turned, block[:, 128:]], axis=1)


def mixed_kernel(ids, first, weight, place, bias, tables, blocks, after=(), lag=0.05):
    rows, depth = first.shape
    heads = bias.shape[1] // (3 * HEAD_DIM)
    unit = rows // blocks
    wide = 3 * HEAD_DIM

    def kernel(ids_ref, a_ref, w_ref, b_ref, low_ref, high_ref, out_ref):
        for part in range(3):
            here = slice(part * HEAD_DIM, (part + 1) * HEAD_DIM)
            value = product(a_ref[...], w_ref[:, here], "NN") + b_ref[:, here]
            if part < 2:
                value = rotate(value, jnp.concatenate([low_ref[...], high_ref[...]], axis=0), 1.0)
            out_ref[:, here] = value.astype(BF16)

    def table(block):
        return pl.BlockSpec((unit, 3 * 128), lambda j, i, ids: (ids[0] ^ (2 * i + block), 0))

    return call(
        kernel,
        ids,
        (heads, blocks // 2),
        [
            pl.BlockSpec((2 * unit, depth), lambda j, i, ids: (i, 0)),
            pl.BlockSpec((pl.Element(depth), pl.Element(wide)), lambda j, i, ids: (0, pl.multiple_of(place + wide * j, 128))),
            pl.BlockSpec((1, wide), lambda j, i, ids: (0, j)),
            table(0),
            table(1),
        ],
        pl.BlockSpec((2 * unit, wide), lambda j, i, ids: (i, j)),
        jax.ShapeDtypeStruct((rows, heads * wide), BF16),
        (first, weight, bias, tables, tables),
        after=after,
        lag=lag,
        name="mixed",
    )


def attend_kernel(ids, mixed, blocks, after=(), lag=0.05):
    rows, width = mixed.shape
    heads = width // (3 * HEAD_DIM)
    unit = rows // blocks
    lanes = range(0, unit, 128)
    scale = HEAD_DIM ** (-0.5)

    def kernel(ids_ref, x_ref, ctx_ref, lse_ref):
        me = ids_ref[0]

        def place(block):
            return pl.ds(pl.multiple_of((me ^ block) * unit, unit), unit)

        def head_of(block, head):
            at = 3 * HEAD_DIM * head
            query = x_ref[place(block), at : at + HEAD_DIM] * jnp.asarray(scale, BF16)
            tiles = []
            for other in range(block + 1):
                scores = product(query, x_ref[place(other), at + HEAD_DIM : at + 2 * HEAD_DIM], "NT")
                if other == block:
                    row_at = lax.broadcasted_iota(jnp.int32, scores.shape, 0)
                    col_at = lax.broadcasted_iota(jnp.int32, scores.shape, 1)
                    scores = jnp.where(col_at <= row_at, scores, BIG)
                tiles.append(scores)
            top = None
            for scores in tiles:
                for lane in lanes:
                    piece = scores[:, lane : lane + 128]
                    top = piece if top is None else jnp.maximum(top, piece)
            top = jnp.max(top, axis=1, keepdims=True)
            total = acc = None
            for other, scores in enumerate(tiles):
                weight = jnp.exp(scores - top)
                for lane in lanes:
                    piece = weight[:, lane : lane + 128]
                    total = piece if total is None else total + piece
                value = x_ref[place(other), at + 2 * HEAD_DIM : at + 3 * HEAD_DIM]
                made = product(weight.astype(BF16), value, "NN")
                acc = made if acc is None else acc + made
            total = jnp.sum(total, axis=1, keepdims=True)
            ctx_ref[:, HEAD_DIM * head : HEAD_DIM * (head + 1)] = (acc / total).astype(BF16)
            log_total = jnp.broadcast_to(top + jnp.log(total), (unit, 128))
            lse_ref[head, 0] = jnp.transpose(log_total)[:8]

        for block in range(blocks):

            @pl.when(pl.program_id(0) == block)
            def _(block=block):
                for head in range(heads):
                    head_of(block, head)

    return call(
        kernel,
        ids,
        (blocks,),
        [pl.BlockSpec((rows, width), lambda b, ids: (0, 0))],
        [
            pl.BlockSpec((unit, heads * HEAD_DIM), lambda b, ids: (ids[0] ^ b, 0)),
            pl.BlockSpec((heads, 1, 8, unit), lambda b, ids: (0, b, 0, 0)),
        ],
        [
            jax.ShapeDtypeStruct((rows, heads * HEAD_DIM), BF16),
            jax.ShapeDtypeStruct((heads, blocks, 8, unit), F32),
        ],
        (mixed,),
        after=after,
        lag=lag,
        name="attend",
    )


def attend_back_kernel(ids, mixed, grad, context, lse, tables, blocks, after=(), lag=0.05):
    rows, width = mixed.shape
    heads = width // (3 * HEAD_DIM)
    unit = rows // blocks
    scale = HEAD_DIM ** (-0.5)

    def kernel(ids_ref, x_ref, g_ref, c_ref, lse_ref, t_ref, out_ref, sum_ref, dk_s, dv_s):
        me = ids_ref[0]

        def place(block):
            return pl.ds(pl.multiple_of((me ^ block) * unit, unit), unit)

        def head_of(block, head):
            at = 3 * HEAD_DIM * head
            cols = slice(HEAD_DIM * head, HEAD_DIM * (head + 1))
            query = x_ref[place(block), at : at + HEAD_DIM] * jnp.asarray(scale, BF16)
            seed = g_ref[place(block), cols]
            inner = jnp.sum(seed.astype(F32) * c_ref[place(block), cols].astype(F32), axis=1, keepdims=True)
            inner = jnp.transpose(jnp.broadcast_to(inner, (unit, 128)))[:1]
            log_total = lse_ref[head, 0][:1]
            dquery = None
            for other in reversed(range(block + 1)):
                key = x_ref[place(other), at + HEAD_DIM : at + 2 * HEAD_DIM]
                value = x_ref[place(other), at + 2 * HEAD_DIM : at + 3 * HEAD_DIM]
                prob = jnp.exp(product(key, query, "NT") - log_total)
                if other == block:
                    key_at = lax.broadcasted_iota(jnp.int32, prob.shape, 0)
                    row_at = lax.broadcasted_iota(jnp.int32, prob.shape, 1)
                    prob = jnp.where(key_at <= row_at, prob, 0.0)
                dscore = (prob * (product(value, seed, "NT") - inner)).astype(BF16)
                dvalue = product(prob.astype(BF16), seed, "NN")
                dkey = product(dscore, query, "NN")
                if block < blocks - 1:
                    dvalue = dvalue + dv_s[head, other]
                    dkey = dkey + dk_s[head, other]
                if other < block:
                    dv_s[head, other] = dvalue
                    dk_s[head, other] = dkey
                else:
                    done = (dkey, dvalue)
                made = product(dscore, key, "TN")
                dquery = made if dquery is None else dquery + made
            dquery = rotate(dquery * scale, t_ref[...], -1.0)
            dkey = rotate(done[0], t_ref[...], -1.0)
            for part, value in enumerate((dquery, dkey, done[1])):
                cols = slice(at + part * HEAD_DIM, at + (part + 1) * HEAD_DIM)
                rounded = value.astype(BF16)
                out_ref[:, cols] = rounded
                column = jnp.sum(rounded.astype(F32), axis=0, keepdims=True)
                if block < blocks - 1:
                    column = column + sum_ref[:, cols]
                sum_ref[:, cols] = column

        for turn in range(blocks):

            @pl.when(pl.program_id(0) == turn)
            def _(turn=turn):
                for head in range(heads):
                    head_of(blocks - 1 - turn, head)

    def whole(cols):
        return pl.BlockSpec((rows, cols), lambda b, ids: (0, 0))

    table = pl.BlockSpec((unit, 3 * 128), lambda b, ids: (blocks - 1 - b, 0))
    return call(
        kernel,
        ids,
        (blocks,),
        [
            whole(width),
            whole(heads * HEAD_DIM),
            whole(heads * HEAD_DIM),
            pl.BlockSpec((heads, 1, 8, unit), lambda b, ids: (0, blocks - 1 - b, 0, 0)),
            table,
        ],
        [
            pl.BlockSpec((unit, width), lambda b, ids: (ids[0] ^ (blocks - 1 - b), 0)),
            pl.BlockSpec((1, width), lambda b, ids: (0, 0)),
        ],
        [jax.ShapeDtypeStruct((rows, width), BF16), jax.ShapeDtypeStruct((1, width), F32)],
        (mixed, grad, context, lse, tables),
        scratch=[
            pltpu.VMEM((heads, blocks, unit, HEAD_DIM), F32),
            pltpu.VMEM((heads, blocks, unit, HEAD_DIM), F32),
        ],
        after=after,
        lag=lag,
        name="attend_back",
    )


def expand_kernel(ids, second, weight, bias, after=(), lag=0.05):
    rows, depth = second.shape
    width = bias.shape[1]
    tall, wide = tile_of(rows, 1024), tile_of(width, 1024)
    unit = tile_of(wide, 512)

    def kernel(ids_ref, a_ref, w_ref, b_ref, hidden_ref, slope_ref):
        for part in range(wide // unit):
            here = slice(part * unit, (part + 1) * unit)
            pre = product(a_ref[...], w_ref[:, here], "NN") + b_ref[:, here]
            phi = 0.5 + 0.5 * lax.erf(pre * 0.7071067811865476)
            hidden_ref[:, here] = (pre * phi).astype(BF16)
            slope = phi + pre * (jnp.exp(-0.5 * pre * pre) * 0.3989422804014327)
            slope_ref[:, here] = slope.astype(BF16)

    out = pl.BlockSpec((tall, wide), lambda i, j, ids: (i, j))
    shape = jax.ShapeDtypeStruct((rows, width), BF16)
    return call(
        kernel,
        ids,
        (rows // tall, width // wide),
        [
            pl.BlockSpec((tall, depth), lambda i, j, ids: (i, 0)),
            pl.BlockSpec((depth, wide), lambda i, j, ids: (0, j)),
            pl.BlockSpec((1, wide), lambda i, j, ids: (0, j)),
        ],
        [out, out],
        [shape, shape],
        (second, weight, bias),
        after=after,
        lag=lag,
        name="expand",
    )


def stack_kernel(ids, pieces, unit, after=(), lag=0.05):
    width = pieces[0].shape[1]
    blocks = group(pieces, unit)

    def kernel(ids_ref, *refs):
        for step, block in enumerate(blocks):

            @pl.when(pl.program_id(0) == step)
            def _(block=block):
                for number, row in block:
                    refs[-1][row : row + pieces[number].shape[0], :] = refs[number][...]

    return call(
        kernel,
        ids,
        (len(blocks),),
        [pl.BlockSpec(piece.shape, lambda i, ids: (0, 0)) for piece in pieces],
        pl.BlockSpec((unit, width), lambda i, ids: (i, 0)),
        jax.ShapeDtypeStruct((len(blocks) * unit, width), BF16),
        tuple(pieces),
        after=after,
        lag=lag,
        name="stack",
    )


def shrink_back_kernel(ids, seed, weight, slope, after=(), lag=0.05):
    rows, depth = seed.shape
    width = slope.shape[1]
    tall, wide = tile_of(rows, 1024), tile_of(width, 1024)
    unit = tile_of(wide, 512)

    def kernel(ids_ref, a_ref, w_ref, s_ref, out_ref, sum_ref):
        @pl.when(pl.program_id(1) == 0)
        def _():
            sum_ref[...] = jnp.zeros_like(sum_ref)

        for part in range(wide // unit):
            here = slice(part * unit, (part + 1) * unit)
            grad = product(a_ref[...], w_ref[here, :], "NT") * s_ref[:, here].astype(F32)
            rounded = grad.astype(BF16)
            out_ref[:, here] = rounded
            sum_ref[:, here] += jnp.sum(rounded.astype(F32), axis=0, keepdims=True)

    tile = pl.BlockSpec((tall, wide), lambda j, i, ids: (i, j))
    return call(
        kernel,
        ids,
        (width // wide, rows // tall),
        [
            pl.BlockSpec((tall, depth), lambda j, i, ids: (i, 0)),
            pl.BlockSpec((wide, depth), lambda j, i, ids: (j, 0)),
            tile,
        ],
        [tile, pl.BlockSpec((1, wide), lambda j, i, ids: (0, j))],
        [jax.ShapeDtypeStruct((rows, width), BF16), jax.ShapeDtypeStruct((1, width), F32)],
        (seed, weight, slope),
        after=after,
        lag=lag,
        name="shrink_back",
    )


def plain_kernel(ids, left, right, place, width, after=(), lag=0.05):
    rows, depth = left.shape
    tall = tile_of(rows, 1024)

    def kernel(ids_ref, a_ref, b_ref, out_ref):
        out_ref[...] = product(a_ref[...], b_ref[...], "NT").astype(BF16)

    return call(
        kernel,
        ids,
        (rows // tall,),
        [
            pl.BlockSpec((tall, depth), lambda i, ids: (i, 0)),
            pl.BlockSpec((width, depth), lambda i, ids: (place // width, 0)),
        ],
        pl.BlockSpec((tall, width), lambda i, ids: (i, 0)),
        jax.ShapeDtypeStruct((rows, width), BF16),
        (left, right),
        after=after,
        lag=lag,
        name="plain",
    )


def branches_kernel(ids, context, hidden, weight, blocks, after=(), lag=0.05):
    rows, deep_b = hidden.shape
    depth, deep_a = weight.shape[1], context.shape[1]
    tall, wide = rows // blocks, tile_of(depth, 1024)
    unit = tile_of(wide, 512)

    def kernel(ids_ref, a_ref, m_ref, h_ref, s_ref, *out_refs):
        for block in range(0, blocks, 2):

            @pl.when(pl.program_id(1) == block // 2)
            def _(block=block):
                for part in range(wide // unit):
                    here = slice(part * unit, (part + 1) * unit)
                    value = product(h_ref[...], s_ref[:, here], "NN")
                    value = value + product(a_ref[...], m_ref[:, here], "NN")
                    out_refs[block][:, here] = value[:tall].astype(BF16)
                    out_refs[block + 1][:, here] = value[tall:].astype(BF16)

    return call(
        kernel,
        ids,
        (depth // wide, blocks // 2),
        [
            pl.BlockSpec((2 * tall, deep_a), lambda j, i, ids: (i, 0)),
            pl.BlockSpec((deep_a, wide), lambda j, i, ids: (deep_b // deep_a, j)),
            pl.BlockSpec((2 * tall, deep_b), lambda j, i, ids: (i, 0)),
            pl.BlockSpec((deep_b, wide), lambda j, i, ids: (0, j)),
        ],
        [pl.BlockSpec((tall, wide), lambda j, i, ids: (0, j))] * blocks,
        [jax.ShapeDtypeStruct((tall, depth), BF16)] * blocks,
        (context, weight, hidden, weight),
        after=after,
        lag=lag,
        name="branches",
    )


def back_kernel(ids, left_a, left_b, right, scales, start, count, blocks, after=(), lag=0.05):
    rows = left_a.shape[0] // blocks
    width = right.shape[0]
    deep_a, deep_b = left_a.shape[1], left_b.shape[1]
    wide = tile_of(width, 512 if count == 1 else 1024)
    unit = tile_of(wide, 512)

    def kernel(ids_ref, a_ref, b_ref, c_ref, d_ref, s_ref, *out_refs):
        for block, out_ref in enumerate(out_refs):

            @pl.when(pl.program_id(1) == block)
            def _(out_ref=out_ref):
                for part in range(wide // unit):
                    here = slice(part * unit, (part + 1) * unit)
                    one = product(a_ref[...], b_ref[here, :], "NT") * s_ref[0:1, here]
                    two = product(c_ref[...], d_ref[here, :], "NT") * s_ref[1:2, here]
                    out_ref[:, here] = (one + two).astype(BF16)

    return call(
        kernel,
        ids,
        (width // wide, count),
        [
            pl.BlockSpec((rows, deep_a), lambda j, i, ids: (start + i, 0)),
            pl.BlockSpec((pl.Element(wide), pl.Element(deep_a)), lambda j, i, ids: (j * wide, deep_b)),
            pl.BlockSpec((rows, deep_b), lambda j, i, ids: (start + i, 0)),
            pl.BlockSpec((wide, deep_b), lambda j, i, ids: (j, 0)),
            pl.BlockSpec((2, wide), lambda j, i, ids: (0, j)),
        ],
        [pl.BlockSpec((rows, wide), lambda j, i, ids: (0, j))] * count,
        [jax.ShapeDtypeStruct((rows, width), BF16)] * count,
        (left_a, right, left_b, right, scales),
        after=after,
        lag=lag,
        name="back",
    )


def piece_grad_kernel(ids, left, pieces, after=(), lag=0.05):
    rows, width = left.shape
    unit, depth = pieces[0].shape
    tall, wide = tile_of(width, 1024), tile_of(depth, 1024)
    cut = tile_of(wide, 512)

    def kernel(ids_ref, a_ref, *refs):
        grad_ref, right_ref = refs[len(pieces) :]
        for part in range(wide // cut):
            here = slice(part * cut, (part + 1) * cut)
            total = None
            for number in range(len(pieces)):
                made = product(a_ref[number * unit : (number + 1) * unit, :], refs[number][:, here], "TN")
                total = made if total is None else total + made
            grad_ref[:, here] = total.astype(BF16)

        @pl.when(pl.program_id(1) == 0)
        def _():
            for number in range(len(pieces)):
                right_ref[number * unit : (number + 1) * unit, :] = refs[number][...]

    return call(
        kernel,
        ids,
        (depth // wide, width // tall),
        [pl.BlockSpec((rows, tall), lambda j, i, ids: (0, i))]
        + [pl.BlockSpec((unit, wide), lambda j, i, ids: (0, j))] * len(pieces),
        [
            pl.BlockSpec((tall, wide), lambda j, i, ids: (i, j)),
            pl.BlockSpec((rows, wide), lambda j, i, ids: (0, j)),
        ],
        [jax.ShapeDtypeStruct((width, depth), BF16), jax.ShapeDtypeStruct((rows, depth), BF16)],
        (left, *pieces),
        after=after,
        lag=lag,
        name="piece_grad",
    )


def full_grad_kernel(ids, left, right, weight=None, total=None, place=0, spare=0, start=0, span=0, kept=(), after=(), lag=0.05):
    rows, depth = left.shape
    width = right.shape[1]
    tall, wide = (tile_of(depth, 512), width) if span else (tile_of(depth, 1024), tile_of(width, 1024))
    unit = tile_of(wide, 512)
    summed = weight is not None

    def kernel(ids_ref, a_ref, b_ref, *refs):
        out_ref = refs[2 if summed else 0]
        if summed:

            @pl.when(pl.program_id(1) == 0)
            def _():
                refs[3][...] = jnp.zeros_like(refs[3])
                refs[4][...] = jnp.zeros_like(refs[4])

        for part in range(wide // unit):
            here = slice(part * unit, (part + 1) * unit)
            value = product(a_ref[...], b_ref[:, here], "TN")
            out_ref[:, here] = value.astype(BF16)
            if summed:
                held = refs[0][:, here].astype(F32)
                one, two = held * value, held * refs[1][:, here]
                refs[3][...] += sum(one[:, lane : lane + 128] for lane in range(0, unit, 128))
                refs[4][...] += sum(two[:, lane : lane + 128] for lane in range(0, unit, 128))

    tile = pl.BlockSpec((tall, wide), lambda i, j, ids: (i, j))
    in_specs = [
        pl.BlockSpec((rows, tall), lambda i, j, ids: (0, i)),
        pl.BlockSpec((rows, wide), lambda i, j, ids: (0, j)),
    ]
    out_specs = [pl.BlockSpec((tall, wide), lambda i, j, ids: (i, start // wide + j))]
    out_shape = [jax.ShapeDtypeStruct((depth, span or width + spare), BF16)]
    args = (left, right)
    if summed:
        args += (weight, total)
        in_specs += [
            pl.BlockSpec((pl.Element(tall), pl.Element(wide)), lambda i, j, ids: (i * tall, pl.multiple_of(place + j * wide, 128))),
            pl.BlockSpec((1, wide), lambda i, j, ids: (0, j)),
        ]
        out_specs += [pl.BlockSpec((tall, 128), lambda i, j, ids: (i, 0))] * 2
        out_shape += [jax.ShapeDtypeStruct((depth, 128), F32)] * 2
    return call(
        kernel,
        ids,
        (depth // tall, width // wide),
        in_specs,
        out_specs,
        out_shape,
        args,
        kept=kept,
        after=after,
        lag=lag,
        name="full_grad",
    )


def sums_kernel(ids, wide, rows, after=(), lag=0.05):
    depth = rows.shape[1]
    count = len(wide)

    def kernel(ids_ref, *refs):
        total = refs[count][...]
        for number, ref in enumerate(refs[:count]):
            row = lax.broadcasted_iota(jnp.int32, (8, 128), 0)
            pick = jnp.where(row == number, 1.0, 0.0).astype(BF16)
            high = ref[...].astype(BF16)
            rest = (ref[...] - high.astype(F32)).astype(BF16)
            total = total + product(pick, high, "NT") + product(pick, rest, "NT")
        refs[-1][...] = total

    def whole(shape):
        return pl.BlockSpec(shape, lambda i, ids: (0, 0))

    return call(
        kernel,
        ids,
        (1,),
        [whole((depth, 128))] * count + [whole((8, depth))],
        whole((8, depth)),
        jax.ShapeDtypeStruct((8, depth), F32),
        (*wide, rows),
        after=after,
        lag=lag,
        name="sums",
    )


def slots_kernel(ids, kept, parts, size, after=(), lag=0.05):
    count, width = parts[0].shape
    each = width // size

    def kernel(ids_ref, *refs):
        total = refs[0][...]
        for ref in refs[1 : len(parts)]:
            total = total + ref[...]
        held = refs[-1]
        held[...] = total
        for number in range(size):
            place = pl.multiple_of((ids_ref[1] ^ number) * each, 128)
            refs[len(parts) + 1 + number][...] = held[:, pl.ds(place, each)]

    return call(
        kernel,
        ids,
        (1,),
        [pl.BlockSpec((count, width), lambda i, ids: (0, 0))] * len(parts),
        [pl.BlockSpec(memory_space=pl.ANY)] + [pl.BlockSpec((count, each), lambda i, ids: (0, 0))] * size,
        [jax.ShapeDtypeStruct(kept.shape, BF16)] + [jax.ShapeDtypeStruct((count, each), F32)] * size,
        tuple(parts),
        scratch=[pltpu.VMEM((count, width), F32)],
        kept=(kept,),
        after=after,
        lag=lag,
        name="slots",
    )


def output_kernel(ids, rows, parts, vectors, after=(), lag=0.05):
    count, width = rows.shape

    def kernel(ids_ref, x_ref, vec, *refs):
        total = refs[0][...].astype(F32)
        for ref in refs[1:-1]:
            total = total + ref[...].astype(F32)
        refs[-1][...] = (x_ref[...].astype(F32) + total + (vec[4:5, :] + vec[5:6, :])).astype(BF16)

    unit = tile_of(count, 256)
    tile = pl.BlockSpec((unit, width), lambda i, ids: (i, 0))
    return call(
        kernel,
        ids,
        (count // unit,),
        [tile, pl.BlockSpec(vectors.shape, lambda i, ids: (0, 0))] + [tile] * len(parts),
        tile,
        jax.ShapeDtypeStruct((count, width), BF16),
        (rows, vectors, *parts),
        after=after,
        lag=lag,
        name="output",
    )


def widen_kernel(ids, rows, widths, after=(), lag=0.05):
    count = rows.shape[0]
    specs, shapes, place = [], [], 0
    for width in widths:
        specs.append(pl.BlockSpec((pl.Element(count), pl.Element(width)), lambda i, ids, place=place: (0, place)))
        shapes.append(jax.ShapeDtypeStruct((count, width), F32))
        place += width

    def kernel(ids_ref, *refs):
        for in_ref, out_ref in zip(refs[: len(specs)], refs[len(specs) :]):
            out_ref[...] = in_ref[...].astype(F32)

    return call(
        kernel,
        ids,
        (1,),
        specs,
        [pl.BlockSpec(shape.shape, lambda i, ids: (0, 0)) for shape in shapes],
        shapes,
        (rows,) * len(specs),
        after=after,
        lag=lag,
        name="widen",
    )


def finish_kernel(ids, rows, widths, heads, parts, scales, last, after=(), lag=0.05):
    count = rows.shape[0]
    one, two = widths
    each = one // heads
    unit = tile_of(count, 128)

    def kernel(ids_ref, in_ref, v_ref, *refs):
        one_ref, two_ref, *sum_refs = refs[len(parts) :]
        for head in range(heads):
            one_ref[:, head, :] = in_ref[:, head * each : (head + 1) * each].astype(F32)
        two_ref[...] = jnp.transpose(in_ref[:, one : one + two].astype(F32))
        sums = refs[0][...]
        for ref in refs[1 : len(parts)]:
            sums = sums + ref[...]
        for number, sum_ref in zip((0, 1, 2, 3, 4, 4, 5, 6), sum_refs):
            value = sums[number : number + 1]
            if number in (0, 2):
                value = (value - v_ref[number + 1 : number + 2, :] * sums[number + 1 : number + 2]) / v_ref[number : number + 1, :]
            wide = sum_ref.shape[1]
            for row in range(sum_ref.shape[0]):
                sum_ref[row : row + 1, :] = value[:, row * wide : (row + 1) * wide]

    def whole(shape):
        return pl.BlockSpec(shape, lambda i, ids: (0,) * len(shape))

    shapes = [(count, heads, each), (two, count)] + [(1, count)] * 6 + last
    return call(
        kernel,
        ids,
        (count // unit,),
        [pl.BlockSpec((unit, rows.shape[1]), lambda i, ids: (i, 0))]
        + [whole(array.shape) for array in (scales, *parts)],
        [
            pl.BlockSpec((unit, heads, each), lambda i, ids: (i, 0, 0)),
            pl.BlockSpec((two, unit), lambda i, ids: (0, i)),
        ]
        + [whole(shape) for shape in shapes[2:]],
        [jax.ShapeDtypeStruct(shape, F32) for shape in shapes],
        (rows, scales, *parts),
        after=after,
        lag=lag,
        name="finish",
    )


def total_kernel(ids, parts, after=(), lag=0.05):
    rows, width = parts[0].shape

    def kernel(ids_ref, *refs):
        total = refs[0][...].astype(F32)
        for ref in refs[1:-1]:
            total = total + ref[...].astype(F32)
        refs[-1][...] = total

    unit = min(rows, 256)
    tile = pl.BlockSpec((unit, width), lambda i, ids: (i, 0))
    return call(
        kernel,
        ids,
        (rows // unit,),
        [tile] * len(parts),
        tile,
        jax.ShapeDtypeStruct((rows, width), F32),
        tuple(parts),
        after=after,
        lag=lag,
        name="total",
    )


def input_kernel(ids, rows, seed, parts, after=(), lag=0.05):
    count, width = rows.shape

    def kernel(ids_ref, x_ref, g_ref, *refs):
        back = refs[0][...].astype(F32)
        for ref in refs[1:-1]:
            back = back + ref[...].astype(F32)
        data = x_ref[...].astype(F32)
        centre = data - jnp.mean(data, axis=-1, keepdims=True)
        rstd = lax.rsqrt(jnp.mean(centre * centre, axis=-1, keepdims=True) + EPSILON)
        scaled = centre * rstd
        inner = jnp.mean(back * scaled, axis=-1, keepdims=True)
        back = back - jnp.mean(back, axis=-1, keepdims=True) - scaled * inner
        refs[-1][...] = g_ref[...].astype(F32) + rstd * back

    unit = tile_of(count, 256)
    tile = pl.BlockSpec((unit, width), lambda i, ids: (i, 0))
    return call(
        kernel,
        ids,
        (count // unit,),
        [tile] * (2 + len(parts)),
        tile,
        jax.ShapeDtypeStruct((count, width), F32),
        (rows, seed, *parts),
        after=after,
        lag=lag,
        name="input",
    )


def rotary_tables(length):
    position = jnp.arange(length, dtype=F32)[:, None]
    lane = jnp.arange(128)
    half = ROTARY // 2
    frequency = 10000.0 ** (-2.0 * (lane % half).astype(F32) / ROTARY)
    angles = position * frequency[None, :]
    sine = jnp.sin(angles)
    tables = (
        jnp.where(lane < ROTARY, jnp.cos(angles), 1.0),
        jnp.where(lane < half, -sine, 0.0),
        jnp.where((lane >= half) & (lane < ROTARY), sine, 0.0),
    )
    return jnp.concatenate(tables, axis=1)


def flip(value, axis, bit, size):
    return lax.ppermute(value, axis, [(i, i ^ bit) for i in range(size)])


def sum_over(value, axis, size):
    bit = 1
    while bit < size:
        value = value + flip(value, axis, bit, size)
        bit *= 2
    return value


def half_kernel(ids, rows, number, after=(), lag=0.05):
    count, width = rows.shape[0] // 2, rows.shape[1]

    def kernel(ids_ref, in_ref, out_ref):
        out_ref[...] = in_ref[...]

    return call(
        kernel,
        ids,
        (1,),
        [pl.BlockSpec((count, width), lambda i, ids: (number, 0))],
        pl.BlockSpec((count, width), lambda i, ids: (0, 0)),
        jax.ShapeDtypeStruct((count, width), BF16),
        (rows,),
        after=after,
        lag=lag,
        name="half",
    )


def gather_rows(ids, rows, size, after=()):
    if size != 4:
        return [rows] + [flip(rows, "tensor", k, size) for k in range(1, size)]
    one = flip(rows, "tensor", 1, size)
    two = flip(rows, "tensor", 2, size)
    upper = flip(half_kernel(ids, two, 0, after), "tensor", 1, size)
    lower = flip(half_kernel(ids, one, 1, after), "tensor", 2, size)
    return [rows, one, two, upper, lower]


def body(
    layer_input,
    cotangent,
    firstgain,
    firstbias,
    secondgain,
    secondbias,
    project,
    projbias,
    merging,
    mergebias,
    expand,
    expandbias,
    shrink,
    shrinkbias,
):
    n_dp, n_tensor = lax.axis_size("dp"), lax.axis_size("tensor")
    dp_at, tensor_at = lax.axis_index("dp"), lax.axis_index("tensor")
    ids = jnp.stack([tensor_at, dp_at]).astype(jnp.int32)
    own_count, width = layer_input.shape
    group_count = own_count * n_tensor
    assert group_count == LENGTH
    depth = width // n_dp
    heads = project.shape[1]
    mixed_width = heads * 3 * HEAD_DIM
    hidden_width = expand.shape[1]

    packed = jnp.concatenate(
        [firstgain, firstbias, secondgain, secondbias, mergebias, shrinkbias, expandbias, projbias.reshape(-1)]
    )
    slots = jnp.where(jnp.arange(n_dp)[:, None] == dp_at, packed[None, :], jnp.zeros((), BF16))
    slots = sum_over(slots, "dp", n_dp).astype(F32)
    vectors = jnp.transpose(slots[:, : 6 * depth].reshape(n_dp, 6, depth), (1, 0, 2)).reshape(6, width)
    at = 6 * depth
    part = hidden_width // n_dp
    b_expand = slots[:, at : at + part].reshape(1, hidden_width)
    at += part
    b_project = jnp.transpose(slots[:, at:].reshape(n_dp, heads, -1), (1, 0, 2)).reshape(1, mixed_width)

    tables = rotary_tables(LENGTH)
    own_project = project.reshape(depth, mixed_width)
    w_in = lax.all_gather(jnp.concatenate([expand, own_project], axis=1), "dp", axis=0, tiled=True)
    w_out = lax.all_gather(jnp.concatenate([shrink, merging], axis=0), "dp", axis=1, tiled=True)

    unit = own_count
    rows_pieces = gather_rows(ids, layer_input, n_tensor, (vectors, tables))
    near, far = (rows_pieces[:-1], rows_pieces[-1:]) if n_tensor != 4 else (rows_pieces[:3], rows_pieces[3:])
    pair = norm_kernel(ids, near, vectors, unit, 0, n_tensor)
    later = stack_kernel(ids, [cotangent], unit, after=(pair[0], *far))
    seed_pieces = [later] + [flip(later, "tensor", k, n_tensor) for k in range(n_tensor - 1, 0, -1)]
    first, second = norm_kernel(ids, far, vectors, unit, n_tensor - 1, n_tensor, kept=pair, after=(later,))
    hidden, slope = expand_kernel(ids, second, w_in, b_expand)
    mixed = mixed_kernel(ids, first, w_in, hidden_width, b_project, tables, n_tensor, after=(hidden,))
    shrink_part, seed = piece_grad_kernel(ids, hidden, seed_pieces[:1] + seed_pieces[:0:-1], after=(mixed,))
    shrink_grad = lax.psum_scatter(shrink_part, "dp", scatter_dimension=1, tiled=True)
    context, lse = attend_kernel(ids, mixed, n_tensor, after=(shrink_part,))
    merge_width = merging.shape[0]
    joint = mixed_width + merge_width
    part = full_grad_kernel(ids, seed, context, start=mixed_width, span=joint)
    branches = branches_kernel(ids, context, hidden, w_out, n_tensor, after=part)
    summed = [branches[0]] + [flip(branches[k], "tensor", k, n_tensor) for k in range(n_tensor - 1, 0, -1)]
    pgrad, expand_sum = shrink_back_kernel(ids, seed, w_out, slope, after=(branches[0],))
    expand_part, gain_two, bias_two = full_grad_kernel(ids, second, pgrad, w_in, expand_sum)
    expand_grad = lax.psum_scatter(expand_part, "dp", scatter_dimension=0, tiled=True)
    cgrad = plain_kernel(ids, seed, w_out, hidden_width, merge_width, after=(expand_part,))
    mgrad, mixed_sum = attend_back_kernel(ids, mixed, cgrad, context, lse, tables, n_tensor)
    project_part, gain_one, bias_one = full_grad_kernel(
        ids, first, mgrad, w_in, mixed_sum, place=hidden_width, span=joint, kept=part
    )

    def slots(values):
        return jnp.pad(values, ((0, 0), (0, depth - values.shape[1]))).reshape(1, width)

    seed_sum = jnp.sum(cotangent.astype(F32), axis=0, keepdims=True)
    over_all = jnp.pad(seed_sum, ((4, 3), (0, 0)))
    over_all = sums_kernel(ids, [gain_one, bias_one, gain_two, bias_two], over_all)
    over_dp = [
        slots(expand_sum.reshape(n_dp, -1)),
        slots(jnp.transpose(mixed_sum.reshape(heads, n_dp, -1), (1, 0, 2)).reshape(n_dp, -1)),
    ]
    over_dp = jnp.pad(jnp.concatenate(over_dp, axis=0), ((5, 1), (0, 0)))
    over_tensor = [over_all] + [flip(over_all, "tensor", k, n_tensor) for k in range(n_tensor - 1, 0, -1)]

    gains = jnp.stack([vectors[0], vectors[2]])
    back = []
    last = over_all
    half = n_tensor // 2
    for start, count in ((half + 1, half - 1), (1, half), (0, 1)):
        made = back_kernel(ids, mgrad, pgrad, w_in, gains, start, count, n_tensor, after=(last,))
        back.append([flip(made[k], "tensor", start + k, n_tensor) if start else made[k] for k in range(count - 1, -1, -1)])
        last = made[0]
        if len(back) == 1:
            layer_output = output_kernel(ids, layer_input, summed, vectors, after=(last,), lag=160)
            project_part, *sums = slots_kernel(ids, project_part, over_tensor + [over_dp], n_dp, after=(layer_output,))
            project_grad = lax.psum_scatter(project_part, "dp", scatter_dimension=0, tiled=True)
            (shrink_grad,) = widen_kernel(ids, shrink_grad, [shrink.shape[1]], after=(sums[0],))
            last = shrink_grad
    (expand_grad,) = widen_kernel(ids, expand_grad, [hidden_width], after=(last,))
    far = total_kernel(ids, back[0] + back[2], after=(expand_grad,), lag=8)
    input_grad = input_kernel(ids, layer_input, cotangent, back[1] + [far], lag=154)
    scales = jnp.stack([firstgain, firstbias, secondgain, secondbias]).astype(F32)
    sums = [sums[0]] + [flip(sums[k], "dp", k, n_dp) for k in range(1, n_dp)]
    project_grad, merging_grad, *sums = finish_kernel(
        ids, project_grad, [mixed_width, merge_width], heads, sums, scales, [(1, expandbias.shape[0]), projbias.shape], after=(input_grad,)
    )
    projbias_grad = sums.pop()
    gain_one, bias_one, gain_two, bias_two, seed_sum, seed_sum_again, expandbias_grad = [value[0] for value in sums]
    return (
        layer_output,
        input_grad,
        gain_one,
        bias_one,
        gain_two,
        bias_two,
        project_grad,
        projbias_grad,
        merging_grad,
        seed_sum,
        expand_grad,
        expandbias_grad,
        shrink_grad,
        seed_sum_again,
    )


def solution(mesh):
    specs = (
        P(("dp", "tensor"), None),
        P(("dp", "tensor"), None),
        P("dp"),
        P("dp"),
        P("dp"),
        P("dp"),
        P("dp", "tensor", None),
        P("tensor", "dp"),
        P("tensor", "dp"),
        P("dp"),
        P("dp", "tensor"),
        P(("tensor", "dp")),
        P("tensor", "dp"),
        P("dp"),
    )
    return jax.shard_map(body, mesh=mesh, in_specs=specs, out_specs=specs, check_vma=False)
```
